32 devices in a mesh: wide: 8 (over z, x), narrow: 4 (over y, core).
Axes of the slice: x: 2, y: 2, z: 4, core: 2. Of those that a mesh axis runs over, the one named last changes fastest.
Arguments:
- tokens: bfloat16 [4, 8, 512, 768], P(None, 'wide', 'narrow'), may hold values from -6 to 6
- clip_ids: int32 [4, 8, 512], P(None, 'wide'), may hold values from -1 to 511, as said below
- w_qkv: bfloat16 [3, 768, 768], P(None, 'wide', 'narrow'), may hold values from -0.21875 to 0.21875
- w_out: bfloat16 [768, 768], P('narrow', 'wide'), may hold values from -0.875 to 0.875
- w_fc1: bfloat16 [768, 3072], P('wide', 'narrow'), may hold values from -0.21875 to 0.21875
- w_fc2: bfloat16 [3072, 768], P('narrow', 'wide'), may hold values from -0.109375 to 0.109375
- norm_bias: bfloat16 [8, 768], P(None, 'wide'), may hold values from -2 to 2
- fc1_bias: bfloat16 [3072], P('wide'), may hold values from -3 to 3
- grad_out: bfloat16 [4, 8, 512, 768], P(None, 'wide', 'narrow'), may hold values from -6 to 6
Outputs:
- out_tokens: bfloat16 [4, 8, 512, 768], P(None, 'wide', 'narrow')
- grad_tokens: float32 [4, 8, 512, 768], P(None, 'wide', 'narrow')
- grad_qkv: float32 [3, 768, 768], P(None, 'wide', 'narrow')
- grad_proj: float32 [768, 768], P('narrow', 'wide')
- grad_fc1: float32 [768, 3072], P('wide', 'narrow')
- grad_fc2: float32 [3072, 768], P('narrow', 'wide')
- grad_norm_bias: float32 [8, 768], P(None, 'wide')
- grad_fc1_bias: float32 [3072], P('wide')
The draws below stay inside these ranges and needn't reach their ends.
Inputs may be any that keep to these rules, and one draw needn't show every extreme that they name: `clip_ids`: in each row a clip's slots are consecutive and clip numbers never fall; one or more padding slots (-1) close every row; the last clip of every row is numbered 512 - 1; in every row one clip begins in the row's first quarter and ends in its last quarter.
All inputs are finite; a program needn't handle non-finite values.
Results may differ from the reference program's by a relative error of at most 0.0093.
Values may be sent and summed in bfloat16 or wider, within the bound.
A program may use at most 128 MiB of HBM per device.

```python
import math
import jax
import jax.numpy as jnp
from jax import lax

D = 768
HEADS = 12
HEAD_DIM = 64
FF = 3072
L = 512
MICRO = 4
ROWS = 8


def draw_clip_ids(key, part):
    key = jax.random.fold_in(key, 11)
    key_start, key_pad, key_reach, key_marks = jax.random.split(key, 4)
    quarter = L // 4
    eighth = max(L // 8, 1)
    shape_rows = (MICRO, ROWS, 1)
    begin = jax.random.randint(key_start, shape_rows, 0, quarter)
    padding = jax.random.randint(key_pad, shape_rows, 1, eighth + 1)
    reach = jax.random.randint(key_reach, shape_rows, 0, 1 << 20) % (quarter - padding)
    finish = L - quarter + 1 + reach
    spacing = max(L // 16, 2)
    marks = (jax.random.randint(key_marks, (MICRO, ROWS, L), 0, spacing) == 0).astype(jnp.int32)
    positions = lax.broadcasted_iota(jnp.int32, (MICRO, ROWS, L), 2)
    inside = (positions > begin) & (positions < finish)
    marks = jnp.where(inside, 0, marks)
    marks = jnp.where((positions == begin) | (positions == finish), 1, marks)
    marks = jnp.where(positions == 0, 0, marks)
    numbers = jnp.cumsum(marks, axis=2).astype(jnp.int32)
    valid = positions < L - padding
    largest = jnp.max(jnp.where(valid, numbers, 0), axis=2, keepdims=True)
    numbers = numbers + (L - 1 - largest)
    return jnp.where(valid, numbers, -1).astype(jnp.int32)


def draw_norm_bias(key, part):
    key = jax.random.fold_in(key, 5)
    noise = jnp.clip(jax.random.normal(key, (8, D), jnp.float32), -3.0, 3.0)
    row_index = lax.broadcasted_iota(jnp.int32, (8, D), 0)
    gain_rows = (row_index == 0) | (row_index == 5)
    return jnp.where(gain_rows, 1.0 + 0.15 * noise, 0.5 * noise).astype(jnp.bfloat16)


def strengthened(values, stream_key, source, target, blocks, factor):
    def block_of(axis_at):
        return (jnp.arange(values.shape[axis_at]) // (values.shape[axis_at] // blocks)).reshape((-1,) + (1,) * (values.ndim - 1 - axis_at))

    first = jax.random.permutation(stream_key, blocks)[block_of(target)]
    second = (block_of(target) + blocks // 2) % blocks
    return jnp.where((block_of(source) == first) | (block_of(source) == second), factor * values, values)


def block_scale(key, extent, pieces, least, high):
    factor_of = 1.0
    for dim, shards_of in pieces:
        draws = jax.random.uniform(jax.random.fold_in(jax.random.fold_in(key, 6), dim), (shards_of,), jnp.float32, least / len(pieces), high / len(pieces))
        factor_of = factor_of * jnp.repeat(jnp.exp(draws), extent[dim] // shards_of).reshape((-1,) + (1,) * (len(extent) - 1 - dim))
    return factor_of


def scatter_about(stream_key, extent, deviation, most, cuts=(), held_as=jnp.bfloat16):
    entries = jax.random.normal(stream_key, extent, jnp.float32) * deviation
    if len(cuts) > 0:
        entries = block_scale(stream_key, extent, cuts, -0.22, 0.18) * entries
    return jnp.clip(entries, min=-most, max=most).astype(held_as)


def bell_draw_with(own_key, dims, width, most, cuts, heavy, kind=jnp.bfloat16):
    drawn = width * jax.random.normal(own_key, dims, jnp.float32)
    if cuts:
        drawn = drawn * block_scale(own_key, dims, cuts, -0.22, 0.18)
    return jnp.clip(strengthened(drawn, jax.random.fold_in(own_key, 3), *heavy), -most, most).astype(kind)


def setup_inputs(seed: int = 0) -> dict:
    key_of = jax.random.split(jax.random.key(seed), 10)
    tokens = scatter_about(key_of[0], (MICRO, ROWS, L, D), 1.0, 6.0, ((1, 8), (2, 4)))
    clip_ids = draw_clip_ids(jax.random.fold_in(key_of[9], 71), 0)
    w_qkv = scatter_about(key_of[2], (3, D, D), D ** -0.5, 0.21875, ((1, 8), (2, 4)))
    w_out = scatter_about(key_of[3], (D, D), (D // 16) ** -0.5, 0.875, ((0, 4), (1, 8)))
    w_fc1 = scatter_about(key_of[4], (D, FF), D ** -0.5, 0.21875, ((0, 8), (1, 4)))
    w_fc2 = scatter_about(key_of[5], (FF, D), FF ** -0.5, 0.109375, ((0, 4), (1, 8)))
    norm_bias = draw_norm_bias(jax.random.fold_in(key_of[9], 71), 0)
    fc1_bias = scatter_about(key_of[7], (FF,), 0.5, 3.0, ((0, 8),))
    grad_out = bell_draw_with(key_of[8], (MICRO, ROWS, L, D), 1.0, 6.0, ((1, 8), (2, 4)), (1, 3, 8, 2.0))
    return {"tokens": tokens, "clip_ids": clip_ids, "w_qkv": w_qkv, "w_out": w_out, "w_fc1": w_fc1, "w_fc2": w_fc2, "norm_bias": norm_bias, "fc1_bias": fc1_bias, "grad_out": grad_out}


@jax.custom_vjp
def low(v):
    return lax.optimization_barrier(v.astype(jnp.bfloat16)).astype(jnp.float32)

@jax.custom_vjp
def low_back(v):
    return v

def low_keep(v):
    return (low(v), None)

def low_pass(kept, grad):
    return (grad,)

def back_keep(v):
    return (v, None)

def back_low(kept, grad):
    return (low(grad),)
low.defvjp(low_keep, low_pass)
low_back.defvjp(back_keep, back_low)

def layer_norm(values, scaling, shifting):
    average = lax.optimization_barrier(jnp.mean(values, axis=-1, keepdims=True))
    centred = values - average
    variance = lax.optimization_barrier(jnp.mean(centred * centred, axis=-1, keepdims=True))
    return centred * lax.rsqrt(variance + 1e-06) * scaling + shifting

def attend_row(element):
    query, keys, values, clip_row = element
    length = query.shape[0]
    query = query.reshape(length, HEADS, HEAD_DIM)
    keys = keys.reshape(length, HEADS, HEAD_DIM)
    values = values.reshape(length, HEADS, HEAD_DIM)
    raw_scores = jnp.einsum('qhd,khd->hqk', query, keys, precision=lax.Precision.HIGHEST) * HEAD_DIM ** (-0.5)
    scores = low_back(raw_scores)
    positions = lax.broadcasted_iota(jnp.int32, (length,), 0)
    allowed = (clip_row[:, None] == clip_row[None, :]) & (clip_row[None, :] >= 0) | (positions[:, None] == positions[None, :])
    scores = jnp.where(allowed[None], scores, -1e+30)
    row_max = lax.optimization_barrier(jnp.max(scores, axis=-1, keepdims=True))
    weights = jnp.exp(scores - row_max)
    probabilities = low(weights / lax.optimization_barrier(jnp.sum(weights, axis=-1, keepdims=True)))
    mixed = jnp.einsum('hqk,khd->qhd', probabilities, values, precision=lax.Precision.HIGHEST)
    return mixed.reshape(length, HEADS * HEAD_DIM)

def block(params, inputs, clip_rows):
    w_qkv, w_out, w_fc1, w_fc2, norm_bias, fc1_bias = params
    highest = lax.Precision.HIGHEST
    normed1 = low(layer_norm(inputs, norm_bias[0], norm_bias[1]))
    projected = jnp.einsum('gld,jde->jgle', normed1, w_qkv, precision=highest)
    bias_three = jnp.stack([norm_bias[2], jnp.zeros_like(norm_bias[2]), norm_bias[3]])
    qkv = low_back(low(projected + bias_three[:, None, None, :]))
    heads = lax.map(jax.checkpoint(attend_row), (qkv[0], qkv[1], qkv[2], clip_rows))
    heads = low_back(low(heads))
    attention = low_back(jnp.einsum('gle,ed->gld', heads, w_out, precision=highest) + norm_bias[4])
    hidden1 = inputs + attention
    normed2 = low(layer_norm(hidden1, norm_bias[5], norm_bias[6]))
    pre_act = low_back(jnp.einsum('gld,df->glf', normed2, w_fc1, precision=highest) + fc1_bias)
    activated = low(jax.nn.gelu(pre_act, approximate=False))
    mlp_out = low_back(jnp.einsum('glf,fd->gld', activated, w_fc2, precision=highest) + norm_bias[7])
    return hidden1 + mlp_out

def reference(tokens, clip_ids, w_qkv, w_out, w_fc1, w_fc2, norm_bias, fc1_bias, grad_out):
    params = tuple((p.astype(jnp.float32) for p in (w_qkv, w_out, w_fc1, w_fc2, norm_bias, fc1_bias)))
    row_total = MICRO * ROWS
    group = math.gcd(row_total, max(1, 4096 // L))
    inputs = tokens.astype(jnp.float32).reshape(row_total // group, group, L, D)
    clip_rows = clip_ids.reshape(row_total // group, group, L)
    upstream = grad_out.astype(jnp.float32).reshape(row_total // group, group, L, D)

    def forward(weights, values):

        def one_group(carried, element):
            return (carried, jax.checkpoint(block)(weights, element[0], element[1]))
        _, results = lax.scan(one_group, None, (values, clip_rows))
        return results
    results, pull = jax.vjp(forward, params, inputs)
    weight_grads, input_grad = pull(upstream)
    return (results.reshape(MICRO, ROWS, L, D).astype(jnp.bfloat16), input_grad.reshape(MICRO, ROWS, L, D), weight_grads[0], weight_grads[1], weight_grads[2], weight_grads[3], weight_grads[4], weight_grads[5])
```

```python
import functools

import jax
import jax.numpy as jnp
from jax import lax
from jax.experimental import pallas as pl
from jax.experimental.pallas import tpu as pltpu
from jax.sharding import PartitionSpec as P

HEAD_DIM = 64
MESH = pl.DeviceIdType.MESH
BF16 = jnp.bfloat16
F32 = jnp.float32
NN = (((1,), (0,)), ((), ()))
NT = (((1,), (1,)), ((), ()))
TN = (((0,), (0,)), ((), ()))
Z_FIRST = (True, False, False)
X_EARLY = ((1, 0), (1, 0), (1, 0))


def dot(a, b, dims):
    return lax.dot_general(a, b, dims, preferred_element_type=F32)


def aligned(value, step):
    return value if isinstance(value, int) else pl.multiple_of(value, step)


def slab_sum(values):
    rows, width = values.shape
    return jnp.sum(values.reshape(rows // 8, 8, width), axis=0)


def row_kernel(
    tok, clip, wqkv, wout, wfc1, wfc2, small, gout,
    out_tok, out_gtok, out_g, out_vec,
    wts, psum, gsend, recv1, recv2, recv3,
    xrow, urow, normed1, normed2, attn_grad, outrow, gtrow,
    qs, ks, vs, heads, dheads, act, dgelu, dqkv,
    fa, fb, mask, stats, lse,
    smalls, vecs, qbias, vbias, hbias, vpart, vrecv, vsum, vnar,
    tok_s, tok_r, gout_s, gout_r, small_s, small_r,
    ag_s, ag_r, sib_r, gs_s, gs_r, rs_s, rs1_r, rs2_r, rs3_r,
    ot_s, ot_r, gt_s, gt_r, vp_s, vp_r, vn_s, vn_r, loc,
):
    depth, width = wfc1.shape[0], tok.shape[-1]
    wide = width // depth
    z_count = wide // 2
    w = lax.axis_index("wide")
    n = lax.axis_index("narrow")
    z, x, y, c = w // 2, w % 2, n // 2, n % 2
    length = xrow.shape[0]
    block = length // 4
    here = (w, n)
    sibling = (w, n ^ 1)
    wide_partners = [(w ^ v, n) for v in range(1, wide)]
    narrow_partners = [(w, n ^ v) for v in range(1, 4)]

    def send(src, dst, s_sem, r_sem, to):
        pltpu.make_async_remote_copy(
            src_ref=src, dst_ref=dst, send_sem=s_sem, recv_sem=r_sem,
            device_id=to, device_id_type=MESH,
        ).start()

    def got(ref, r_sem):
        pltpu.make_async_remote_copy(
            src_ref=ref, dst_ref=ref, send_sem=loc.at[0], recv_sem=r_sem,
            device_id=sibling, device_id_type=MESH,
        ).wait_recv()

    def sent(ref, s_sem):
        pltpu.make_async_remote_copy(
            src_ref=ref, dst_ref=ref, send_sem=s_sem, recv_sem=loc.at[0],
            device_id=sibling, device_id_type=MESH,
        ).wait_send()

    early = [jnp.where(c == 0, X_EARLY[k][0], X_EARLY[k][1]) for k in range(3)]

    def origin(k, rel):
        rz, ra, rb = rel
        e = early[k]
        ox = x ^ (e * ra + (1 - e) * rb)
        oy = y ^ (e * rb + (1 - e) * ra)
        return z ^ rz, ox, oy

    def wts_at(k, rel):
        oz, ox, oy = origin(k, rel)
        start = (k * 4 + oy * 2 + c) * width + (oz * 2 + ox) * depth
        return wts.at[pl.ds(aligned(start, 32), depth), :]

    def psum_at(k, rel):
        oz, ox, oy = origin(k, rel)
        start = (k * 2 + oy) * width + (oz * 2 + ox) * depth
        return psum.at[pl.ds(aligned(start, 32), depth), :]

    def partner(k, dim, v):
        e = early[k]
        if dim == 0:
            return (w ^ (2 * v), n)
        x_hop = e if dim == 1 else 1 - e
        return (w ^ x_hop, n ^ (2 * (1 - x_hop)))

    def number(rel):
        return rel[0] * 4 + rel[1] * 2 + rel[2]

    order = [(0, 1, 2) if Z_FIRST[k] else (1, 0, 2) for k in range(3)]
    extent = (z_count, 2, 2)

    def hand_on(k, rel, phase):
        for later in range(phase + 1, 3):
            dim = order[k][later]
            for v in range(1, extent[dim]):
                there = list(rel)
                there[dim] = v
                send(
                    wts_at(k, rel), wts_at(k, rel), ag_s.at[k],
                    ag_r.at[k, number(there)], partner(k, dim, v),
                )
        send(wts_at(k, rel), wts_at(k, rel), ag_s.at[k], sib_r.at[k], sibling)

    def gather_steps(k):
        steps = []
        held = [(0, 0, 0)]
        for phase in range(3):
            dim = order[k][phase]
            fresh = []
            for v in range(1, extent[dim]):
                for rel in held:
                    there = list(rel)
                    there[dim] = v
                    fresh.append(tuple(there))

            def step(rel, phase):
                got(wts_at(k, rel), ag_r.at[k, number(rel)])
                hand_on(k, rel, phase)

            steps += [functools.partial(step, rel, phase) for rel in fresh]
            held = held + fresh
        return steps

    def add_up(k, rel, others):
        here_ref = psum_at(k, rel)
        total = here_ref[...].astype(F32)
        for other in others:
            total = total + other[...].astype(F32)
        return here_ref, total

    def scatter_steps(k):
        def first():
            for rz in list(range(1, z_count)) + [0]:
                for ra in (1, 0):
                    send(
                        psum_at(k, (rz, ra, 1)), recv1.at[k, rz * 2 + ra], rs_s.at[k],
                        rs1_r.at[k, rz * 2 + ra], partner(k, 2, 1),
                    )

        def fresh1(rz, ra):
            ref = recv1.at[k, rz * 2 + ra]
            got(ref, rs1_r.at[k, rz * 2 + ra])
            return ref

        def fresh2(i):
            ref = recv2.at[k, i]
            got(ref, rs2_r.at[k, i])
            return ref

        def fresh3(i):
            ref = recv3.at[k, i]
            got(ref, rs3_r.at[k, i])
            return ref

        steps = [first]
        if Z_FIRST[k]:
            def along(rz):
                ref, total = add_up(k, (rz, 1, 0), [fresh1(rz, 1)])
                ref[...] = total.astype(BF16)
                send(ref, recv2.at[k, rz], rs_s.at[k], rs2_r.at[k, rz], partner(k, 1, 1))

            def across(rz):
                ref, total = add_up(k, (rz, 0, 0), [fresh1(rz, 0), fresh2(rz)])
                ref[...] = total.astype(BF16)
                send(ref, recv3.at[k, rz - 1], rs_s.at[k], rs3_r.at[k, rz - 1], partner(k, 0, rz))

            def last():
                others = [fresh1(0, 0), fresh2(0)] + [fresh3(i) for i in range(z_count - 1)]
                _, total = add_up(k, (0, 0, 0), others)
                out_g[k] = total

            steps += [functools.partial(along, rz) for rz in list(range(1, z_count)) + [0]]
            steps += [functools.partial(across, rz) for rz in range(1, z_count)]
        else:
            def along(rz, ra):
                ref, total = add_up(k, (rz, ra, 0), [fresh1(rz, ra)])
                ref[...] = total.astype(BF16)
                i = (rz - 1) * 2 + ra
                send(ref, recv2.at[k, i], rs_s.at[k], rs2_r.at[k, i], partner(k, 0, rz))

            def across():
                others = [fresh1(0, 1)] + [fresh2(i * 2 + 1) for i in range(z_count - 1)]
                ref, total = add_up(k, (0, 1, 0), others)
                ref[...] = total.astype(BF16)
                send(ref, recv3.at[k, 0], rs_s.at[k], rs3_r.at[k, 0], partner(k, 1, 1))

            def last():
                others = [fresh1(0, 0)] + [fresh2(i * 2) for i in range(z_count - 1)] + [fresh3(0)]
                _, total = add_up(k, (0, 0, 0), others)
                out_g[k] = total

            for rz in range(1, z_count):
                steps += [functools.partial(along, rz, 1), functools.partial(along, rz, 0)]
            steps += [across]
        return steps + [last]

    pending = []
    done = {}

    def enqueue(tag, steps):
        done[tag] = len(steps)
        pending.extend((tag, step) for step in steps)

    def service(count=1):
        for _ in range(count):
            if pending:
                tag, step = pending.pop(0)
                step()
                done[tag] -= 1

    def finish(tag):
        while done[tag] > 0:
            service()

    def weights_here(k):
        finish(("gather", k))
        got(wts.at[pl.ds(0, 2 * width), :], sib_r.at[k])

    def weight(k, j, columns=slice(None)):
        return wts[pl.ds(aligned((k * 4 + j) * width, 128), width), columns]

    def own_place(k):
        return pl.ds(aligned((k * 4 + n) * width + w * depth, 32), depth)

    wts[own_place(0), 0:192] = wqkv[0]
    wts[own_place(0), 192:384] = wqkv[2]
    wts[own_place(0), 384:576] = wqkv[1]
    wts[own_place(0), 576:768] = wout[...]
    wts[own_place(1), :] = wfc1[...]
    wts[own_place(2), :] = wfc2[...]
    smalls[w] = small[...]

    barrier = pltpu.get_barrier_semaphore()
    for to in wide_partners + narrow_partners:
        pl.semaphore_signal(barrier, inc=1, device_id=to, device_id_type=MESH)
    pl.semaphore_wait(barrier, len(wide_partners) + len(narrow_partners))

    rows_here = pl.ds(aligned(n * block, 128), block)
    for i, to in enumerate(wide_partners):
        send(smalls.at[w], smalls.at[w], small_s.at[i], small_r.at[i], to)
    for i, to in enumerate(narrow_partners):
        send(tok.at[to[1]], xrow.at[rows_here, :], tok_s.at[i], tok_r.at[i], to)
    own_tok = pltpu.make_async_copy(tok.at[n], xrow.at[rows_here, :], loc.at[1])
    own_tok.start()
    own_gout = pltpu.make_async_copy(gout.at[n], urow.at[rows_here, :], loc.at[2])
    own_gout.start()

    def start_gout():
        for i, to in enumerate(narrow_partners):
            send(gout.at[to[1]], urow.at[rows_here, :], gout_s.at[i], gout_r.at[i], to)

    starts = [functools.partial(hand_on, k, (0, 0, 0), -1) for k in range(3)]
    steps0, steps1, steps2 = (gather_steps(k) for k in range(3))
    half = len(steps0) // 2
    enqueue(("gather", 0), [starts[0]] + steps0[:half] + [starts[1]] + steps0[half:])
    enqueue(("gather", 1), [start_gout] + steps1[:half] + [starts[2]] + steps1[half:])
    enqueue(("gather", 2), steps2)
    service(1)

    ids = clip[n]
    place = lax.broadcasted_iota(jnp.int32, (1, length), 1)
    ids = jnp.where(ids >= 0, ids, -1 - place).astype(F32)
    ids_down = jnp.transpose(jnp.broadcast_to(ids, (128, length)))[:, 0:1]
    mask[...] = jnp.where(ids_down == ids, 0.0, -1e30)

    for i, to in enumerate(wide_partners):
        got(smalls.at[to[0]], small_r.at[i])
    qbias[...] = jnp.zeros_like(qbias)
    vbias[...] = jnp.zeros_like(vbias)
    for i in range(wide):
        part = smalls[i]
        vecs[:, i * depth : (i + 1) * depth] = part[0:8, 0:depth]
        j, half_at = i // 2, (i % 2) * depth
        qbias[j, :, half_at : half_at + depth] = part[2:3, 0:depth]
        vbias[j, :, 64 + half_at : 64 + half_at + depth] = part[3:4, 0:depth]
        for r in range(4):
            at = (i % 2) * 4 * depth + r * depth
            hbias[j, :, at : at + depth] = part[8 + r : 9 + r, 0:depth]

    own_tok.wait()
    for i, to in enumerate(narrow_partners):
        got(xrow.at[pl.ds(aligned(to[1] * block, 128), block), :], tok_r.at[i])

    def norm_forward(source, gain, shift, column, target):
        def body(i, _):
            rows = pl.ds(aligned(i * block, 128), block)
            v = source[rows, :].astype(F32)
            average = jnp.mean(v, axis=-1, keepdims=True)
            centred = v - average
            rr = lax.rsqrt(jnp.mean(centred * centred, axis=-1, keepdims=True) + 1e-6)
            stats[rows, column : column + 1] = average
            stats[rows, column + 1 : column + 2] = rr
            target[rows, :] = (centred * rr * vecs[gain : gain + 1] + vecs[shift : shift + 1]).astype(BF16)
            return 0

        lax.fori_loop(0, 4, body, 0)

    norm_forward(xrow, 0, 1, 0, normed1)

    weights_here(0)
    lane = lax.broadcasted_iota(jnp.int32, (1, 256), 1)
    low = lane[:, 0:128] < 64
    for j in range(4):
        projected = dot(normed1[...], weight(0, j, slice(0, 640)), NN)
        slot = slice(256 * j, 256 * j + 256)
        query = (projected[:, 0:256] + qbias[j]).astype(BF16).astype(F32) * 0.125
        qs[:, slot] = jnp.where(lane < 192, query, 0.0).astype(BF16)
        value = projected[:, 128:384] + vbias[j]
        vs[:, slot] = jnp.where(lane >= 64, value, 0.0).astype(BF16)
        ks[:, slot] = jnp.where(lane < 192, projected[:, 384:640], 0.0).astype(BF16)
        service(1)

    def lanes(j, second):
        return pl.ds(aligned(256 * j + 128 * second, 128), 128)

    def only(head, values):
        return jnp.where(low if head == 0 else ~low, values, jnp.zeros_like(values))

    def query_of(j, head):
        return only(head, qs[:, lanes(j, 0)]) if head < 2 else qs[:, lanes(j, 1)]

    def key_of(j, head):
        return ks[:, lanes(j, 0)] if head < 2 else ks[:, lanes(j, 1)]

    for j in range(4):
        mixed = []
        for head in range(3):
            scores = dot(query_of(j, head), key_of(j, head), NT) + mask[...]
            row_max = jnp.max(scores, axis=1, keepdims=True)
            weights = jnp.exp(scores - row_max)
            row_sum = jnp.sum(weights, axis=1, keepdims=True)
            probs = (weights * (1.0 / row_sum)).astype(BF16)
            lse[j, :, head : head + 1] = row_max + jnp.log(row_sum)
            value = vs[:, lanes(j, 0)] if head == 0 else vs[:, lanes(j, 1)]
            mixed.append(dot(probs, value, NN))
            service(1)
        heads[:, lanes(j, 0)] = mixed[0].astype(BF16)
        heads[:, lanes(j, 1)] = jnp.where(low, mixed[1], mixed[2]).astype(BF16)

    fb[...] = xrow[...].astype(F32) + vecs[4:5]
    for j in range(4):
        fb[...] += dot(heads[:, 256 * j : 256 * j + 256], weight(0, j, slice(512, 768)), NT)
        service(1)
    fa[...] = fb[...]
    norm_forward(fa, 5, 6, 2, normed2)

    weights_here(1)
    for j in range(4):
        pre = dot(normed2[...], weight(1, j), NN) + hbias[j]
        cumulative = 0.5 * (1.0 + lax.erf(pre * (0.5**0.5)))
        density = jnp.exp(pre * pre * -0.5) * (0.5 / jnp.pi) ** 0.5
        act[j] = (pre * cumulative).astype(BF16)
        dgelu[j] = (cumulative + pre * density).astype(BF16)
        service(2)

    def give(k, j, slot, product):
        if k < 2:
            sent(gsend.at[slot], gs_s.at[slot])
        gsend[slot] = product.astype(BF16)
        place = pl.ds(aligned((k * 2 + j) * width, 128), width)
        send(gsend.at[slot], psum.at[place, :], gs_s.at[slot], gs_r.at[k * 2 + j], sibling)

    def keep(k, j, product):
        place = pl.ds(aligned((k * 2 + j) * width, 128), width)
        got(psum.at[place, :], gs_r.at[k * 2 + j])
        psum[place, :] = (product + psum[place, :].astype(F32)).astype(BF16)

    own_gout.wait()
    service(1)
    finish(("gather", 1))
    for i, to in enumerate(narrow_partners):
        got(urow.at[pl.ds(aligned(to[1] * block, 128), block), :], gout_r.at[i])
    for j in range(2):
        give(2, j, j, dot(urow[...], act[2 * j + 1 - c], TN))
        service(1)
    for j in range(2):
        keep(2, j, dot(urow[...], act[2 * j + c], TN))
        service(1)
    weights_here(2)
    enqueue(("scatter", 2), scatter_steps(2))
    service(1)

    fb[...] = fa[...] + vecs[7:8]
    for j in range(4):
        fb[...] += dot(act[j], weight(2, j), NT)
        service(1)
    outrow[...] = fb[...].astype(BF16)
    for i, to in enumerate(narrow_partners):
        rows = pl.ds(aligned(to[1] * block, 128), block)
        send(outrow.at[rows, :], out_tok.at[n], ot_s.at[i], ot_r.at[i], to)
    own_out = pltpu.make_async_copy(outrow.at[rows_here, :], out_tok.at[n], loc.at[3])
    own_out.start()

    def put(row, i, values):
        vpart[i, row : row + 1, 0:depth] = values

    def put_row(row, values):
        for i in range(wide):
            put(row, i, values[:, i * depth : (i + 1) * depth])

    def column_sum(values):
        return jnp.sum(values.astype(F32), axis=0, keepdims=True)

    vpart[...] = jnp.zeros_like(vpart)
    put_row(7, column_sum(urow[...]))
    for j in range(4):
        grad = dot(urow[...], weight(2, j), NN) * dgelu[j].astype(F32)
        dgelu[j] = grad.astype(BF16)
        total = column_sum(dgelu[j])
        for i in range(2):
            for r in range(4):
                at = (i * 4 + r) * depth
                put(8 + r, 2 * j + i, total[:, at : at + depth])
        service(1)
    for j in range(2):
        give(1, j, j, dot(normed2[...], dgelu[2 * j + 1 - c], TN))
        service(1)
    for j in range(2):
        keep(1, j, dot(normed2[...], dgelu[2 * j + c], TN))
        service(1)
    enqueue(("scatter", 1), scatter_steps(1))
    fb[...] = dot(dgelu[0], weight(1, 0), NT)
    for j in range(1, 4):
        fb[...] += dot(dgelu[j], weight(1, j), NT)
        service(1)

    def norm_backward(source, grad, gain, column, extra, target, rounded):
        def body(i, sums):
            rows = pl.ds(aligned(i * block, 128), block)
            rr = stats[rows, column + 1 : column + 2]
            xhat = (source[rows, :].astype(F32) - stats[rows, column : column + 1]) * rr
            n_grad = grad[rows, :]
            u = n_grad * vecs[gain : gain + 1]
            inner = u - jnp.mean(u, axis=-1, keepdims=True) - xhat * jnp.mean(u * xhat, axis=-1, keepdims=True)
            result = rr * inner + extra[rows, :].astype(F32)
            if target is not None:
                target[rows, :] = result
            low_result = result.astype(BF16)
            rounded[rows, :] = low_result
            return (
                sums[0] + slab_sum(n_grad * xhat),
                sums[1] + slab_sum(n_grad),
                sums[2] + slab_sum(low_result.astype(F32)),
            )

        zero = jnp.zeros((8, width), F32)
        sums = lax.fori_loop(0, 4, body, (zero, zero, zero))
        return [jnp.sum(s, axis=0, keepdims=True) for s in sums]

    gain2, shift2, attn_total = norm_backward(fa, fb, 5, 2, urow, fb, attn_grad)
    put_row(5, gain2)
    put_row(6, shift2)
    put_row(4, attn_total)
    service(1)

    for j in range(4):
        back = dot(attn_grad[...], weight(0, j, slice(512, 768)), NN)
        dheads[:, 256 * j : 256 * j + 256] = jnp.where(lane >= 64, back, 0.0).astype(BF16)
        service(1)

    def attention_backward(j):
        def value_of(head):
            return vs[:, lanes(j, 0)] if head == 0 else vs[:, lanes(j, 1)]

        def upstream_of(head):
            if head == 0:
                return dheads[:, lanes(j, 0)]
            return only(head - 1, dheads[:, lanes(j, 1)])

        dq, dk, dv = [], [], []
        for head in range(3):
            query, key, up = query_of(j, head), key_of(j, head), upstream_of(head)
            second = int(head > 0)
            delta = jnp.sum(
                up.astype(F32) * heads[:, lanes(j, second)].astype(F32), axis=1, keepdims=True
            )
            scores = dot(query, key, NT) + mask[...]
            soft = jnp.exp(scores - lse[j, :, head : head + 1])
            prob_grad = dot(up, value_of(head), NT)
            score_grad = (soft * (prob_grad - delta)).astype(BF16)
            dq.append(dot(score_grad, key, NN))
            dk.append(dot(score_grad, query, TN))
            dv.append(dot(soft.astype(BF16), up, TN))
            service(1)
        dqkv[:, 0:128] = (jnp.where(low, dq[0], dq[1]) * 0.125).astype(BF16)
        dqkv[:, 128:256] = (dq[2] * 0.125 + dv[0]).astype(BF16)
        dqkv[:, 256:384] = (dv[1] + dv[2]).astype(BF16)
        dqkv[:, 384:512] = (dk[0] + dk[1]).astype(BF16)
        dqkv[:, 512:640] = dk[2].astype(BF16)
        total = column_sum(dqkv[:, 0:384])
        for i in range(2):
            put(2, 2 * j + i, total[:, i * depth : (i + 1) * depth])
            put(3, 2 * j + i, total[:, (2 + i) * depth : (3 + i) * depth])

    def projection_grad(j):
        first = dot(normed1[...], dqkv[...], TN)
        second = dot(attn_grad[...], heads[:, pl.ds(aligned(256 * j, 128), 256)], TN)
        return jnp.concatenate(
            [first[:, 0:512], first[:, 512:640] + second[:, 0:128], second[:, 128:256]], axis=1
        )

    fa[...] = jnp.zeros_like(fa)
    for i, half in enumerate((1 - y, y)):
        for own in (False, True):
            j = 2 * half + (c if own else 1 - c)
            attention_backward(j)
            if own:
                keep(0, half, projection_grad(j))
            else:
                give(0, half, i, projection_grad(j))
            service(1)
            fa[...] += dot(dqkv[...], weight(0, j, slice(0, 640)), NT)
            service(1)
    enqueue(("scatter", 0), scatter_steps(0))
    finish(("scatter", 1))
    service(1)

    gain1, shift1, _ = norm_backward(xrow, fa, 0, 0, fb, None, gtrow)
    for i, to in enumerate(narrow_partners):
        rows = pl.ds(aligned(to[1] * block, 128), block)
        send(gtrow.at[rows, :], out_gtok.at[n], gt_s.at[i], gt_r.at[i], to)
    own_gtok = pltpu.make_async_copy(gtrow.at[rows_here, :], out_gtok.at[n], loc.at[4])
    own_gtok.start()
    put_row(0, gain1)
    put_row(1, shift1)
    for i, to in enumerate(wide_partners):
        send(vpart.at[to[0]], vrecv.at[i], vp_s.at[i], vp_r.at[i], to)
    service(4)
    total = vpart[w]
    for i in range(len(wide_partners)):
        got(vrecv.at[i], vp_r.at[i])
        total = total + vrecv[i]
    vsum[...] = total
    for i, to in enumerate(narrow_partners):
        send(vsum, vnar.at[i], vn_s.at[i], vn_r.at[i], to)
    finish(("scatter", 0))
    for i in range(3):
        got(vnar.at[i], vn_r.at[i])
        total = total + vnar[i]
    out_vec[...] = total

    for i, to in enumerate(narrow_partners):
        got(out_tok.at[to[1]], ot_r.at[i])
        got(out_gtok.at[to[1]], gt_r.at[i])
        sent(tok.at[0], tok_s.at[i])
        sent(gout.at[0], gout_s.at[i])
        sent(outrow.at[pl.ds(0, block), :], ot_s.at[i])
        sent(gtrow.at[pl.ds(0, block), :], gt_s.at[i])
        sent(vsum, vn_s.at[i])
    for i in range(len(wide_partners)):
        sent(smalls.at[0], small_s.at[i])
        sent(vpart.at[0], vp_s.at[i])
    for k in range(3):
        sends = (4 * z_count - 1) + 4 * z_count
        sent(wts.at[pl.ds(0, sends * depth), :], ag_s.at[k])
        sends = 4 * z_count - 1
        sent(psum.at[pl.ds(0, sends * depth), :], rs_s.at[k])
    for slot in range(2):
        sent(gsend.at[slot], gs_s.at[slot])
    own_out.wait()
    own_gtok.wait()


def fused_local(tokens, clip_ids, w_qkv, w_out, w_fc1, w_fc2, norm_bias, fc1_bias, grad_out):
    micro, _, block, width = tokens.shape
    depth, hidden = w_fc1.shape
    wide = width // depth
    z_count = wide // 2
    length = micro * block
    small = jnp.concatenate([norm_bias, fc1_bias.reshape(4, depth)]).astype(F32)
    small = jnp.pad(small, ((0, 4), (0, 128 - depth)))

    def anywhere():
        return pl.BlockSpec(memory_space=pl.ANY)

    def vmem():
        return pl.BlockSpec(memory_space=pltpu.VMEM)

    def flat(*shape):
        return pltpu.VMEM(shape, BF16)

    def wide_type(*shape):
        return pltpu.VMEM(shape, F32)

    def sems(*shape):
        return pltpu.SemaphoreType.DMA(shape)

    out_tok, out_gtok, out_g, out_vec = pl.pallas_call(
        row_kernel,
        out_shape=(
            jax.ShapeDtypeStruct((micro, block, width), BF16),
            jax.ShapeDtypeStruct((micro, block, width), BF16),
            jax.ShapeDtypeStruct((3, depth, width), F32),
            jax.ShapeDtypeStruct((16, 128), F32),
        ),
        in_specs=[anywhere()] + [vmem()] * 6 + [anywhere()],
        out_specs=(anywhere(), anywhere(), vmem(), vmem()),
        scratch_shapes=[
            flat(12 * width, hidden),
            flat(6 * width, hidden),
            flat(2, width, hidden),
            flat(3, 2 * z_count, depth, hidden),
            flat(3, 2 * (z_count - 1), depth, hidden),
            flat(3, z_count - 1, depth, hidden),
            *[flat(length, width)] * 7,
            *[flat(length, 1024)] * 5,
            flat(4, length, hidden),
            flat(4, length, hidden),
            flat(length, 640),
            wide_type(length, width),
            wide_type(length, width),
            wide_type(length, length),
            wide_type(length, 128),
            wide_type(4, length, 128),
            wide_type(wide, 16, 128),
            wide_type(8, width),
            wide_type(4, 1, 256),
            wide_type(4, 1, 256),
            wide_type(4, 1, hidden),
            wide_type(wide, 16, 128),
            wide_type(wide - 1, 16, 128),
            wide_type(16, 128),
            wide_type(3, 16, 128),
            sems(3), sems(3), sems(3), sems(3), sems(wide - 1), sems(wide - 1),
            sems(3), sems(3, 4 * z_count), sems(3), sems(2), sems(6),
            sems(3), sems(3, 2 * z_count), sems(3, 2 * (z_count - 1)), sems(3, z_count - 1),
            sems(3), sems(3), sems(3), sems(3), sems(wide - 1), sems(wide - 1), sems(3), sems(3),
            sems(5),
        ],
        compiler_params=pltpu.CompilerParams(
            collective_id=0, has_side_effects=True, vmem_limit_bytes=62 * 2**20
        ),
    )(
        tokens.reshape(micro, block, width), clip_ids, w_qkv, w_out.T, w_fc1, w_fc2.T, small,
        grad_out.reshape(micro, block, width),
    )
    part = width // 4
    grad_qkv = jnp.stack([out_g[0, :, 0:part], out_g[0, :, 2 * part : 3 * part], out_g[0, :, part : 2 * part]])
    return (
        out_tok[:, None],
        out_gtok.astype(F32)[:, None],
        grad_qkv,
        out_g[0, :, 3 * part :].T,
        out_g[1],
        out_g[2].T,
        out_vec[0:8, 0:depth],
        out_vec[8:12, 0:depth].reshape(4 * depth),
    )


def layer_norm(values, scaling, shifting):
    average = jnp.mean(values, axis=-1, keepdims=True)
    centred = values - average
    variance = jnp.mean(centred * centred, axis=-1, keepdims=True)
    return centred * lax.rsqrt(variance + 1e-06) * scaling + shifting


def exact_gelu(values):
    return jax.nn.gelu(values, approximate=False)


def block_scores(query_block, keys, clip_block, clip_row, block_start, score_scale):
    block_rows = query_block.shape[0]
    length = keys.shape[0]
    scores = (
        jnp.einsum("qhd,khd->hqk", query_block, keys, preferred_element_type=jnp.float32)
        * score_scale
    )
    key_place = lax.broadcasted_iota(jnp.int32, (block_rows, length), 1)
    query_place = block_start + lax.broadcasted_iota(jnp.int32, (block_rows, length), 0)
    allowed = (clip_block[:, None] == clip_row[None, :]) & (clip_row[None, :] >= 0) | (
        query_place == key_place
    )
    return jnp.where(allowed[None], scores, -1e30)


def row_forward(query, keys, values, clip_row, score_scale):
    length = query.shape[0]
    block_rows = min(512, length)

    def one_block(block_start):
        scores = block_scores(query, keys, clip_row, clip_row, block_start, score_scale)
        row_max = jnp.max(scores, axis=-1, keepdims=True)
        weights = jnp.exp(scores - row_max)
        row_sum = jnp.sum(weights, axis=-1, keepdims=True)
        probabilities = (weights / row_sum).astype(jnp.bfloat16)
        mixed = jnp.einsum(
            "hqk,khd->qhd", probabilities, values, preferred_element_type=jnp.float32
        )
        return (mixed, (row_max + jnp.log(row_sum))[..., 0])

    starts = lax.broadcasted_iota(jnp.int32, (length // block_rows,), 0) * block_rows
    mixed, log_totals = lax.map(one_block, starts)
    return (mixed.reshape(length, -1), log_totals)


def row_backward(query, keys, values, clip_row, log_totals, grad_heads, score_scale):
    length = query.shape[0]
    block_rows = min(512, length)

    def one_block(running, element):
        key_grad, value_grad = running
        block_start, block_totals = element
        scores = block_scores(query, keys, clip_row, clip_row, block_start, score_scale)
        probabilities = jnp.exp(scores - block_totals[..., None])
        prob_grad = jnp.einsum(
            "qhd,khd->hqk", grad_heads, values, preferred_element_type=jnp.float32
        )
        value_grad = value_grad + jnp.einsum(
            "hqk,qhd->khd",
            probabilities.astype(jnp.bfloat16),
            grad_heads,
            preferred_element_type=jnp.float32,
        )
        score_grad = probabilities * (
            prob_grad - jnp.sum(probabilities * prob_grad, axis=-1, keepdims=True)
        )
        score_grad = score_grad.astype(jnp.bfloat16)
        query_grad = (
            jnp.einsum("hqk,khd->qhd", score_grad, keys, preferred_element_type=jnp.float32)
            * score_scale
        )
        key_grad = (
            key_grad
            + jnp.einsum("hqk,qhd->khd", score_grad, query, preferred_element_type=jnp.float32)
            * score_scale
        )
        return ((key_grad, value_grad), query_grad)

    starts = lax.broadcasted_iota(jnp.int32, (length // block_rows,), 0) * block_rows
    zero_grads = jnp.zeros(keys.shape, jnp.float32)
    (key_grad, value_grad), query_grads = lax.scan(
        one_block, (zero_grads, zero_grads), (starts, log_totals)
    )
    return (query_grads.reshape(query.shape), key_grad, value_grad)


def local(tokens, clip_ids, w_qkv, w_out, w_fc1, w_fc2, norm_bias, fc1_bias, grad_out):
    micro_count = tokens.shape[0]
    row_count = tokens.shape[1]
    width = tokens.shape[3]
    local_width = w_qkv.shape[2]
    local_hidden = w_fc1.shape[1]
    heads_here = local_width // HEAD_DIM
    score_scale = HEAD_DIM ** (-0.5)
    narrow_index = lax.axis_index("narrow")

    def spread_rows(values):
        return lax.all_gather(values, "narrow", axis=1, tiled=True)

    def fold_rows(values):
        return lax.psum_scatter(values, "narrow", scatter_dimension=1, tiled=True)

    def spread_grads(values):
        return lax.all_gather(values, "narrow", axis=1, tiled=True)

    def fold_grads(values):
        return lax.psum_scatter(values, "narrow", scatter_dimension=1, tiled=True)

    def forward_rows(element):
        return row_forward(element[0], element[1], element[2], element[3], score_scale)

    def backward_rows(element):
        return row_backward(
            element[0], element[1], element[2], element[3], element[4], element[5], score_scale
        )

    results = []
    input_grads = []
    shards = None
    for number in range(micro_count):
        qkv_full = lax.all_gather(w_qkv, "wide", axis=1, tiled=True)
        out_full = lax.all_gather(w_out, "wide", axis=1, tiled=True)
        fc1_full = lax.all_gather(w_fc1, "wide", axis=0, tiled=True)
        fc2_full = lax.all_gather(w_fc2, "wide", axis=1, tiled=True)
        vector_full = lax.all_gather(norm_bias, "wide", axis=1, tiled=True)
        hidden_bias_full = lax.all_gather(fc1_bias, "wide", axis=0, tiled=True)
        vectors = vector_full.astype(jnp.float32)
        hidden_total = hidden_bias_full.shape[0]
        column_start = narrow_index * local_width
        hidden_start = narrow_index * local_hidden
        fc_bias = lax.dynamic_slice_in_dim(hidden_bias_full, hidden_start, local_hidden, 0).astype(
            jnp.float32
        )
        query_bias = lax.dynamic_slice_in_dim(vectors[2], column_start, local_width, 0)
        value_bias = lax.dynamic_slice_in_dim(vectors[3], column_start, local_width, 0)
        inputs = tokens[number].astype(jnp.float32)
        clip_rows = clip_ids[number]
        normed1 = layer_norm(inputs, vectors[0], vectors[1]).astype(jnp.bfloat16)
        rows_one = spread_rows(normed1)
        length = rows_one.shape[1]
        projected = jnp.einsum(
            "rld,jde->jrle", rows_one, qkv_full, preferred_element_type=jnp.float32
        )
        bias_three = jnp.stack([query_bias, jnp.zeros_like(query_bias), value_bias])
        qkv_low = (projected + bias_three[:, None, None, :]).astype(jnp.bfloat16)
        split_heads = qkv_low.reshape(3, row_count, length, heads_here, HEAD_DIM)
        attended, log_totals = lax.map(
            forward_rows, (split_heads[0], split_heads[1], split_heads[2], clip_rows)
        )
        attended = attended.astype(jnp.bfloat16)
        attention_part = jnp.einsum(
            "rle,ed->rld", attended, out_full, preferred_element_type=jnp.float32
        )
        hidden1 = inputs + fold_rows(attention_part) + vectors[4]
        normed2 = layer_norm(hidden1, vectors[5], vectors[6]).astype(jnp.bfloat16)
        rows_two = spread_rows(normed2)
        pre_act = (
            jnp.einsum("rld,df->rlf", rows_two, fc1_full, preferred_element_type=jnp.float32)
            + fc_bias
        )
        act_low = exact_gelu(pre_act).astype(jnp.bfloat16)
        mlp_part = jnp.einsum("rlf,fd->rld", act_low, fc2_full, preferred_element_type=jnp.float32)
        result = (hidden1 + fold_rows(mlp_part) + vectors[7]).astype(jnp.bfloat16)
        upstream = grad_out[number].astype(jnp.float32)
        up_low = grad_out[number]
        fc2_bias_grad = jnp.sum(upstream, axis=(0, 1))
        up_rows = spread_grads(up_low)
        fc2_grad = jnp.einsum("rlf,rld->fd", act_low, up_rows, preferred_element_type=jnp.float32)
        act_grad = jnp.einsum("rld,fd->rlf", up_rows, fc2_full, preferred_element_type=jnp.float32)
        _, gelu_pull = jax.vjp(exact_gelu, pre_act)
        pre_grad = gelu_pull(act_grad)[0].astype(jnp.bfloat16)
        fc1_bias_grad = jnp.sum(pre_grad.astype(jnp.float32), axis=(0, 1))
        fc1_grad = jnp.einsum("rld,rlf->df", rows_two, pre_grad, preferred_element_type=jnp.float32)
        normed2_grad = fold_grads(
            jnp.einsum("rlf,df->rld", pre_grad, fc1_full, preferred_element_type=jnp.float32)
        )
        _, norm2_pull = jax.vjp(layer_norm, hidden1, vectors[5], vectors[6])
        hidden1_grad, gain2_grad, shift2_grad = norm2_pull(normed2_grad)
        hidden1_grad = hidden1_grad + upstream
        attn_low = hidden1_grad.astype(jnp.bfloat16)
        out_bias_grad = jnp.sum(attn_low.astype(jnp.float32), axis=(0, 1))
        attn_rows = spread_grads(attn_low)
        out_grad = jnp.einsum(
            "rle,rld->ed", attended, attn_rows, preferred_element_type=jnp.float32
        )
        heads_grad = jnp.einsum(
            "rld,ed->rle", attn_rows, out_full, preferred_element_type=jnp.float32
        ).astype(jnp.bfloat16)
        heads_grad = heads_grad.reshape(row_count, length, heads_here, HEAD_DIM)
        query_grad, key_grad, value_grad = lax.map(
            backward_rows,
            (split_heads[0], split_heads[1], split_heads[2], clip_rows, log_totals, heads_grad),
        )
        qkv_grad = (
            jnp.stack([query_grad, key_grad, value_grad])
            .reshape(3, row_count, length, local_width)
            .astype(jnp.bfloat16)
        )
        qkv_grad_wide = qkv_grad.astype(jnp.float32)
        query_bias_grad = jnp.sum(qkv_grad_wide[0], axis=(0, 1))
        value_bias_grad = jnp.sum(qkv_grad_wide[2], axis=(0, 1))
        qkv_weight_grad = jnp.einsum(
            "rld,jrle->jde", rows_one, qkv_grad, preferred_element_type=jnp.float32
        )
        normed1_grad = fold_grads(
            jnp.einsum("jrle,jde->rld", qkv_grad, qkv_full, preferred_element_type=jnp.float32)
        )
        _, norm1_pull = jax.vjp(layer_norm, inputs, vectors[0], vectors[1])
        input_grad, gain1_grad, shift1_grad = norm1_pull(normed1_grad)
        input_grad = input_grad + hidden1_grad
        blank_width = jnp.zeros((width,), jnp.float32)
        query_placed = lax.dynamic_update_slice_in_dim(
            blank_width, query_bias_grad, column_start, 0
        )
        value_placed = lax.dynamic_update_slice_in_dim(
            blank_width, value_bias_grad, column_start, 0
        )
        vector_grad = jnp.stack(
            [
                gain1_grad,
                shift1_grad,
                query_placed,
                value_placed,
                out_bias_grad,
                gain2_grad,
                shift2_grad,
                fc2_bias_grad,
            ]
        )
        hidden_placed = lax.dynamic_update_slice_in_dim(
            jnp.zeros((hidden_total,), jnp.float32), fc1_bias_grad, hidden_start, 0
        )
        grads = (qkv_weight_grad, out_grad, fc1_grad, fc2_grad, vector_grad, hidden_placed)
        result, input_grad, grads = (result, input_grad, grads)
        results.append(result)
        input_grads.append(input_grad)
        vector_sums = lax.psum(
            (
                lax.psum_scatter(grads[4], "wide", scatter_dimension=1, tiled=True),
                lax.psum_scatter(grads[5], "wide", scatter_dimension=0, tiled=True),
            ),
            "narrow",
        )
        settled = (
            lax.psum_scatter(grads[0], "wide", scatter_dimension=1, tiled=True),
            lax.psum_scatter(grads[1], "wide", scatter_dimension=1, tiled=True),
            lax.psum_scatter(grads[2], "wide", scatter_dimension=0, tiled=True),
            lax.psum_scatter(grads[3], "wide", scatter_dimension=1, tiled=True),
            vector_sums[0],
            vector_sums[1],
        )
        shards = settled if shards is None else jax.tree.map(jnp.add, shards, settled)
    return (
        jnp.stack(results),
        jnp.stack(input_grads),
        shards[0],
        shards[1],
        shards[2],
        shards[3],
        shards[4],
        shards[5],
    )


def solution(mesh):
    in_specs = (
        P(None, "wide", "narrow", None),
        P(None, "wide", None),
        P(None, "wide", "narrow"),
        P("narrow", "wide"),
        P("wide", "narrow"),
        P("narrow", "wide"),
        P(None, "wide"),
        P("wide"),
        P(None, "wide", "narrow", None),
    )
    out_specs = (
        P(None, "wide", "narrow", None),
        P(None, "wide", "narrow", None),
        P(None, "wide", "narrow"),
        P("narrow", "wide"),
        P("wide", "narrow"),
        P("narrow", "wide"),
        P(None, "wide"),
        P("wide"),
    )

    def fits(tokens, w_qkv, w_fc1):
        wide, narrow = mesh.shape["wide"], mesh.shape["narrow"]
        width, hidden = w_fc1.shape
        return (
            wide == 8
            and narrow == 4
            and tokens.shape[:2] == (narrow, wide)
            and tokens.shape[2] % (128 * narrow) == 0
            and width == 12 * HEAD_DIM
            and hidden == narrow * width
        )

    def whole(tokens, clip_ids, w_qkv, w_out, w_fc1, w_fc2, norm_bias, fc1_bias, grad_out):
        chosen = fused_local if fits(tokens, w_qkv, w_fc1) else local
        placed = jax.shard_map(chosen, mesh=mesh, in_specs=in_specs, out_specs=out_specs, check_vma=False)
        return placed(tokens, clip_ids, w_qkv, w_out, w_fc1, w_fc2, norm_bias, fc1_bias, grad_out)

    return whole
```

```python
import functools

import jax
import jax.numpy as jnp
from jax import lax
from jax.experimental import pallas as pl
from jax.experimental.pallas import tpu as pltpu
from jax.sharding import PartitionSpec as P

HEAD_DIM = 64
LATE_OUTPUT = 1
MESH = pl.DeviceIdType.MESH
BF16 = jnp.bfloat16
F32 = jnp.float32
NN = (((1,), (0,)), ((), ()))
NT = (((1,), (1,)), ((), ()))
TN = (((0,), (0,)), ((), ()))
GATHER_Z_FIRST = (False, False, False)
GATHER_X_EARLY = ((1, 0), (0, 0), (1, 0))
SCATTER_Z_FIRST = (True, False, False)
SCATTER_X_EARLY = ((1, 0), (0, 0), (1, 0))
SCHEDULE = {
    1: ((0, 1, 1, 0), ("z1",), (1, 1, 1, 0), (0, 1, 2, 0),),
    3: ((0, 1, 3, 0), (0, 0, 1, 0), (0, 1, 1, 1), (0, 2, 1, 0), (0, 2, 1, 4), (0, 2, 1, 1), (0, 1, 2, 1), (0, 1, 3, 1), (0, 2, 1, 5), (0, 2, 1, 2), (0, 2, 1, 6), (1, 2, 1, 2), (1, 1, 2, 0), (0, 2, 1, 3), ("xy1",), (0, 2, 1, 7),),
    4: ((1, 1, 3, 0), (1, 0, 1, 0),),
    5: (("gout",), (1, 2, 1, 0),),
    11: ((1, 2, 1, 4),),
    12: ((1, 2, 1, 6),),
    17: ((1, 1, 2, 1),),
    19: (("xy2",),),
    20: ((1, 1, 1, 1), ("z2",),),
    24: ((1, 1, 3, 1),),
    34: ((2, 0, 1, 0),),
    35: ((2, 1, 1, 0),),
    36: ((1, 2, 1, 1), (1, 2, 1, 3), (1, 2, 1, 5), (1, 2, 1, 7), (2, 1, 2, 0), (2, 2, 1, 0),),
    37: ((2, 1, 3, 0),),
    40: ((2, 1, 1, 1),),
    47: ((2, 2, 1, 1), (2, 1, 2, 1), (2, 2, 1, 4),),
    48: ((2, 1, 3, 1), (2, 2, 1, 3),),
    50: ((2, 2, 1, 2), (2, 2, 1, 5),),
    52: ((2, 2, 1, 6), (2, 2, 1, 7),),
    54: (("rs", 2, "a", 2, 1),),
    57: (("rs", 2, "a", 3, 1),),
    58: (("rs", 2, "a", 1, 0),),
    62: (("rs", 2, "a", 1, 1), ("rs", 2, "a", 2, 0),),
    63: (("rs", 2, "a", 3, 0),),
    80: (("rs", 2, "b"),),
    88: (("rs", 1, "a", 3, 1),),
    99: (("rs", 1, "a", 2, 0), ("rs", 1, "a", 1, 0),),
    104: (("rs", 1, "a", 2, 1),),
    107: (("rs", 1, "a", 3, 0), ("rs", 0, "a", 2),),
    108: (("rs", 2, "c"),),
    109: (("rs", 1, "a", 1, 1), ("rs", 0, "a", 1), ("rs", 0, "a", 3),),
    110: (("rs", 1, "b"), ("rs", 0, "b", 3), ("rs", 0, "b", 2), ("rs", 1, "c"), ("rs", 0, "a", 0), ("rs", 0, "b", 1), ("rs", 0, "c"),),
}


def dot(a, b, dims):
    return lax.dot_general(a, b, dims, preferred_element_type=F32)


def aligned(value, step):
    return value if isinstance(value, int) else pl.multiple_of(value, step)


def slab_sum(values):
    rows, width = values.shape
    return jnp.sum(values.reshape(rows // 8, 8, width), axis=0)


def row_kernel(
    tok, clip, wqkv, wout, wfc1, wfc2, small, gout,
    out_tok, out_gtok, out_g, out_vec,
    wts, psum, gsend, recv1, recv2, recv3,
    xrow, urow, normed1, normed2, attn_grad, outrow, gtrow,
    qs, ks, vs, heads, dheads, act, dgelu, dqkv,
    fa, fb, outacc, mask, stats, lse,
    smalls, vecs, qbias, vbias, hbias, vpart, vrecv, vsum, vnar,
    tok_s, tok_r, gout_s, gout_r, small_s, small_r,
    ag_s, ag_r, sib_r, gs_s, gs_r, rs_s, rs1_r, rs2_r, rs3_r,
    ot_s, ot_r, gt_s, gt_r, vp_s, vp_r, vn_s, vn_r, loc,
):
    depth, width = wfc1.shape[0], tok.shape[-1]
    wide = width // depth
    z_count = wide // 2
    w = lax.axis_index("wide")
    n = lax.axis_index("narrow")
    z, x, y, c = w // 2, w % 2, n // 2, n % 2
    length = xrow.shape[0]
    block = length // 4
    here = (w, n)
    sibling = (w, n ^ 1)
    wide_partners = [(w ^ v, n) for v in range(1, wide)]
    narrow_partners = [(w, n ^ v) for v in range(1, 4)]

    def send(src, dst, s_sem, r_sem, to):
        pltpu.make_async_remote_copy(
            src_ref=src, dst_ref=dst, send_sem=s_sem, recv_sem=r_sem,
            device_id=to, device_id_type=MESH,
        ).start()

    def got(ref, r_sem):
        pltpu.make_async_remote_copy(
            src_ref=ref, dst_ref=ref, send_sem=loc.at[0], recv_sem=r_sem,
            device_id=sibling, device_id_type=MESH,
        ).wait_recv()

    def sent(ref, s_sem):
        pltpu.make_async_remote_copy(
            src_ref=ref, dst_ref=ref, send_sem=s_sem, recv_sem=loc.at[0],
            device_id=sibling, device_id_type=MESH,
        ).wait_send()

    def chosen(table, k):
        first, second = table[k]
        return first if first == second else jnp.where(c == 0, first, second)

    gather_x = [chosen(GATHER_X_EARLY, k) for k in range(3)]
    scatter_x = [chosen(SCATTER_X_EARLY, k) for k in range(3)]
    inner = (z == 1) | (z == 2)
    z_offset = [0, 1, jnp.where(inner, 3, 2), jnp.where(inner, 2, 3)]

    def origin(x_early, rel):
        rz, ra, rb = rel
        ox = x ^ (x_early * ra + (1 - x_early) * rb)
        oy = y ^ (x_early * rb + (1 - x_early) * ra)
        return z ^ rz, ox, oy

    def wts_at(k, rel):
        oz, ox, oy = origin(gather_x[k], rel)
        start = (k * 4 + oy * 2 + c) * width + (oz * 2 + ox) * depth
        return wts.at[pl.ds(aligned(start, 32), depth), :]

    def psum_at(k, rel):
        oz, ox, oy = origin(scatter_x[k], rel)
        start = (k * 2 + oy) * width + (oz * 2 + ox) * depth
        return psum.at[pl.ds(aligned(start, 32), depth), :]

    def partner(x_early, dim, v):
        if dim == 0:
            return (w ^ (2 * v), n)
        x_hop = x_early if dim == 1 else 1 - x_early
        return (w ^ x_hop, n ^ (2 * (1 - x_hop)))

    def pass_on(k, rel, dim, v):
        there = list(rel)
        there[dim] = rel[dim] ^ v
        send(
            wts_at(k, rel), wts_at(k, rel), ag_s.at[k],
            ag_r.at[k, there[0] * 4 + there[1] * 2 + there[2]], partner(gather_x[k], dim, v),
        )

    def along_z(k, i, rel):
        if i == 0:
            pass_on(k, rel, 0, 1)
        pl.when(inner)(lambda: pass_on(k, rel, 0, 3 if i < 2 else 1))

    def hand_on(k, phase, i, rel):
        order = (0, 1, 2) if GATHER_Z_FIRST[k] else (1, 0, 2)
        if phase >= 0 and order[phase] == 0:
            along_z(k, i, rel)
        for dim in order[phase + 1 :]:
            if dim == 0:
                along_z(k, i, rel)
            else:
                pass_on(k, rel, dim, 1)
        send(wts_at(k, rel), wts_at(k, rel), ag_s.at[k], sib_r.at[k], sibling)

    def own_along_z(k):
        along_z(k, 0, (0, 0, 0))

    def own_across(k):
        rel = (0, 0, 0)
        pass_on(k, rel, 1, 1)
        pass_on(k, rel, 2, 1)
        send(wts_at(k, rel), wts_at(k, rel), ag_s.at[k], sib_r.at[k], sibling)

    steps = {}

    def gather_steps(k):
        order = (0, 1, 2) if GATHER_Z_FIRST[k] else (1, 0, 2)
        held = [(0, 0, 0)]

        def step(phase, named):
            rel = (z_offset[named[0]], named[1], named[2])
            got(wts_at(k, rel), ag_r.at[k, rel[0] * 4 + rel[1] * 2 + rel[2]])
            hand_on(k, phase, named[0], rel)

        for phase, dim in enumerate(order):
            fresh = []
            for i in range(1, z_count if dim == 0 else 2):
                for j, named in enumerate(held):
                    there = list(named)
                    there[dim] = i
                    fresh.append(tuple(there))
                    steps[(k, phase, i, j)] = functools.partial(step, phase, tuple(there))
            held = held + fresh

    def add_up(k, rel, others):
        here_ref = psum_at(k, rel)
        total = here_ref[...].astype(F32)
        for other in others:
            total = total + other[...].astype(F32)
        return here_ref, total

    nearest_last = list(range(1, z_count)) + [0]

    def scatter_send(k, rz, ra):
        send(
            psum_at(k, (rz, ra, 1)), recv1.at[k, rz * 2 + ra], rs_s.at[k],
            rs1_r.at[k, rz * 2 + ra], partner(scatter_x[k], 2, 1),
        )

    def scatter_first(k):
        for rz in nearest_last:
            for ra in (1, 0):
                scatter_send(k, rz, ra)

    def scatter_first_part(k, part):
        if part == 0:
            for rz in nearest_last:
                scatter_send(k, rz, 1)

        @pl.when(scatter_x[k] == 1 - part)
        def _():
            for rz in nearest_last:
                scatter_send(k, rz, 0)

    def scatter_steps(k):
        def fresh(buffer, sems, i):
            ref = buffer.at[k, i]
            got(ref, sems.at[k, i])
            return ref

        fresh1 = functools.partial(fresh, recv1, rs1_r)
        fresh2 = functools.partial(fresh, recv2, rs2_r)
        fresh3 = functools.partial(fresh, recv3, rs3_r)
        x_early = scatter_x[k]

        def sum_on(rel, others, there, sem, to):
            ref, total = add_up(k, rel, others)
            ref[...] = total.astype(BF16)
            send(ref, there, rs_s.at[k], sem, to)

        def finish_sum(others):
            _, total = add_up(k, (0, 0, 0), others)
            out_g[k] = total

        if SCATTER_Z_FIRST[k]:

            def early_hop(rz):
                sum_on((rz, 1, 0), [fresh1(rz * 2 + 1)], recv2.at[k, rz], rs2_r.at[k, rz], partner(x_early, 1, 1))

            def z_hop(rz):
                others = [fresh1(rz * 2), fresh2(rz)]
                sum_on((rz, 0, 0), others, recv3.at[k, rz - 1], rs3_r.at[k, rz - 1], partner(x_early, 0, rz))

            for rz in range(z_count):
                steps[("rs", k, "a", rz)] = functools.partial(early_hop, rz)
                if rz > 0:
                    steps[("rs", k, "b", rz)] = functools.partial(z_hop, rz)
            steps[("rs", k, "c")] = lambda: finish_sum(
                [fresh1(0), fresh2(0)] + [fresh3(i) for i in range(z_count - 1)]
            )
        else:

            def z_hop(rz, ra):
                i = (rz - 1) * 2 + ra
                sum_on((rz, ra, 0), [fresh1(rz * 2 + ra)], recv2.at[k, i], rs2_r.at[k, i], partner(x_early, 0, rz))

            def early_hop():
                others = [fresh1(1)] + [fresh2(i * 2 + 1) for i in range(z_count - 1)]
                sum_on((0, 1, 0), others, recv3.at[k, 0], rs3_r.at[k, 0], partner(x_early, 1, 1))

            for rz in range(1, z_count):
                for ra in range(2):
                    steps[("rs", k, "a", rz, ra)] = functools.partial(z_hop, rz, ra)
            steps[("rs", k, "b")] = early_hop
            steps[("rs", k, "c")] = lambda: finish_sum(
                [fresh1(0)] + [fresh2(i * 2) for i in range(z_count - 1)] + [fresh3(0)]
            )

    point = [0]

    def service():
        point[0] += 1
        for name in SCHEDULE.get(point[0], ()):
            steps.pop(name)()

    def weights_here(k):
        service()
        got(wts.at[pl.ds(0, 2 * width), :], sib_r.at[k])

    def weight(k, j, columns=slice(None)):
        return wts[pl.ds(aligned((k * 4 + j) * width, 128), width), columns]

    def own_place(k):
        return pl.ds(aligned((k * 4 + n) * width + w * depth, 32), depth)

    wts[own_place(0), 0:192] = wqkv[0]
    wts[own_place(0), 192:384] = wqkv[2]
    wts[own_place(0), 384:576] = wqkv[1]
    wts[own_place(0), 576:768] = wout[...]
    wts[own_place(1), :] = wfc1[...]
    wts[own_place(2), :] = wfc2[...]
    smalls[w] = small[...]

    barrier = pltpu.get_barrier_semaphore()
    for to in wide_partners + narrow_partners:
        pl.semaphore_signal(barrier, inc=1, device_id=to, device_id_type=MESH)
    pl.semaphore_wait(barrier, len(wide_partners) + len(narrow_partners))

    rows_here = pl.ds(aligned(n * block, 128), block)

    def rows_of(to):
        return pl.ds(aligned(to[1] * block, 128), block)

    for i, to in enumerate(wide_partners):
        send(smalls.at[w], smalls.at[w], small_s.at[i], small_r.at[i], to)
    for i, to in enumerate(narrow_partners):
        send(tok.at[to[1]], xrow.at[rows_here, :], tok_s.at[i], tok_r.at[i], to)
    own_along_z(0)
    own_across(0)
    own_tok = pltpu.make_async_copy(tok.at[n], xrow.at[rows_here, :], loc.at[1])
    own_tok.start()
    own_gout = pltpu.make_async_copy(gout.at[n], urow.at[rows_here, :], loc.at[2])
    own_gout.start()

    def start_gout():
        for i, to in enumerate(narrow_partners):
            send(gout.at[to[1]], urow.at[rows_here, :], gout_s.at[i], gout_r.at[i], to)

    for k in range(3):
        gather_steps(k)
    steps[("z1",)] = functools.partial(own_along_z, 1)
    steps[("xy1",)] = functools.partial(own_across, 1)
    steps[("z2",)] = functools.partial(own_along_z, 2)
    steps[("xy2",)] = functools.partial(own_across, 2)
    steps[("gout",)] = start_gout

    ids = clip[n]
    place = lax.broadcasted_iota(jnp.int32, (1, length), 1)
    ids = jnp.where(ids >= 0, ids, -1 - place).astype(F32)
    ids_down = jnp.transpose(jnp.broadcast_to(ids, (128, length)))[:, 0:1]
    mask[...] = jnp.where(ids_down == ids, 0.0, -1e30)

    for i, to in enumerate(wide_partners):
        got(smalls.at[to[0]], small_r.at[i])
    qbias[...] = jnp.zeros_like(qbias)
    vbias[...] = jnp.zeros_like(vbias)
    for i in range(wide):
        part = smalls[i]
        vecs[:, i * depth : (i + 1) * depth] = part[0:8, 0:depth]
        j, half_at = i // 2, (i % 2) * depth
        qbias[j, :, half_at : half_at + depth] = part[2:3, 0:depth]
        vbias[j, :, 64 + half_at : 64 + half_at + depth] = part[3:4, 0:depth]
        for r in range(4):
            at = (i % 2) * 4 * depth + r * depth
            hbias[j, :, at : at + depth] = part[8 + r : 9 + r, 0:depth]

    service()
    own_tok.wait()
    for i, to in enumerate(narrow_partners):
        got(xrow.at[rows_of(to), :], tok_r.at[i])

    def norm_forward(source, gain, shift, column, target):
        def body(i, _):
            rows = pl.ds(aligned(i * block, 128), block)
            v = source[rows, :].astype(F32)
            average = jnp.mean(v, axis=-1, keepdims=True)
            centred = v - average
            rr = lax.rsqrt(jnp.mean(centred * centred, axis=-1, keepdims=True) + 1e-6)
            stats[rows, column : column + 1] = average
            stats[rows, column + 1 : column + 2] = rr
            target[rows, :] = (centred * rr * vecs[gain : gain + 1] + vecs[shift : shift + 1]).astype(BF16)
            return 0

        lax.fori_loop(0, 4, body, 0)

    norm_forward(xrow, 0, 1, 0, normed1)
    service()

    weights_here(0)
    lane = lax.broadcasted_iota(jnp.int32, (1, 256), 1)
    low = lane[:, 0:128] < 64
    for j in range(4):
        projected = dot(normed1[...], weight(0, j, slice(0, 640)), NN)
        slot = slice(256 * j, 256 * j + 256)
        query = (projected[:, 0:256] + qbias[j]).astype(BF16).astype(F32) * 0.125
        qs[:, slot] = jnp.where(lane < 192, query, 0.0).astype(BF16)
        value = projected[:, 128:384] + vbias[j]
        vs[:, slot] = jnp.where(lane >= 64, value, 0.0).astype(BF16)
        ks[:, slot] = jnp.where(lane < 192, projected[:, 384:640], 0.0).astype(BF16)
        service()

    def lanes(j, second):
        return pl.ds(aligned(256 * j + 128 * second, 128), 128)

    def only(head, values):
        return jnp.where(low if head == 0 else ~low, values, jnp.zeros_like(values))

    def query_of(j, head):
        return only(head, qs[:, lanes(j, 0)]) if head < 2 else qs[:, lanes(j, 1)]

    def key_of(j, head):
        return ks[:, lanes(j, 0)] if head < 2 else ks[:, lanes(j, 1)]

    for j in range(4):
        mixed = []
        for head in range(3):
            scores = dot(query_of(j, head), key_of(j, head), NT) + mask[...]
            row_max = jnp.max(scores, axis=1, keepdims=True)
            weights = jnp.exp(scores - row_max)
            row_sum = jnp.sum(weights, axis=1, keepdims=True)
            probs = (weights * (1.0 / row_sum)).astype(BF16)
            lse[j, :, head : head + 1] = row_max + jnp.log(row_sum)
            service()
            value = vs[:, lanes(j, 0)] if head == 0 else vs[:, lanes(j, 1)]
            mixed.append(dot(probs, value, NN))
            service()
        heads[:, lanes(j, 0)] = mixed[0].astype(BF16)
        heads[:, lanes(j, 1)] = jnp.where(low, mixed[1], mixed[2]).astype(BF16)

    fb[...] = xrow[...].astype(F32) + vecs[4:5]
    for j in range(4):
        fb[...] += dot(heads[:, 256 * j : 256 * j + 256], weight(0, j, slice(512, 768)), NT)
        service()
    fa[...] = fb[...]
    norm_forward(fa, 5, 6, 2, normed2)

    weights_here(1)
    for j in range(4):
        pre = dot(normed2[...], weight(1, j), NN) + hbias[j]
        service()
        cumulative = 0.5 * (1.0 + lax.erf(pre * (0.5**0.5)))
        density = jnp.exp(pre * pre * -0.5) * (0.5 / jnp.pi) ** 0.5
        act[j] = (pre * cumulative).astype(BF16)
        dgelu[j] = (cumulative + pre * density).astype(BF16)
        service()

    def give(k, j, slot, product):
        if k < 2:
            sent(gsend.at[slot], gs_s.at[slot])
        gsend[slot] = product.astype(BF16)
        place = pl.ds(aligned((k * 2 + j) * width, 128), width)
        send(gsend.at[slot], psum.at[place, :], gs_s.at[slot], gs_r.at[k * 2 + j], sibling)

    def keep(k, j, product):
        place = pl.ds(aligned((k * 2 + j) * width, 128), width)
        service()
        got(psum.at[place, :], gs_r.at[k * 2 + j])
        psum[place, :] = (product + psum[place, :].astype(F32)).astype(BF16)

    service()
    own_gout.wait()
    for i, to in enumerate(narrow_partners):
        got(urow.at[rows_of(to), :], gout_r.at[i])
    for j in range(2):
        give(2, j, j, dot(urow[...], act[2 * j + 1 - c], TN))
        service()
    for j in range(2):
        keep(2, j, dot(urow[...], act[2 * j + c], TN))
        service()
    scatter_first(2)
    scatter_steps(2)
    weights_here(2)

    def output():
        for j in range(4):
            outacc[...] = (fa if j == 0 else outacc)[...] + dot(act[j], weight(2, j), NT)
            service()
        outrow[...] = (outacc[...] + vecs[7:8]).astype(BF16)
        for i, to in enumerate(narrow_partners):
            send(outrow.at[rows_of(to), :], out_tok.at[n], ot_s.at[i], ot_r.at[i], to)
        copy = pltpu.make_async_copy(outrow.at[rows_here, :], out_tok.at[n], loc.at[3])
        copy.start()
        return copy

    if LATE_OUTPUT == 0:
        own_out = output()

    def put(row, i, values):
        vpart[i, row : row + 1, 0:depth] = values

    def put_row(row, values):
        for i in range(wide):
            put(row, i, values[:, i * depth : (i + 1) * depth])

    def column_sum(values):
        return jnp.sum(values.astype(F32), axis=0, keepdims=True)

    vpart[...] = jnp.zeros_like(vpart)
    put_row(7, column_sum(urow[...]))
    for j in range(4):
        grad = dot(urow[...], weight(2, j), NN) * dgelu[j].astype(F32)
        dgelu[j] = grad.astype(BF16)
        total = column_sum(dgelu[j])
        for i in range(2):
            for r in range(4):
                at = (i * 4 + r) * depth
                put(8 + r, 2 * j + i, total[:, at : at + depth])
        service()
    for j in range(2):
        give(1, j, j, dot(normed2[...], dgelu[2 * j + 1 - c], TN))
        service()
    for j in range(2):
        keep(1, j, dot(normed2[...], dgelu[2 * j + c], TN))
        service()
    scatter_first(1)
    scatter_steps(1)
    for j in range(4):
        product = dot(dgelu[j], weight(1, j), NT)
        fb[...] = product if j == 0 else fb[...] + product
        service()

    def norm_backward(source, grad, gain, column, extra, target, rounded):
        def body(i, sums):
            rows = pl.ds(aligned(i * block, 128), block)
            rr = stats[rows, column + 1 : column + 2]
            xhat = (source[rows, :].astype(F32) - stats[rows, column : column + 1]) * rr
            n_grad = grad[rows, :]
            u = n_grad * vecs[gain : gain + 1]
            inner = u - jnp.mean(u, axis=-1, keepdims=True) - xhat * jnp.mean(u * xhat, axis=-1, keepdims=True)
            result = rr * inner + extra[rows, :].astype(F32)
            if target is not None:
                target[rows, :] = result
            low_result = result.astype(BF16)
            rounded[rows, :] = low_result
            return (
                sums[0] + slab_sum(n_grad * xhat),
                sums[1] + slab_sum(n_grad),
                sums[2] + slab_sum(low_result.astype(F32)),
            )

        zero = jnp.zeros((8, width), F32)
        sums = lax.fori_loop(0, 4, body, (zero, zero, zero))
        return [jnp.sum(s, axis=0, keepdims=True) for s in sums]

    gain2, shift2, attn_total = norm_backward(fa, fb, 5, 2, urow, fb, attn_grad)
    if LATE_OUTPUT == 1:
        own_out = output()
    put_row(5, gain2)
    put_row(6, shift2)
    put_row(4, attn_total)

    for j in range(4):
        back = dot(attn_grad[...], weight(0, j, slice(512, 768)), NN)
        dheads[:, 256 * j : 256 * j + 256] = jnp.where(lane >= 64, back, 0.0).astype(BF16)
        service()

    def attention_backward(j):
        def value_of(head):
            return vs[:, lanes(j, 0)] if head == 0 else vs[:, lanes(j, 1)]

        def upstream_of(head):
            if head == 0:
                return dheads[:, lanes(j, 0)]
            return only(head - 1, dheads[:, lanes(j, 1)])

        dq, dk, dv = [], [], []
        for head in range(3):
            query, key, up = query_of(j, head), key_of(j, head), upstream_of(head)
            second = int(head > 0)
            delta = jnp.sum(
                up.astype(F32) * heads[:, lanes(j, second)].astype(F32), axis=1, keepdims=True
            )
            scores = dot(query, key, NT) + mask[...]
            soft = jnp.exp(scores - lse[j, :, head : head + 1])
            prob_grad = dot(up, value_of(head), NT)
            score_grad = (soft * (prob_grad - delta)).astype(BF16)
            service()
            dq.append(dot(score_grad, key, NN))
            dk.append(dot(score_grad, query, TN))
            dv.append(dot(soft.astype(BF16), up, TN))
            service()
        dqkv[:, 0:128] = (jnp.where(low, dq[0], dq[1]) * 0.125).astype(BF16)
        dqkv[:, 128:256] = (dq[2] * 0.125 + dv[0]).astype(BF16)
        dqkv[:, 256:384] = (dv[1] + dv[2]).astype(BF16)
        dqkv[:, 384:512] = (dk[0] + dk[1]).astype(BF16)
        dqkv[:, 512:640] = dk[2].astype(BF16)
        total = column_sum(dqkv[:, 0:384])
        for i in range(2):
            put(2, 2 * j + i, total[:, i * depth : (i + 1) * depth])
            put(3, 2 * j + i, total[:, (2 + i) * depth : (3 + i) * depth])

    def projection_grad(j):
        first = dot(normed1[...], dqkv[...], TN)
        second = dot(attn_grad[...], heads[:, pl.ds(aligned(256 * j, 128), 256)], TN)
        return jnp.concatenate(
            [first[:, 0:512], first[:, 512:640] + second[:, 0:128], second[:, 128:256]], axis=1
        )

    for i, half in enumerate((1 - y, y)):
        for own in (False, True):
            j = 2 * half + (c if own else 1 - c)
            attention_backward(j)
            if own:
                keep(0, half, projection_grad(j))
            else:
                give(0, half, i, projection_grad(j))
            service()
            product = dot(dqkv[...], weight(0, j, slice(0, 640)), NT)
            fa[...] = product if i == 0 and not own else fa[...] + product
            service()
        scatter_first_part(0, i)
        if i == 0:
            scatter_steps(0)

    gain1, shift1, _ = norm_backward(xrow, fa, 0, 0, fb, None, gtrow)
    for i, to in enumerate(narrow_partners):
        rows = pl.ds(aligned(to[1] * block, 128), block)
        send(gtrow.at[rows, :], out_gtok.at[n], gt_s.at[i], gt_r.at[i], to)
    own_gtok = pltpu.make_async_copy(gtrow.at[rows_here, :], out_gtok.at[n], loc.at[4])
    own_gtok.start()
    service()
    put_row(0, gain1)
    put_row(1, shift1)
    for i, to in enumerate(wide_partners):
        send(vpart.at[to[0]], vrecv.at[i], vp_s.at[i], vp_r.at[i], to)
    total = vpart[w]
    for i in range(len(wide_partners)):
        got(vrecv.at[i], vp_r.at[i])
        total = total + vrecv[i]
    vsum[...] = total
    for i, to in enumerate(narrow_partners):
        send(vsum, vnar.at[i], vn_s.at[i], vn_r.at[i], to)
    service()
    assert not steps
    for i in range(3):
        got(vnar.at[i], vn_r.at[i])
        total = total + vnar[i]
    out_vec[...] = total

    for i, to in enumerate(narrow_partners):
        got(out_tok.at[to[1]], ot_r.at[i])
        got(out_gtok.at[to[1]], gt_r.at[i])
        sent(tok.at[0], tok_s.at[i])
        sent(gout.at[0], gout_s.at[i])
        sent(outrow.at[pl.ds(0, block), :], ot_s.at[i])
        sent(gtrow.at[pl.ds(0, block), :], gt_s.at[i])
        sent(vsum, vn_s.at[i])
    for i in range(len(wide_partners)):
        sent(smalls.at[0], small_s.at[i])
        sent(vpart.at[0], vp_s.at[i])
    for k in range(3):
        z_sends = (1, 2 + 3) if GATHER_Z_FIRST[k] else (2, 4 + 6)
        across = (1 + 3) + (1 + 3 + 4) if GATHER_Z_FIRST[k] else 1 + (1 + 1 + 6)
        for place, count in zip((~inner, inner), z_sends):
            rows = (count + across + 4 * z_count) * depth
            pl.when(place)(functools.partial(sent, wts.at[pl.ds(0, rows), :], ag_s.at[k]))
        sends = 4 * z_count - 1
        sent(psum.at[pl.ds(0, sends * depth), :], rs_s.at[k])
    for slot in range(2):
        sent(gsend.at[slot], gs_s.at[slot])
    own_out.wait()
    own_gtok.wait()


def fused_local(tokens, clip_ids, w_qkv, w_out, w_fc1, w_fc2, norm_bias, fc1_bias, grad_out):
    micro, _, block, width = tokens.shape
    depth, hidden = w_fc1.shape
    wide = width // depth
    z_count = wide // 2
    length = micro * block
    small = jnp.concatenate([norm_bias, fc1_bias.reshape(4, depth)]).astype(F32)
    small = jnp.pad(small, ((0, 4), (0, 128 - depth)))

    def anywhere():
        return pl.BlockSpec(memory_space=pl.ANY)

    def vmem():
        return pl.BlockSpec(memory_space=pltpu.VMEM)

    def flat(*shape):
        return pltpu.VMEM(shape, BF16)

    def wide_type(*shape):
        return pltpu.VMEM(shape, F32)

    def sems(*shape):
        return pltpu.SemaphoreType.DMA(shape)

    out_tok, out_gtok, out_g, out_vec = pl.pallas_call(
        row_kernel,
        out_shape=(
            jax.ShapeDtypeStruct((micro, block, width), BF16),
            jax.ShapeDtypeStruct((micro, block, width), BF16),
            jax.ShapeDtypeStruct((3, depth, width), F32),
            jax.ShapeDtypeStruct((16, 128), F32),
        ),
        in_specs=[anywhere()] + [vmem()] * 6 + [anywhere()],
        out_specs=(anywhere(), anywhere(), vmem(), vmem()),
        scratch_shapes=[
            flat(12 * width, hidden),
            flat(6 * width, hidden),
            flat(2, width, hidden),
            flat(3, 2 * z_count, depth, hidden),
            flat(3, 2 * (z_count - 1), depth, hidden),
            flat(3, z_count - 1, depth, hidden),
            *[flat(length, width)] * 7,
            *[flat(length, 1024)] * 5,
            flat(4, length, hidden),
            flat(4, length, hidden),
            flat(length, 640),
            wide_type(length, width),
            wide_type(length, width),
            wide_type(length, width),
            wide_type(length, length),
            wide_type(length, 128),
            wide_type(4, length, 128),
            wide_type(wide, 16, 128),
            wide_type(8, width),
            wide_type(4, 1, 256),
            wide_type(4, 1, 256),
            wide_type(4, 1, hidden),
            wide_type(wide, 16, 128),
            wide_type(wide - 1, 16, 128),
            wide_type(16, 128),
            wide_type(3, 16, 128),
            sems(3), sems(3), sems(3), sems(3), sems(wide - 1), sems(wide - 1),
            sems(3), sems(3, 4 * z_count), sems(3), sems(2), sems(6),
            sems(3), sems(3, 2 * z_count), sems(3, 2 * (z_count - 1)), sems(3, z_count - 1),
            sems(3), sems(3), sems(3), sems(3), sems(wide - 1), sems(wide - 1), sems(3), sems(3),
            sems(5),
        ],
        compiler_params=pltpu.CompilerParams(
            collective_id=0, has_side_effects=True, vmem_limit_bytes=62 * 2**20
        ),
    )(
        tokens.reshape(micro, block, width), clip_ids, w_qkv, w_out.T, w_fc1, w_fc2.T, small,
        grad_out.reshape(micro, block, width),
    )
    part = width // 4
    grad_qkv = jnp.stack([out_g[0, :, 0:part], out_g[0, :, 2 * part : 3 * part], out_g[0, :, part : 2 * part]])
    return (
        out_tok[:, None],
        out_gtok.astype(F32)[:, None],
        grad_qkv,
        out_g[0, :, 3 * part :].T,
        out_g[1],
        out_g[2].T,
        out_vec[0:8, 0:depth],
        out_vec[8:12, 0:depth].reshape(4 * depth),
    )


def layer_norm(values, scaling, shifting):
    average = jnp.mean(values, axis=-1, keepdims=True)
    centred = values - average
    variance = jnp.mean(centred * centred, axis=-1, keepdims=True)
    return centred * lax.rsqrt(variance + 1e-06) * scaling + shifting


def exact_gelu(values):
    return jax.nn.gelu(values, approximate=False)


def block_scores(query_block, keys, clip_block, clip_row, block_start, score_scale):
    block_rows = query_block.shape[0]
    length = keys.shape[0]
    scores = (
        jnp.einsum("qhd,khd->hqk", query_block, keys, preferred_element_type=jnp.float32)
        * score_scale
    )
    key_place = lax.broadcasted_iota(jnp.int32, (block_rows, length), 1)
    query_place = block_start + lax.broadcasted_iota(jnp.int32, (block_rows, length), 0)
    allowed = (clip_block[:, None] == clip_row[None, :]) & (clip_row[None, :] >= 0) | (
        query_place == key_place
    )
    return jnp.where(allowed[None], scores, -1e30)


def row_forward(query, keys, values, clip_row, score_scale):
    length = query.shape[0]
    block_rows = min(512, length)

    def one_block(block_start):
        scores = block_scores(query, keys, clip_row, clip_row, block_start, score_scale)
        row_max = jnp.max(scores, axis=-1, keepdims=True)
        weights = jnp.exp(scores - row_max)
        row_sum = jnp.sum(weights, axis=-1, keepdims=True)
        probabilities = (weights / row_sum).astype(jnp.bfloat16)
        mixed = jnp.einsum(
            "hqk,khd->qhd", probabilities, values, preferred_element_type=jnp.float32
        )
        return (mixed, (row_max + jnp.log(row_sum))[..., 0])

    starts = lax.broadcasted_iota(jnp.int32, (length // block_rows,), 0) * block_rows
    mixed, log_totals = lax.map(one_block, starts)
    return (mixed.reshape(length, -1), log_totals)


def row_backward(query, keys, values, clip_row, log_totals, grad_heads, score_scale):
    length = query.shape[0]
    block_rows = min(512, length)

    def one_block(running, element):
        key_grad, value_grad = running
        block_start, block_totals = element
        scores = block_scores(query, keys, clip_row, clip_row, block_start, score_scale)
        probabilities = jnp.exp(scores - block_totals[..., None])
        prob_grad = jnp.einsum(
            "qhd,khd->hqk", grad_heads, values, preferred_element_type=jnp.float32
        )
        value_grad = value_grad + jnp.einsum(
            "hqk,qhd->khd",
            probabilities.astype(jnp.bfloat16),
            grad_heads,
            preferred_element_type=jnp.float32,
        )
        score_grad = probabilities * (
            prob_grad - jnp.sum(probabilities * prob_grad, axis=-1, keepdims=True)
        )
        score_grad = score_grad.astype(jnp.bfloat16)
        query_grad = (
            jnp.einsum("hqk,khd->qhd", score_grad, keys, preferred_element_type=jnp.float32)
            * score_scale
        )
        key_grad = (
            key_grad
            + jnp.einsum("hqk,qhd->khd", score_grad, query, preferred_element_type=jnp.float32)
            * score_scale
        )
        return ((key_grad, value_grad), query_grad)

    starts = lax.broadcasted_iota(jnp.int32, (length // block_rows,), 0) * block_rows
    zero_grads = jnp.zeros(keys.shape, jnp.float32)
    (key_grad, value_grad), query_grads = lax.scan(
        one_block, (zero_grads, zero_grads), (starts, log_totals)
    )
    return (query_grads.reshape(query.shape), key_grad, value_grad)


def local(tokens, clip_ids, w_qkv, w_out, w_fc1, w_fc2, norm_bias, fc1_bias, grad_out):
    micro_count = tokens.shape[0]
    row_count = tokens.shape[1]
    width = tokens.shape[3]
    local_width = w_qkv.shape[2]
    local_hidden = w_fc1.shape[1]
    heads_here = local_width // HEAD_DIM
    score_scale = HEAD_DIM ** (-0.5)
    narrow_index = lax.axis_index("narrow")

    def spread_rows(values):
        return lax.all_gather(values, "narrow", axis=1, tiled=True)

    def fold_rows(values):
        return lax.psum_scatter(values, "narrow", scatter_dimension=1, tiled=True)

    def spread_grads(values):
        return lax.all_gather(values, "narrow", axis=1, tiled=True)

    def fold_grads(values):
        return lax.psum_scatter(values, "narrow", scatter_dimension=1, tiled=True)

    def forward_rows(element):
        return row_forward(element[0], element[1], element[2], element[3], score_scale)

    def backward_rows(element):
        return row_backward(
            element[0], element[1], element[2], element[3], element[4], element[5], score_scale
        )

    results = []
    input_grads = []
    shards = None
    for number in range(micro_count):
        qkv_full = lax.all_gather(w_qkv, "wide", axis=1, tiled=True)
        out_full = lax.all_gather(w_out, "wide", axis=1, tiled=True)
        fc1_full = lax.all_gather(w_fc1, "wide", axis=0, tiled=True)
        fc2_full = lax.all_gather(w_fc2, "wide", axis=1, tiled=True)
        vector_full = lax.all_gather(norm_bias, "wide", axis=1, tiled=True)
        hidden_bias_full = lax.all_gather(fc1_bias, "wide", axis=0, tiled=True)
        vectors = vector_full.astype(jnp.float32)
        hidden_total = hidden_bias_full.shape[0]
        column_start = narrow_index * local_width
        hidden_start = narrow_index * local_hidden
        fc_bias = lax.dynamic_slice_in_dim(hidden_bias_full, hidden_start, local_hidden, 0).astype(
            jnp.float32
        )
        query_bias = lax.dynamic_slice_in_dim(vectors[2], column_start, local_width, 0)
        value_bias = lax.dynamic_slice_in_dim(vectors[3], column_start, local_width, 0)
        inputs = tokens[number].astype(jnp.float32)
        clip_rows = clip_ids[number]
        normed1 = layer_norm(inputs, vectors[0], vectors[1]).astype(jnp.bfloat16)
        rows_one = spread_rows(normed1)
        length = rows_one.shape[1]
        projected = jnp.einsum(
            "rld,jde->jrle", rows_one, qkv_full, preferred_element_type=jnp.float32
        )
        bias_three = jnp.stack([query_bias, jnp.zeros_like(query_bias), value_bias])
        qkv_low = (projected + bias_three[:, None, None, :]).astype(jnp.bfloat16)
        split_heads = qkv_low.reshape(3, row_count, length, heads_here, HEAD_DIM)
        attended, log_totals = lax.map(
            forward_rows, (split_heads[0], split_heads[1], split_heads[2], clip_rows)
        )
        attended = attended.astype(jnp.bfloat16)
        attention_part = jnp.einsum(
            "rle,ed->rld", attended, out_full, preferred_element_type=jnp.float32
        )
        hidden1 = inputs + fold_rows(attention_part) + vectors[4]
        normed2 = layer_norm(hidden1, vectors[5], vectors[6]).astype(jnp.bfloat16)
        rows_two = spread_rows(normed2)
        pre_act = (
            jnp.einsum("rld,df->rlf", rows_two, fc1_full, preferred_element_type=jnp.float32)
            + fc_bias
        )
        act_low = exact_gelu(pre_act).astype(jnp.bfloat16)
        mlp_part = jnp.einsum("rlf,fd->rld", act_low, fc2_full, preferred_element_type=jnp.float32)
        result = (hidden1 + fold_rows(mlp_part) + vectors[7]).astype(jnp.bfloat16)
        upstream = grad_out[number].astype(jnp.float32)
        up_low = grad_out[number]
        fc2_bias_grad = jnp.sum(upstream, axis=(0, 1))
        up_rows = spread_grads(up_low)
        fc2_grad = jnp.einsum("rlf,rld->fd", act_low, up_rows, preferred_element_type=jnp.float32)
        act_grad = jnp.einsum("rld,fd->rlf", up_rows, fc2_full, preferred_element_type=jnp.float32)
        _, gelu_pull = jax.vjp(exact_gelu, pre_act)
        pre_grad = gelu_pull(act_grad)[0].astype(jnp.bfloat16)
        fc1_bias_grad = jnp.sum(pre_grad.astype(jnp.float32), axis=(0, 1))
        fc1_grad = jnp.einsum("rld,rlf->df", rows_two, pre_grad, preferred_element_type=jnp.float32)
        normed2_grad = fold_grads(
            jnp.einsum("rlf,df->rld", pre_grad, fc1_full, preferred_element_type=jnp.float32)
        )
        _, norm2_pull = jax.vjp(layer_norm, hidden1, vectors[5], vectors[6])
        hidden1_grad, gain2_grad, shift2_grad = norm2_pull(normed2_grad)
        hidden1_grad = hidden1_grad + upstream
        attn_low = hidden1_grad.astype(jnp.bfloat16)
        out_bias_grad = jnp.sum(attn_low.astype(jnp.float32), axis=(0, 1))
        attn_rows = spread_grads(attn_low)
        out_grad = jnp.einsum(
            "rle,rld->ed", attended, attn_rows, preferred_element_type=jnp.float32
        )
        heads_grad = jnp.einsum(
            "rld,ed->rle", attn_rows, out_full, preferred_element_type=jnp.float32
        ).astype(jnp.bfloat16)
        heads_grad = heads_grad.reshape(row_count, length, heads_here, HEAD_DIM)
        query_grad, key_grad, value_grad = lax.map(
            backward_rows,
            (split_heads[0], split_heads[1], split_heads[2], clip_rows, log_totals, heads_grad),
        )
        qkv_grad = (
            jnp.stack([query_grad, key_grad, value_grad])
            .reshape(3, row_count, length, local_width)
            .astype(jnp.bfloat16)
        )
        qkv_grad_wide = qkv_grad.astype(jnp.float32)
        query_bias_grad = jnp.sum(qkv_grad_wide[0], axis=(0, 1))
        value_bias_grad = jnp.sum(qkv_grad_wide[2], axis=(0, 1))
        qkv_weight_grad = jnp.einsum(
            "rld,jrle->jde", rows_one, qkv_grad, preferred_element_type=jnp.float32
        )
        normed1_grad = fold_grads(
            jnp.einsum("jrle,jde->rld", qkv_grad, qkv_full, preferred_element_type=jnp.float32)
        )
        _, norm1_pull = jax.vjp(layer_norm, inputs, vectors[0], vectors[1])
        input_grad, gain1_grad, shift1_grad = norm1_pull(normed1_grad)
        input_grad = input_grad + hidden1_grad
        blank_width = jnp.zeros((width,), jnp.float32)
        query_placed = lax.dynamic_update_slice_in_dim(
            blank_width, query_bias_grad, column_start, 0
        )
        value_placed = lax.dynamic_update_slice_in_dim(
            blank_width, value_bias_grad, column_start, 0
        )
        vector_grad = jnp.stack(
            [
                gain1_grad,
                shift1_grad,
                query_placed,
                value_placed,
                out_bias_grad,
                gain2_grad,
                shift2_grad,
                fc2_bias_grad,
            ]
        )
        hidden_placed = lax.dynamic_update_slice_in_dim(
            jnp.zeros((hidden_total,), jnp.float32), fc1_bias_grad, hidden_start, 0
        )
        grads = (qkv_weight_grad, out_grad, fc1_grad, fc2_grad, vector_grad, hidden_placed)
        result, input_grad, grads = (result, input_grad, grads)
        results.append(result)
        input_grads.append(input_grad)
        vector_sums = lax.psum(
            (
                lax.psum_scatter(grads[4], "wide", scatter_dimension=1, tiled=True),
                lax.psum_scatter(grads[5], "wide", scatter_dimension=0, tiled=True),
            ),
            "narrow",
        )
        settled = (
            lax.psum_scatter(grads[0], "wide", scatter_dimension=1, tiled=True),
            lax.psum_scatter(grads[1], "wide", scatter_dimension=1, tiled=True),
            lax.psum_scatter(grads[2], "wide", scatter_dimension=0, tiled=True),
            lax.psum_scatter(grads[3], "wide", scatter_dimension=1, tiled=True),
            vector_sums[0],
            vector_sums[1],
        )
        shards = settled if shards is None else jax.tree.map(jnp.add, shards, settled)
    return (
        jnp.stack(results),
        jnp.stack(input_grads),
        shards[0],
        shards[1],
        shards[2],
        shards[3],
        shards[4],
        shards[5],
    )


def solution(mesh):
    in_specs = (
        P(None, "wide", "narrow", None),
        P(None, "wide", None),
        P(None, "wide", "narrow"),
        P("narrow", "wide"),
        P("wide", "narrow"),
        P("narrow", "wide"),
        P(None, "wide"),
        P("wide"),
        P(None, "wide", "narrow", None),
    )
    out_specs = (
        P(None, "wide", "narrow", None),
        P(None, "wide", "narrow", None),
        P(None, "wide", "narrow"),
        P("narrow", "wide"),
        P("wide", "narrow"),
        P("narrow", "wide"),
        P(None, "wide"),
        P("wide"),
    )

    def fits(tokens, w_qkv, w_fc1):
        wide, narrow = mesh.shape["wide"], mesh.shape["narrow"]
        width, hidden = w_fc1.shape
        return (
            wide == 8
            and narrow == 4
            and tokens.shape[:2] == (narrow, wide)
            and tokens.shape[2] % (128 * narrow) == 0
            and width == 12 * HEAD_DIM
            and hidden == narrow * width
        )

    def whole(tokens, clip_ids, w_qkv, w_out, w_fc1, w_fc2, norm_bias, fc1_bias, grad_out):
        chosen = fused_local if fits(tokens, w_qkv, w_fc1) else local
        placed = jax.shard_map(chosen, mesh=mesh, in_specs=in_specs, out_specs=out_specs, check_vma=False)
        return placed(tokens, clip_ids, w_qkv, w_out, w_fc1, w_fc2, norm_bias, fc1_bias, grad_out)

    return whole
```

```python
import functools

import jax
import jax.numpy as jnp
from jax import lax
from jax.experimental import pallas as pl
from jax.experimental.pallas import tpu as pltpu
from jax.sharding import PartitionSpec as P

HEAD_DIM = 64
LATE_OUTPUT = 1
MESH = pl.DeviceIdType.MESH
BF16 = jnp.bfloat16
F32 = jnp.float32
NN = (((1,), (0,)), ((), ()))
NT = (((1,), (1,)), ((), ()))
TN = (((0,), (0,)), ((), ()))
GATHER_Z_FIRST = (False, False, False)
GATHER_X_EARLY = ((0, 0), (1, 0), (1, 0))
SCATTER_Z_FIRST = (True, True, False)
SCATTER_X_EARLY = ((0, 0), (1, 0), (1, 0))
SCHEDULE = {
    1: (("z1",), ("xy1",), (0, 1, 1, 0), (0, 1, 2, 0), (0, 0, 1, 0), (0, 1, 3, 0), ("gout",),),
    2: ((0, 1, 2, 1), (1, 2, 1, 0),),
    3: ((0, 1, 1, 1), (0, 1, 3, 1), (1, 0, 1, 0), (1, 1, 1, 0), (1, 1, 2, 1), (0, 2, 1, 3), (0, 2, 1, 1), (0, 2, 1, 6), (0, 2, 1, 5), (0, 2, 1, 4), (0, 2, 1, 2), (0, 2, 1, 0), (0, 2, 1, 7), ("xy2",), (1, 1, 2, 0), (1, 1, 1, 1),),
    4: ((1, 1, 3, 1),),
    7: (("z2",),),
    10: ((1, 2, 1, 1),),
    14: ((2, 0, 1, 0),),
    20: ((1, 2, 1, 3),),
    25: ((1, 2, 1, 7),),
    26: ((1, 1, 3, 0),),
    28: ((2, 1, 1, 0),),
    33: ((2, 1, 2, 1),),
    34: ((1, 2, 1, 2),),
    35: ((2, 1, 1, 1), (1, 2, 1, 4), (1, 2, 1, 5), (1, 2, 1, 6), (2, 2, 1, 0),),
    36: ((2, 1, 2, 0),),
    41: ((2, 1, 3, 1),),
    42: ((2, 2, 1, 1),),
    46: ((2, 1, 3, 0),),
    47: ((2, 2, 1, 3), (2, 2, 1, 4),),
    48: ((2, 2, 1, 2), (2, 2, 1, 7), (2, 2, 1, 5), (2, 2, 1, 6),),
    63: (("rs", 2, "a", 1, 1), ("rs", 2, "a", 2, 1),),
    64: (("rs", 2, "a", 3, 1),),
    68: (("rs", 2, "a", 1, 0),),
    69: (("rs", 2, "a", 3, 0),),
    76: (("rs", 1, "a", 2),),
    79: (("rs", 1, "a", 1), ("rs", 2, "b"),),
    83: (("rs", 1, "a", 3),),
    90: (("rs", 2, "a", 2, 0),),
    92: (("rs", 1, "a", 0),),
    96: (("rs", 0, "a", 1), ("rs", 1, "b", 2),),
    101: (("rs", 1, "b", 3), ("rs", 0, "a", 3), ("rs", 1, "b", 1),),
    102: (("rs", 0, "a", 2),),
    105: (("rs", 0, "a", 0),),
    107: (("rs", 2, "c"),),
    110: (("rs", 0, "b", 2), ("rs", 0, "b", 3), ("rs", 0, "b", 1), ("rs", 1, "c"), ("rs", 0, "c"),),
}


def dot(a, b, dims):
    return lax.dot_general(a, b, dims, preferred_element_type=F32)


def aligned(value, step):
    return value if isinstance(value, int) else pl.multiple_of(value, step)


def slab_sum(values):
    rows, width = values.shape
    return jnp.sum(values.reshape(rows // 8, 8, width), axis=0)


def row_kernel(
    tok, clip, wqkv, wout, wfc1, wfc2, norm_bias, fc1_bias, gout,
    out_tok, out_gtok, out_g, out_vec,
    wts, psum, gsend, recv1, recv2, recv3,
    xrow, urow, normed1, normed2, attn_grad, outrow, gtrow,
    qs, ks, vs, heads, dheads, act, dgelu, dqkv,
    fa, fb, outacc, mask, stats, lse,
    smalls, vecs, qbias, vbias, hbias, vpart, vrecv, vsum, vnar,
    tok_s, tok_r, gout_s, gout_r, small_s, small_r,
    ag_s, ag_r, sib_r, gs_s, gs_r, rs_s, rs1_r, rs2_r, rs3_r,
    ot_s, ot_r, gt_s, gt_r, vp_s, vp_r, vn_s, vn_r, loc,
):
    depth, width = wfc1.shape[0], tok.shape[-1]
    wide = width // depth
    z_count = wide // 2
    w = lax.axis_index("wide")
    n = lax.axis_index("narrow")
    z, x, y, c = w // 2, w % 2, n // 2, n % 2
    length = xrow.shape[0]
    block = length // 4
    here = (w, n)
    sibling = (w, n ^ 1)
    wide_partners = [(w ^ v, n) for v in range(1, wide)]
    narrow_partners = [(w, n ^ v) for v in range(1, 4)]

    def send(src, dst, s_sem, r_sem, to):
        pltpu.make_async_remote_copy(
            src_ref=src, dst_ref=dst, send_sem=s_sem, recv_sem=r_sem,
            device_id=to, device_id_type=MESH,
        ).start()

    def got(ref, r_sem):
        pltpu.make_async_remote_copy(
            src_ref=ref, dst_ref=ref, send_sem=loc.at[0], recv_sem=r_sem,
            device_id=sibling, device_id_type=MESH,
        ).wait_recv()

    def sent(ref, s_sem):
        pltpu.make_async_remote_copy(
            src_ref=ref, dst_ref=ref, send_sem=s_sem, recv_sem=loc.at[0],
            device_id=sibling, device_id_type=MESH,
        ).wait_send()

    def chosen(table, k):
        first, second = table[k]
        return first if first == second else jnp.where(c == 0, first, second)

    gather_x = [chosen(GATHER_X_EARLY, k) for k in range(3)]
    scatter_x = [chosen(SCATTER_X_EARLY, k) for k in range(3)]
    inner = (z == 1) | (z == 2)
    z_offset = [0, 1, jnp.where(inner, 3, 2), jnp.where(inner, 2, 3)]

    def origin(x_early, rel):
        rz, ra, rb = rel
        ox = x ^ (x_early * ra + (1 - x_early) * rb)
        oy = y ^ (x_early * rb + (1 - x_early) * ra)
        return z ^ rz, ox, oy

    def wts_at(k, rel):
        oz, ox, oy = origin(gather_x[k], rel)
        start = (k * 4 + oy * 2 + c) * width + (oz * 2 + ox) * depth
        return wts.at[pl.ds(aligned(start, 32), depth), :]

    def psum_at(k, rel):
        oz, ox, oy = origin(scatter_x[k], rel)
        start = (k * 2 + oy) * width + (oz * 2 + ox) * depth
        return psum.at[pl.ds(aligned(start, 32), depth), :]

    def partner(x_early, dim, v):
        if dim == 0:
            return (w ^ (2 * v), n)
        x_hop = x_early if dim == 1 else 1 - x_early
        return (w ^ x_hop, n ^ (2 * (1 - x_hop)))

    def pass_on(k, rel, dim, v):
        there = list(rel)
        there[dim] = rel[dim] ^ v
        send(
            wts_at(k, rel), wts_at(k, rel), ag_s.at[k],
            ag_r.at[k, there[0] * 4 + there[1] * 2 + there[2]], partner(gather_x[k], dim, v),
        )

    def along_z(k, i, rel):
        if i == 0:
            pass_on(k, rel, 0, 1)
        pl.when(inner)(lambda: pass_on(k, rel, 0, 3 if i < 2 else 1))

    def hand_on(k, phase, i, rel):
        order = (0, 1, 2) if GATHER_Z_FIRST[k] else (1, 0, 2)
        if phase >= 0 and order[phase] == 0:
            along_z(k, i, rel)
        for dim in order[phase + 1 :]:
            if dim == 0:
                along_z(k, i, rel)
            else:
                pass_on(k, rel, dim, 1)
        send(wts_at(k, rel), wts_at(k, rel), ag_s.at[k], sib_r.at[k], sibling)

    def own_along_z(k):
        along_z(k, 0, (0, 0, 0))

    def own_across(k):
        rel = (0, 0, 0)
        pass_on(k, rel, 1, 1)
        pass_on(k, rel, 2, 1)
        send(wts_at(k, rel), wts_at(k, rel), ag_s.at[k], sib_r.at[k], sibling)

    steps = {}

    def gather_steps(k):
        order = (0, 1, 2) if GATHER_Z_FIRST[k] else (1, 0, 2)
        held = [(0, 0, 0)]

        def step(phase, named):
            rel = (z_offset[named[0]], named[1], named[2])
            got(wts_at(k, rel), ag_r.at[k, rel[0] * 4 + rel[1] * 2 + rel[2]])
            hand_on(k, phase, named[0], rel)

        for phase, dim in enumerate(order):
            fresh = []
            for i in range(1, z_count if dim == 0 else 2):
                for j, named in enumerate(held):
                    there = list(named)
                    there[dim] = i
                    fresh.append(tuple(there))
                    steps[(k, phase, i, j)] = functools.partial(step, phase, tuple(there))
            held = held + fresh

    def add_up(k, rel, others):
        here_ref = psum_at(k, rel)
        total = here_ref[...].astype(F32)
        for other in others:
            total = total + other[...].astype(F32)
        return here_ref, total

    nearest_last = list(range(1, z_count)) + [0]

    def scatter_send(k, rz, ra):
        send(
            psum_at(k, (rz, ra, 1)), recv1.at[k, rz * 2 + ra], rs_s.at[k],
            rs1_r.at[k, rz * 2 + ra], partner(scatter_x[k], 2, 1),
        )

    def scatter_first(k):
        for rz in nearest_last:
            for ra in (1, 0):
                scatter_send(k, rz, ra)

    def scatter_first_part(k, part):
        if part == 0:
            for rz in nearest_last:
                scatter_send(k, rz, 1)

        @pl.when(scatter_x[k] == 1 - part)
        def _():
            for rz in nearest_last:
                scatter_send(k, rz, 0)

    def scatter_steps(k):
        def fresh(buffer, sems, i):
            ref = buffer.at[k, i]
            got(ref, sems.at[k, i])
            return ref

        fresh1 = functools.partial(fresh, recv1, rs1_r)
        fresh2 = functools.partial(fresh, recv2, rs2_r)
        fresh3 = functools.partial(fresh, recv3, rs3_r)
        x_early = scatter_x[k]

        def sum_on(rel, others, there, sem, to):
            ref, total = add_up(k, rel, others)
            ref[...] = total.astype(BF16)
            send(ref, there, rs_s.at[k], sem, to)

        def finish_sum(others):
            _, total = add_up(k, (0, 0, 0), others)
            out_g[k] = total

        if SCATTER_Z_FIRST[k]:

            def early_hop(rz):
                sum_on((rz, 1, 0), [fresh1(rz * 2 + 1)], recv2.at[k, rz], rs2_r.at[k, rz], partner(x_early, 1, 1))

            def z_hop(rz):
                others = [fresh1(rz * 2), fresh2(rz)]
                sum_on((rz, 0, 0), others, recv3.at[k, rz - 1], rs3_r.at[k, rz - 1], partner(x_early, 0, rz))

            for rz in range(z_count):
                steps[("rs", k, "a", rz)] = functools.partial(early_hop, rz)
                if rz > 0:
                    steps[("rs", k, "b", rz)] = functools.partial(z_hop, rz)
            steps[("rs", k, "c")] = lambda: finish_sum(
                [fresh1(0), fresh2(0)] + [fresh3(i) for i in range(z_count - 1)]
            )
        else:

            def z_hop(rz, ra):
                i = (rz - 1) * 2 + ra
                sum_on((rz, ra, 0), [fresh1(rz * 2 + ra)], recv2.at[k, i], rs2_r.at[k, i], partner(x_early, 0, rz))

            def early_hop():
                others = [fresh1(1)] + [fresh2(i * 2 + 1) for i in range(z_count - 1)]
                sum_on((0, 1, 0), others, recv3.at[k, 0], rs3_r.at[k, 0], partner(x_early, 1, 1))

            for rz in range(1, z_count):
                for ra in range(2):
                    steps[("rs", k, "a", rz, ra)] = functools.partial(z_hop, rz, ra)
            steps[("rs", k, "b")] = early_hop
            steps[("rs", k, "c")] = lambda: finish_sum(
                [fresh1(0)] + [fresh2(i * 2) for i in range(z_count - 1)] + [fresh3(0)]
            )

    point = [0]

    def service(before_last=None):
        point[0] += 1
        names = SCHEDULE.get(point[0], ())
        for i, name in enumerate(names):
            if before_last is not None and i == len(names) - 1:
                before_last()
            steps.pop(name)()

    def weights_here(k):
        service()
        got(wts.at[pl.ds(0, 2 * width), :], sib_r.at[k])

    def weight(k, j, columns=slice(None)):
        return wts[pl.ds(aligned((k * 4 + j) * width, 128), width), columns]

    def own_place(k):
        return pl.ds(aligned((k * 4 + n) * width + w * depth, 32), depth)

    wts[own_place(0), 0:192] = wqkv[0]
    wts[own_place(0), 192:384] = wqkv[2]
    wts[own_place(0), 384:576] = wqkv[1]
    wts[own_place(0), 576:768] = jnp.transpose(wout[...].astype(F32)).astype(BF16)
    wts[own_place(1), :] = wfc1[...]
    wts[own_place(2), :] = wfc2[...]
    smalls[w] = jnp.zeros(smalls.shape[1:], F32)
    smalls[w, 0:8, 0:depth] = norm_bias[...].astype(F32)
    hidden_bias = fc1_bias[...].astype(F32)
    for r in range(4):
        smalls[w, 8 + r : 9 + r, 0:depth] = hidden_bias[:, r * depth : (r + 1) * depth]

    barrier = pltpu.get_barrier_semaphore()
    for to in wide_partners + narrow_partners:
        pl.semaphore_signal(barrier, inc=1, device_id=to, device_id_type=MESH)
    pl.semaphore_wait(barrier, len(wide_partners) + len(narrow_partners))

    rows_here = pl.ds(aligned(n * block, 128), block)

    def rows_of(to):
        return pl.ds(aligned(to[1] * block, 128), block)

    for i, to in enumerate(wide_partners):
        send(smalls.at[w], smalls.at[w], small_s.at[i], small_r.at[i], to)
    for i, to in enumerate(narrow_partners):
        send(tok.at[to[1]], xrow.at[rows_here, :], tok_s.at[i], tok_r.at[i], to)
    own_along_z(0)
    own_across(0)
    own_tok = pltpu.make_async_copy(tok.at[n], xrow.at[rows_here, :], loc.at[1])
    own_tok.start()
    own_gout = pltpu.make_async_copy(gout.at[n], urow.at[rows_here, :], loc.at[2])
    own_gout.start()

    def start_gout():
        for i, to in enumerate(narrow_partners):
            send(gout.at[to[1]], urow.at[rows_here, :], gout_s.at[i], gout_r.at[i], to)

    for k in range(3):
        gather_steps(k)
    steps[("z1",)] = functools.partial(own_along_z, 1)
    steps[("xy1",)] = functools.partial(own_across, 1)
    steps[("z2",)] = functools.partial(own_along_z, 2)
    steps[("xy2",)] = functools.partial(own_across, 2)
    steps[("gout",)] = start_gout

    ids = clip[n]
    place = lax.broadcasted_iota(jnp.int32, (1, length), 1)
    ids = jnp.where(ids >= 0, ids, -1 - place).astype(F32)
    ids_down = jnp.transpose(jnp.broadcast_to(ids, (128, length)))[:, 0:1]
    mask[...] = jnp.where(ids_down == ids, 0.0, -1e30)

    for i, to in enumerate(wide_partners):
        got(smalls.at[to[0]], small_r.at[i])
    qbias[...] = jnp.zeros_like(qbias)
    vbias[...] = jnp.zeros_like(vbias)
    for i in range(wide):
        part = smalls[i]
        vecs[:, i * depth : (i + 1) * depth] = part[0:8, 0:depth]
        j, half_at = i // 2, (i % 2) * depth
        qbias[j, :, half_at : half_at + depth] = part[2:3, 0:depth]
        vbias[j, :, 64 + half_at : 64 + half_at + depth] = part[3:4, 0:depth]
        for r in range(4):
            at = (i % 2) * 4 * depth + r * depth
            hbias[j, :, at : at + depth] = part[8 + r : 9 + r, 0:depth]

    service()
    own_tok.wait()
    for i, to in enumerate(narrow_partners):
        got(xrow.at[rows_of(to), :], tok_r.at[i])

    def norm_forward(source, gain, shift, column, target):
        def body(i, _):
            rows = pl.ds(aligned(i * block, 128), block)
            v = source[rows, :].astype(F32)
            average = jnp.mean(v, axis=-1, keepdims=True)
            centred = v - average
            rr = lax.rsqrt(jnp.mean(centred * centred, axis=-1, keepdims=True) + 1e-6)
            stats[rows, column : column + 1] = average
            stats[rows, column + 1 : column + 2] = rr
            target[rows, :] = (centred * rr * vecs[gain : gain + 1] + vecs[shift : shift + 1]).astype(BF16)
            return 0

        lax.fori_loop(0, 4, body, 0)

    norm_forward(xrow, 0, 1, 0, normed1)
    service()

    weights_here(0)
    lane = lax.broadcasted_iota(jnp.int32, (1, 256), 1)
    low = lane[:, 0:128] < 64
    for j in range(4):
        projected = dot(normed1[...], weight(0, j, slice(0, 640)), NN)
        slot = slice(256 * j, 256 * j + 256)
        query = (projected[:, 0:256] + qbias[j]).astype(BF16).astype(F32) * 0.125
        qs[:, slot] = jnp.where(lane < 192, query, 0.0).astype(BF16)
        value = projected[:, 128:384] + vbias[j]
        vs[:, slot] = jnp.where(lane >= 64, value, 0.0).astype(BF16)
        ks[:, slot] = jnp.where(lane < 192, projected[:, 384:640], 0.0).astype(BF16)
        service()

    def lanes(j, second):
        return pl.ds(aligned(256 * j + 128 * second, 128), 128)

    def only(head, values):
        return jnp.where(low if head == 0 else ~low, values, jnp.zeros_like(values))

    def query_of(j, head):
        return only(head, qs[:, lanes(j, 0)]) if head < 2 else qs[:, lanes(j, 1)]

    def key_of(j, head):
        return ks[:, lanes(j, 0)] if head < 2 else ks[:, lanes(j, 1)]

    for j in range(4):
        mixed = []
        for head in range(3):
            scores = dot(query_of(j, head), key_of(j, head), NT) + mask[...]
            row_max = jnp.max(scores, axis=1, keepdims=True)
            weights = jnp.exp(scores - row_max)
            row_sum = jnp.sum(weights, axis=1, keepdims=True)
            probs = (weights * (1.0 / row_sum)).astype(BF16)
            lse[j, :, head : head + 1] = row_max + jnp.log(row_sum)
            service()
            value = vs[:, lanes(j, 0)] if head == 0 else vs[:, lanes(j, 1)]
            mixed.append(dot(probs, value, NN))
            service()
        heads[:, lanes(j, 0)] = mixed[0].astype(BF16)
        heads[:, lanes(j, 1)] = jnp.where(low, mixed[1], mixed[2]).astype(BF16)

    fb[...] = xrow[...].astype(F32) + vecs[4:5]
    for j in range(4):
        fb[...] += dot(heads[:, 256 * j : 256 * j + 256], weight(0, j, slice(512, 768)), NT)
        service()
    fa[...] = fb[...]
    norm_forward(fa, 5, 6, 2, normed2)

    weights_here(1)
    for j in range(4):
        pre = dot(normed2[...], weight(1, j), NN) + hbias[j]
        service()
        cumulative = 0.5 * (1.0 + lax.erf(pre * (0.5**0.5)))
        density = jnp.exp(pre * pre * -0.5) * (0.5 / jnp.pi) ** 0.5
        act[j] = (pre * cumulative).astype(BF16)
        dgelu[j] = (cumulative + pre * density).astype(BF16)
        service()

    def give(k, j, slot, product):
        if k < 2:
            sent(gsend.at[slot], gs_s.at[slot])
        gsend[slot] = product.astype(BF16)
        place = pl.ds(aligned((k * 2 + j) * width, 128), width)
        send(gsend.at[slot], psum.at[place, :], gs_s.at[slot], gs_r.at[k * 2 + j], sibling)

    def keep(k, j, product):
        place = pl.ds(aligned((k * 2 + j) * width, 128), width)
        service()
        got(psum.at[place, :], gs_r.at[k * 2 + j])
        psum[place, :] = (product + psum[place, :].astype(F32)).astype(BF16)

    service()
    own_gout.wait()
    for i, to in enumerate(narrow_partners):
        got(urow.at[rows_of(to), :], gout_r.at[i])
    for j in range(2):
        give(2, j, j, dot(urow[...], act[2 * j + 1 - c], TN))
        service()
    for j in range(2):
        keep(2, j, dot(urow[...], act[2 * j + c], TN))
        service()
    scatter_first(2)
    scatter_steps(2)
    weights_here(2)

    def output():
        for j in range(4):
            outacc[...] = (fa if j == 0 else outacc)[...] + dot(act[j], weight(2, j), NT)
            service()
        outrow[...] = (outacc[...] + vecs[7:8]).astype(BF16)
        for i, to in enumerate(narrow_partners):
            send(outrow.at[rows_of(to), :], out_tok.at[n], ot_s.at[i], ot_r.at[i], to)
        copy = pltpu.make_async_copy(outrow.at[rows_here, :], out_tok.at[n], loc.at[3])
        copy.start()
        return copy

    if LATE_OUTPUT == 0:
        own_out = output()

    def put(row, i, values):
        vpart[i, row : row + 1, 0:depth] = values

    def put_row(row, values):
        for i in range(wide):
            put(row, i, values[:, i * depth : (i + 1) * depth])

    def column_sum(values):
        return jnp.sum(values.astype(F32), axis=0, keepdims=True)

    vpart[...] = jnp.zeros_like(vpart)
    put_row(7, column_sum(urow[...]))
    for j in range(4):
        grad = dot(urow[...], weight(2, j), NN) * dgelu[j].astype(F32)
        dgelu[j] = grad.astype(BF16)
        total = column_sum(dgelu[j])
        for i in range(2):
            for r in range(4):
                at = (i * 4 + r) * depth
                put(8 + r, 2 * j + i, total[:, at : at + depth])
        service()
    for j in range(2):
        give(1, j, j, dot(normed2[...], dgelu[2 * j + 1 - c], TN))
        service()
    for j in range(4):
        product = dot(dgelu[j], weight(1, j), NT)
        fb[...] = product if j == 0 else fb[...] + product
        service()
    for j in range(2):
        keep(1, j, dot(normed2[...], dgelu[2 * j + c], TN))
        service()
    scatter_first(1)
    scatter_steps(1)

    def norm_backward(source, grad, gain, column, extra, target, rounded):
        def body(i, sums):
            rows = pl.ds(aligned(i * block, 128), block)
            rr = stats[rows, column + 1 : column + 2]
            xhat = (source[rows, :].astype(F32) - stats[rows, column : column + 1]) * rr
            n_grad = grad[rows, :]
            u = n_grad * vecs[gain : gain + 1]
            inner = u - jnp.mean(u, axis=-1, keepdims=True) - xhat * jnp.mean(u * xhat, axis=-1, keepdims=True)
            result = rr * inner + extra[rows, :].astype(F32)
            if target is not None:
                target[rows, :] = result
            low_result = result.astype(BF16)
            rounded[rows, :] = low_result
            return (
                sums[0] + slab_sum(n_grad * xhat),
                sums[1] + slab_sum(n_grad),
                sums[2] + slab_sum(low_result.astype(F32)),
            )

        zero = jnp.zeros((8, width), F32)
        sums = lax.fori_loop(0, 4, body, (zero, zero, zero))
        return [jnp.sum(s, axis=0, keepdims=True) for s in sums]

    gain2, shift2, attn_total = norm_backward(fa, fb, 5, 2, urow, fb, attn_grad)
    if LATE_OUTPUT == 1:
        own_out = output()
    put_row(5, gain2)
    put_row(6, shift2)
    put_row(4, attn_total)

    for j in range(4):
        back = dot(attn_grad[...], weight(0, j, slice(512, 768)), NN)
        dheads[:, 256 * j : 256 * j + 256] = jnp.where(lane >= 64, back, 0.0).astype(BF16)
        service()

    def attention_backward(j):
        def value_of(head):
            return vs[:, lanes(j, 0)] if head == 0 else vs[:, lanes(j, 1)]

        def upstream_of(head):
            if head == 0:
                return dheads[:, lanes(j, 0)]
            return only(head - 1, dheads[:, lanes(j, 1)])

        dq, dk, dv = [], [], []
        for head in range(3):
            query, key, up = query_of(j, head), key_of(j, head), upstream_of(head)
            second = int(head > 0)
            delta = jnp.sum(
                up.astype(F32) * heads[:, lanes(j, second)].astype(F32), axis=1, keepdims=True
            )
            scores = dot(query, key, NT) + mask[...]
            soft = jnp.exp(scores - lse[j, :, head : head + 1])
            prob_grad = dot(up, value_of(head), NT)
            score_grad = (soft * (prob_grad - delta)).astype(BF16)
            service()
            dq.append(dot(score_grad, key, NN))
            dk.append(dot(score_grad, query, TN))
            dv.append(dot(soft.astype(BF16), up, TN))
            service()
        dqkv[j, :, 0:128] = (jnp.where(low, dq[0], dq[1]) * 0.125).astype(BF16)
        dqkv[j, :, 128:256] = (dq[2] * 0.125 + dv[0]).astype(BF16)
        dqkv[j, :, 256:384] = (dv[1] + dv[2]).astype(BF16)
        dqkv[j, :, 384:512] = (dk[0] + dk[1]).astype(BF16)
        dqkv[j, :, 512:640] = dk[2].astype(BF16)
        total = column_sum(dqkv[j, :, 0:384])
        for i in range(2):
            put(2, 2 * j + i, total[:, i * depth : (i + 1) * depth])
            put(3, 2 * j + i, total[:, (2 + i) * depth : (3 + i) * depth])

    def projection_grad(j):
        first = dot(normed1[...], dqkv[j], TN)
        second = dot(attn_grad[...], heads[:, pl.ds(aligned(256 * j, 128), 256)], TN)
        return jnp.concatenate(
            [first[:, 0:512], first[:, 512:640] + second[:, 0:128], second[:, 128:256]], axis=1
        )

    for i, half in enumerate((1 - y, y)):
        for own in (False, True):
            j = 2 * half + (c if own else 1 - c)
            attention_backward(j)
            if own:
                keep(0, half, projection_grad(j))
            else:
                give(0, half, i, projection_grad(j))
            service()
        scatter_first_part(0, i)
        if i == 0:
            scatter_steps(0)
    for j in range(4):
        product = dot(dqkv[j], weight(0, j, slice(0, 640)), NT)
        fa[...] = product if j == 0 else fa[...] + product
        service()

    gain1, shift1, _ = norm_backward(xrow, fa, 0, 0, fb, None, gtrow)
    for i, to in enumerate(narrow_partners):
        rows = pl.ds(aligned(to[1] * block, 128), block)
        send(gtrow.at[rows, :], out_gtok.at[n], gt_s.at[i], gt_r.at[i], to)
    own_gtok = pltpu.make_async_copy(gtrow.at[rows_here, :], out_gtok.at[n], loc.at[4])
    own_gtok.start()
    service()
    put_row(0, gain1)
    put_row(1, shift1)
    for i, to in enumerate(wide_partners):
        send(vpart.at[to[0]], vrecv.at[i], vp_s.at[i], vp_r.at[i], to)

    def share_vectors():
        total = vpart[w]
        for i in range(len(wide_partners)):
            got(vrecv.at[i], vp_r.at[i])
            total = total + vrecv[i]
        vsum[...] = total
        for i, to in enumerate(narrow_partners):
            send(vsum, vnar.at[i], vn_s.at[i], vn_r.at[i], to)

    service(share_vectors)
    assert not steps
    total = vsum[...]
    for i in range(3):
        got(vnar.at[i], vn_r.at[i])
        total = total + vnar[i]
    out_vec[...] = total

    for i, to in enumerate(narrow_partners):
        got(out_tok.at[to[1]], ot_r.at[i])
        got(out_gtok.at[to[1]], gt_r.at[i])
        sent(tok.at[0], tok_s.at[i])
        sent(gout.at[0], gout_s.at[i])
        sent(outrow.at[pl.ds(0, block), :], ot_s.at[i])
        sent(gtrow.at[pl.ds(0, block), :], gt_s.at[i])
        sent(vsum, vn_s.at[i])
    for i in range(len(wide_partners)):
        sent(smalls.at[0], small_s.at[i])
        sent(vpart.at[0], vp_s.at[i])
    for k in range(3):
        z_sends = (1, 2 + 3) if GATHER_Z_FIRST[k] else (2, 4 + 6)
        across = (1 + 3) + (1 + 3 + 4) if GATHER_Z_FIRST[k] else 1 + (1 + 1 + 6)
        for place, count in zip((~inner, inner), z_sends):
            rows = (count + across + 4 * z_count) * depth
            pl.when(place)(functools.partial(sent, wts.at[pl.ds(0, rows), :], ag_s.at[k]))
        sends = 4 * z_count - 1
        sent(psum.at[pl.ds(0, sends * depth), :], rs_s.at[k])
    for slot in range(2):
        sent(gsend.at[slot], gs_s.at[slot])
    own_out.wait()
    own_gtok.wait()


def settle_kernel(tok, gtok, g, vec, out_tok, out_gtok, out_qkv, out_proj, out_fc1, out_fc2, out_nb, out_fb):
    out_tok[...] = tok[...]
    out_gtok[...] = gtok[...].astype(F32)

    @pl.when(pl.program_id(0) == 0)
    def _():
        depth, part = out_qkv.shape[1:]
        out_qkv[0] = g[0, :, 0:part]
        out_qkv[1] = g[0, :, 2 * part : 3 * part]
        out_qkv[2] = g[0, :, part : 2 * part]
        out_proj[...] = jnp.transpose(g[0, :, 3 * part :])
        out_fc1[...] = g[1]
        out_fc2[...] = g[2]
        out_nb[...] = vec[0:8, 0:depth]
        for r in range(4):
            out_fb[:, r * depth : (r + 1) * depth] = vec[8 + r : 9 + r, 0:depth]


def fused_local(tokens, clip_ids, w_qkv, w_out, w_fc1, w_fc2, norm_bias, fc1_bias, grad_out):
    micro, _, block, width = tokens.shape
    depth, hidden = w_fc1.shape
    wide = width // depth
    z_count = wide // 2
    length = micro * block

    def anywhere():
        return pl.BlockSpec(memory_space=pl.ANY)

    def vmem():
        return pl.BlockSpec(memory_space=pltpu.VMEM)

    def flat(*shape):
        return pltpu.VMEM(shape, BF16)

    def wide_type(*shape):
        return pltpu.VMEM(shape, F32)

    def sems(*shape):
        return pltpu.SemaphoreType.DMA(shape)

    out_tok, out_gtok, out_g, out_vec = pl.pallas_call(
        row_kernel,
        out_shape=(
            jax.ShapeDtypeStruct((micro, block, width), BF16),
            jax.ShapeDtypeStruct((micro, block, width), BF16),
            jax.ShapeDtypeStruct((3, depth, width), F32),
            jax.ShapeDtypeStruct((16, 128), F32),
        ),
        in_specs=[anywhere()] + [vmem()] * 7 + [anywhere()],
        out_specs=(anywhere(), anywhere(), vmem(), vmem()),
        scratch_shapes=[
            flat(12 * width, hidden),
            flat(6 * width, hidden),
            flat(2, width, hidden),
            flat(3, 2 * z_count, depth, hidden),
            flat(3, 2 * (z_count - 1), depth, hidden),
            flat(3, z_count - 1, depth, hidden),
            *[flat(length, width)] * 7,
            *[flat(length, 1024)] * 5,
            flat(4, length, hidden),
            flat(4, length, hidden),
            flat(4, length, 640),
            wide_type(length, width),
            wide_type(length, width),
            wide_type(length, width),
            wide_type(length, length),
            wide_type(length, 128),
            wide_type(4, length, 128),
            wide_type(wide, 16, 128),
            wide_type(8, width),
            wide_type(4, 1, 256),
            wide_type(4, 1, 256),
            wide_type(4, 1, hidden),
            wide_type(wide, 16, 128),
            wide_type(wide - 1, 16, 128),
            wide_type(16, 128),
            wide_type(3, 16, 128),
            sems(3), sems(3), sems(3), sems(3), sems(wide - 1), sems(wide - 1),
            sems(3), sems(3, 4 * z_count), sems(3), sems(2), sems(6),
            sems(3), sems(3, 2 * z_count), sems(3, 2 * (z_count - 1)), sems(3, z_count - 1),
            sems(3), sems(3), sems(3), sems(3), sems(wide - 1), sems(wide - 1), sems(3), sems(3),
            sems(5),
        ],
        compiler_params=pltpu.CompilerParams(
            collective_id=0, has_side_effects=True, vmem_limit_bytes=62 * 2**20
        ),
    )(
        tokens.reshape(micro, block, width), clip_ids, w_qkv, w_out, w_fc1, w_fc2.T, norm_bias,
        fc1_bias.reshape(1, 4 * depth), grad_out.reshape(micro, block, width),
    )
    part = width // 4
    shapes = [(3, depth, part), (part, depth), (depth, width), (depth, width), (8, depth), (1, 4 * depth)]
    rows_spec = pl.BlockSpec((1, block, width), lambda i: (i, 0, 0))

    def fixed(shape):
        return pl.BlockSpec(shape, lambda i: (0,) * len(shape))

    out, gtok, grad_qkv, grad_proj, grad_fc1, grad_fc2, grad_nb, grad_fb = pl.pallas_call(
        settle_kernel,
        grid=(micro,),
        out_shape=[
            jax.ShapeDtypeStruct((micro, block, width), BF16),
            jax.ShapeDtypeStruct((micro, block, width), F32),
            *[jax.ShapeDtypeStruct(shape, F32) for shape in shapes],
        ],
        in_specs=[rows_spec, rows_spec, fixed((3, depth, width)), fixed((16, 128))],
        out_specs=[rows_spec, rows_spec, *[fixed(shape) for shape in shapes]],
    )(out_tok, out_gtok, out_g, out_vec)
    return (
        out[:, None],
        gtok[:, None],
        grad_qkv,
        grad_proj,
        grad_fc1,
        grad_fc2.T,
        grad_nb,
        grad_fb.reshape(4 * depth),
    )


def layer_norm(values, scaling, shifting):
    average = jnp.mean(values, axis=-1, keepdims=True)
    centred = values - average
    variance = jnp.mean(centred * centred, axis=-1, keepdims=True)
    return centred * lax.rsqrt(variance + 1e-06) * scaling + shifting


def exact_gelu(values):
    return jax.nn.gelu(values, approximate=False)


def block_scores(query_block, keys, clip_block, clip_row, block_start, score_scale):
    block_rows = query_block.shape[0]
    length = keys.shape[0]
    scores = (
        jnp.einsum("qhd,khd->hqk", query_block, keys, preferred_element_type=jnp.float32)
        * score_scale
    )
    key_place = lax.broadcasted_iota(jnp.int32, (block_rows, length), 1)
    query_place = block_start + lax.broadcasted_iota(jnp.int32, (block_rows, length), 0)
    allowed = (clip_block[:, None] == clip_row[None, :]) & (clip_row[None, :] >= 0) | (
        query_place == key_place
    )
    return jnp.where(allowed[None], scores, -1e30)


def row_forward(query, keys, values, clip_row, score_scale):
    length = query.shape[0]
    block_rows = min(512, length)

    def one_block(block_start):
        scores = block_scores(query, keys, clip_row, clip_row, block_start, score_scale)
        row_max = jnp.max(scores, axis=-1, keepdims=True)
        weights = jnp.exp(scores - row_max)
        row_sum = jnp.sum(weights, axis=-1, keepdims=True)
        probabilities = (weights / row_sum).astype(jnp.bfloat16)
        mixed = jnp.einsum(
            "hqk,khd->qhd", probabilities, values, preferred_element_type=jnp.float32
        )
        return (mixed, (row_max + jnp.log(row_sum))[..., 0])

    starts = lax.broadcasted_iota(jnp.int32, (length // block_rows,), 0) * block_rows
    mixed, log_totals = lax.map(one_block, starts)
    return (mixed.reshape(length, -1), log_totals)


def row_backward(query, keys, values, clip_row, log_totals, grad_heads, score_scale):
    length = query.shape[0]
    block_rows = min(512, length)

    def one_block(running, element):
        key_grad, value_grad = running
        block_start, block_totals = element
        scores = block_scores(query, keys, clip_row, clip_row, block_start, score_scale)
        probabilities = jnp.exp(scores - block_totals[..., None])
        prob_grad = jnp.einsum(
            "qhd,khd->hqk", grad_heads, values, preferred_element_type=jnp.float32
        )
        value_grad = value_grad + jnp.einsum(
            "hqk,qhd->khd",
            probabilities.astype(jnp.bfloat16),
            grad_heads,
            preferred_element_type=jnp.float32,
        )
        score_grad = probabilities * (
            prob_grad - jnp.sum(probabilities * prob_grad, axis=-1, keepdims=True)
        )
        score_grad = score_grad.astype(jnp.bfloat16)
        query_grad = (
            jnp.einsum("hqk,khd->qhd", score_grad, keys, preferred_element_type=jnp.float32)
            * score_scale
        )
        key_grad = (
            key_grad
            + jnp.einsum("hqk,qhd->khd", score_grad, query, preferred_element_type=jnp.float32)
            * score_scale
        )
        return ((key_grad, value_grad), query_grad)

    starts = lax.broadcasted_iota(jnp.int32, (length // block_rows,), 0) * block_rows
    zero_grads = jnp.zeros(keys.shape, jnp.float32)
    (key_grad, value_grad), query_grads = lax.scan(
        one_block, (zero_grads, zero_grads), (starts, log_totals)
    )
    return (query_grads.reshape(query.shape), key_grad, value_grad)


def local(tokens, clip_ids, w_qkv, w_out, w_fc1, w_fc2, norm_bias, fc1_bias, grad_out):
    micro_count = tokens.shape[0]
    row_count = tokens.shape[1]
    width = tokens.shape[3]
    local_width = w_qkv.shape[2]
    local_hidden = w_fc1.shape[1]
    heads_here = local_width // HEAD_DIM
    score_scale = HEAD_DIM ** (-0.5)
    narrow_index = lax.axis_index("narrow")

    def spread_rows(values):
        return lax.all_gather(values, "narrow", axis=1, tiled=True)

    def fold_rows(values):
        return lax.psum_scatter(values, "narrow", scatter_dimension=1, tiled=True)

    def spread_grads(values):
        return lax.all_gather(values, "narrow", axis=1, tiled=True)

    def fold_grads(values):
        return lax.psum_scatter(values, "narrow", scatter_dimension=1, tiled=True)

    def forward_rows(element):
        return row_forward(element[0], element[1], element[2], element[3], score_scale)

    def backward_rows(element):
        return row_backward(
            element[0], element[1], element[2], element[3], element[4], element[5], score_scale
        )

    results = []
    input_grads = []
    shards = None
    for number in range(micro_count):
        qkv_full = lax.all_gather(w_qkv, "wide", axis=1, tiled=True)
        out_full = lax.all_gather(w_out, "wide", axis=1, tiled=True)
        fc1_full = lax.all_gather(w_fc1, "wide", axis=0, tiled=True)
        fc2_full = lax.all_gather(w_fc2, "wide", axis=1, tiled=True)
        vector_full = lax.all_gather(norm_bias, "wide", axis=1, tiled=True)
        hidden_bias_full = lax.all_gather(fc1_bias, "wide", axis=0, tiled=True)
        vectors = vector_full.astype(jnp.float32)
        hidden_total = hidden_bias_full.shape[0]
        column_start = narrow_index * local_width
        hidden_start = narrow_index * local_hidden
        fc_bias = lax.dynamic_slice_in_dim(hidden_bias_full, hidden_start, local_hidden, 0).astype(
            jnp.float32
        )
        query_bias = lax.dynamic_slice_in_dim(vectors[2], column_start, local_width, 0)
        value_bias = lax.dynamic_slice_in_dim(vectors[3], column_start, local_width, 0)
        inputs = tokens[number].astype(jnp.float32)
        clip_rows = clip_ids[number]
        normed1 = layer_norm(inputs, vectors[0], vectors[1]).astype(jnp.bfloat16)
        rows_one = spread_rows(normed1)
        length = rows_one.shape[1]
        projected = jnp.einsum(
            "rld,jde->jrle", rows_one, qkv_full, preferred_element_type=jnp.float32
        )
        bias_three = jnp.stack([query_bias, jnp.zeros_like(query_bias), value_bias])
        qkv_low = (projected + bias_three[:, None, None, :]).astype(jnp.bfloat16)
        split_heads = qkv_low.reshape(3, row_count, length, heads_here, HEAD_DIM)
        attended, log_totals = lax.map(
            forward_rows, (split_heads[0], split_heads[1], split_heads[2], clip_rows)
        )
        attended = attended.astype(jnp.bfloat16)
        attention_part = jnp.einsum(
            "rle,ed->rld", attended, out_full, preferred_element_type=jnp.float32
        )
        hidden1 = inputs + fold_rows(attention_part) + vectors[4]
        normed2 = layer_norm(hidden1, vectors[5], vectors[6]).astype(jnp.bfloat16)
        rows_two = spread_rows(normed2)
        pre_act = (
            jnp.einsum("rld,df->rlf", rows_two, fc1_full, preferred_element_type=jnp.float32)
            + fc_bias
        )
        act_low = exact_gelu(pre_act).astype(jnp.bfloat16)
        mlp_part = jnp.einsum("rlf,fd->rld", act_low, fc2_full, preferred_element_type=jnp.float32)
        result = (hidden1 + fold_rows(mlp_part) + vectors[7]).astype(jnp.bfloat16)
        upstream = grad_out[number].astype(jnp.float32)
        up_low = grad_out[number]
        fc2_bias_grad = jnp.sum(upstream, axis=(0, 1))
        up_rows = spread_grads(up_low)
        fc2_grad = jnp.einsum("rlf,rld->fd", act_low, up_rows, preferred_element_type=jnp.float32)
        act_grad = jnp.einsum("rld,fd->rlf", up_rows, fc2_full, preferred_element_type=jnp.float32)
        _, gelu_pull = jax.vjp(exact_gelu, pre_act)
        pre_grad = gelu_pull(act_grad)[0].astype(jnp.bfloat16)
        fc1_bias_grad = jnp.sum(pre_grad.astype(jnp.float32), axis=(0, 1))
        fc1_grad = jnp.einsum("rld,rlf->df", rows_two, pre_grad, preferred_element_type=jnp.float32)
        normed2_grad = fold_grads(
            jnp.einsum("rlf,df->rld", pre_grad, fc1_full, preferred_element_type=jnp.float32)
        )
        _, norm2_pull = jax.vjp(layer_norm, hidden1, vectors[5], vectors[6])
        hidden1_grad, gain2_grad, shift2_grad = norm2_pull(normed2_grad)
        hidden1_grad = hidden1_grad + upstream
        attn_low = hidden1_grad.astype(jnp.bfloat16)
        out_bias_grad = jnp.sum(attn_low.astype(jnp.float32), axis=(0, 1))
        attn_rows = spread_grads(attn_low)
        out_grad = jnp.einsum(
            "rle,rld->ed", attended, attn_rows, preferred_element_type=jnp.float32
        )
        heads_grad = jnp.einsum(
            "rld,ed->rle", attn_rows, out_full, preferred_element_type=jnp.float32
        ).astype(jnp.bfloat16)
        heads_grad = heads_grad.reshape(row_count, length, heads_here, HEAD_DIM)
        query_grad, key_grad, value_grad = lax.map(
            backward_rows,
            (split_heads[0], split_heads[1], split_heads[2], clip_rows, log_totals, heads_grad),
        )
        qkv_grad = (
            jnp.stack([query_grad, key_grad, value_grad])
            .reshape(3, row_count, length, local_width)
            .astype(jnp.bfloat16)
        )
        qkv_grad_wide = qkv_grad.astype(jnp.float32)
        query_bias_grad = jnp.sum(qkv_grad_wide[0], axis=(0, 1))
        value_bias_grad = jnp.sum(qkv_grad_wide[2], axis=(0, 1))
        qkv_weight_grad = jnp.einsum(
            "rld,jrle->jde", rows_one, qkv_grad, preferred_element_type=jnp.float32
        )
        normed1_grad = fold_grads(
            jnp.einsum("jrle,jde->rld", qkv_grad, qkv_full, preferred_element_type=jnp.float32)
        )
        _, norm1_pull = jax.vjp(layer_norm, inputs, vectors[0], vectors[1])
        input_grad, gain1_grad, shift1_grad = norm1_pull(normed1_grad)
        input_grad = input_grad + hidden1_grad
        blank_width = jnp.zeros((width,), jnp.float32)
        query_placed = lax.dynamic_update_slice_in_dim(
            blank_width, query_bias_grad, column_start, 0
        )
        value_placed = lax.dynamic_update_slice_in_dim(
            blank_width, value_bias_grad, column_start, 0
        )
        vector_grad = jnp.stack(
            [
                gain1_grad,
                shift1_grad,
                query_placed,
                value_placed,
                out_bias_grad,
                gain2_grad,
                shift2_grad,
                fc2_bias_grad,
            ]
        )
        hidden_placed = lax.dynamic_update_slice_in_dim(
            jnp.zeros((hidden_total,), jnp.float32), fc1_bias_grad, hidden_start, 0
        )
        grads = (qkv_weight_grad, out_grad, fc1_grad, fc2_grad, vector_grad, hidden_placed)
        result, input_grad, grads = (result, input_grad, grads)
        results.append(result)
        input_grads.append(input_grad)
        vector_sums = lax.psum(
            (
                lax.psum_scatter(grads[4], "wide", scatter_dimension=1, tiled=True),
                lax.psum_scatter(grads[5], "wide", scatter_dimension=0, tiled=True),
            ),
            "narrow",
        )
        settled = (
            lax.psum_scatter(grads[0], "wide", scatter_dimension=1, tiled=True),
            lax.psum_scatter(grads[1], "wide", scatter_dimension=1, tiled=True),
            lax.psum_scatter(grads[2], "wide", scatter_dimension=0, tiled=True),
            lax.psum_scatter(grads[3], "wide", scatter_dimension=1, tiled=True),
            vector_sums[0],
            vector_sums[1],
        )
        shards = settled if shards is None else jax.tree.map(jnp.add, shards, settled)
    return (
        jnp.stack(results),
        jnp.stack(input_grads),
        shards[0],
        shards[1],
        shards[2],
        shards[3],
        shards[4],
        shards[5],
    )


def solution(mesh):
    in_specs = (
        P(None, "wide", "narrow", None),
        P(None, "wide", None),
        P(None, "wide", "narrow"),
        P("narrow", "wide"),
        P("wide", "narrow"),
        P("narrow", "wide"),
        P(None, "wide"),
        P("wide"),
        P(None, "wide", "narrow", None),
    )
    out_specs = (
        P(None, "wide", "narrow", None),
        P(None, "wide", "narrow", None),
        P(None, "wide", "narrow"),
        P("narrow", "wide"),
        P("wide", "narrow"),
        P("narrow", "wide"),
        P(None, "wide"),
        P("wide"),
    )

    def fits(tokens, w_qkv, w_fc1):
        wide, narrow = mesh.shape["wide"], mesh.shape["narrow"]
        width, hidden = w_fc1.shape
        return (
            wide == 8
            and narrow == 4
            and tokens.shape[:2] == (narrow, wide)
            and tokens.shape[2] % (128 * narrow) == 0
            and width == 12 * HEAD_DIM
            and hidden == narrow * width
        )

    def whole(tokens, clip_ids, w_qkv, w_out, w_fc1, w_fc2, norm_bias, fc1_bias, grad_out):
        chosen = fused_local if fits(tokens, w_qkv, w_fc1) else local
        placed = jax.shard_map(chosen, mesh=mesh, in_specs=in_specs, out_specs=out_specs, check_vma=False)
        return placed(tokens, clip_ids, w_qkv, w_out, w_fc1, w_fc2, norm_bias, fc1_bias, grad_out)

    return whole
```

```python
import functools

import jax
import jax.numpy as jnp
from jax import lax
from jax.experimental import pallas as pl
from jax.experimental.pallas import tpu as pltpu
from jax.sharding import PartitionSpec as P

HEAD_DIM = 64
LATE_OUTPUT = 0
MESH = pl.DeviceIdType.MESH
BF16 = jnp.bfloat16
F32 = jnp.float32
NN = (((1,), (0,)), ((), ()))
NT = (((1,), (1,)), ((), ()))
TN = (((0,), (0,)), ((), ()))
GATHER = (((False, False), (False, False)), ((False, True), (False, False)), ((True, True), (True, False)))
SCATTER = (((True, False), (True, False)), ((False, True), (True, False)), ((False, True), (False, False)))
SCHEDULE = {
    1: (("xy1",), ("z1",), ("gout",), (0, 1, 1, 0), (0, 1, 2, 0), (0, 0, 1, 0), (0, 1, 3, 0), (0, 1, 2, 1), (0, 1, 1, 1), (1, 2, 1, 0),),
    2: ((0, 1, 3, 1),),
    3: ((0, 2, 1, 4), (0, 2, 1, 0), (1, 0, 1, 0), (0, 2, 1, 1), (0, 2, 1, 5), (0, 2, 1, 3), ("z2",), (0, 2, 1, 6), ("xy2",), (1, 1, 2, 0), (0, 2, 1, 2), (0, 2, 1, 7), (1, 1, 1, 0),),
    4: ((1, 1, 1, 1), (1, 1, 2, 1),),
    8: ((1, 2, 1, 1),),
    10: ((1, 1, 3, 0),),
    19: ((1, 1, 3, 1), (2, 0, 1, 0),),
    21: ((2, 1, 1, 0),),
    27: ((1, 2, 1, 4),),
    28: ((2, 0, 2, 0), (1, 2, 1, 5),),
    29: ((1, 2, 1, 6), (1, 2, 1, 3),),
    31: ((1, 2, 1, 2), (1, 2, 1, 7),),
    32: ((2, 0, 3, 0),),
    36: ((2, 2, 1, 0),),
    37: ((2, 1, 1, 1),),
    43: ((2, 2, 1, 2),),
    44: ((2, 1, 1, 2),),
    47: ((2, 1, 1, 3),),
    48: ((2, 2, 1, 1), (2, 2, 1, 3), (2, 2, 1, 4),),
    49: ((2, 2, 1, 6),),
    52: ((2, 2, 1, 5), (2, 2, 1, 7),),
    55: (("rs", 2, "a", 1, 1),),
    56: (("rs", 2, "a", 2, 1),),
    58: (("rs", 2, "a", 3, 1),),
    67: (("rs", 2, "a", 3, 0),),
    72: (("rs", 2, "a", 2, 0),),
    73: (("rs", 2, "b"),),
    81: (("rs", 1, "a", 2),),
    83: (("rs", 1, "a", 2, 0), ("rs", 1, "a", 3, 1),),
    88: (("rs", 1, "a", 2, 1), ("rs", 1, "a", 3, 0),),
    94: (("rs", 1, "a", 3),),
    95: (("rs", 2, "a", 1, 0),),
    96: (("rs", 1, "a", 0),),
    98: (("rs", 1, "a", 1),),
    100: (("rs", 1, "a", 1, 1), ("rs", 1, "b", 2), ("rs", 0, "a", 1), ("rs", 1, "a", 1, 0), ("rs", 0, "a", 3),),
    103: (("rs", 0, "a", 2),),
    104: (("rs", 1, "b", 3),),
    106: (("rs", 1, "b"), ("rs", 0, "a", 0),),
    108: (("rs", 0, "b", 1),),
    110: (("rs", 0, "b", 2), ("rs", 2, "c"), ("rs", 0, "b", 3), ("rs", 1, "b", 1), ("rs", 1, "c"), ("rs", 0, "c"),),
}


def dot(a, b, dims):
    return lax.dot_general(a, b, dims, preferred_element_type=F32)


def aligned(value, step):
    return value if isinstance(value, int) else pl.multiple_of(value, step)


def slab_sum(values):
    rows, width = values.shape
    return jnp.sum(values.reshape(rows // 8, 8, width), axis=0)


def row_kernel(
    tok, clip, wqkv, wout, wfc1, wfc2, norm_bias, fc1_bias, gout,
    out_tok, out_gtok, out_g, out_vec,
    wts, psum, gsend, recv,
    xrow, urow, normed1, normed2, attn_grad, outrow, gtrow,
    qs, ks, vs, heads, dheads, act, dgelu, dqkv,
    fa, fb, late, mask, stats, lse,
    smalls, vecs, qbias, vbias, hbias, vpart, vrecv, vsum, vnar,
    tok_s, tok_r, gout_s, gout_r, small_s, small_r,
    ag_s, ag_r, sib_r, gs_s, gs_r, rs_s, rs_r,
    ot_s, ot_r, gt_s, gt_r, vp_s, vp_r, vn_s, vn_r, loc,
):
    depth, width = wfc1.shape[0], tok.shape[-1]
    wide = width // depth
    z_count = wide // 2
    w = lax.axis_index("wide")
    n = lax.axis_index("narrow")
    z, x, y, c = w // 2, w % 2, n // 2, n % 2
    length = xrow.shape[0]
    block = length // 4
    here = (w, n)
    sibling = (w, n ^ 1)
    wide_partners = [(w ^ v, n) for v in range(1, wide)]
    narrow_partners = [(w, n ^ v) for v in range(1, 4)]

    def send(src, dst, s_sem, r_sem, to):
        pltpu.make_async_remote_copy(
            src_ref=src, dst_ref=dst, send_sem=s_sem, recv_sem=r_sem,
            device_id=to, device_id_type=MESH,
        ).start()

    def got(ref, r_sem):
        pltpu.make_async_remote_copy(
            src_ref=ref, dst_ref=ref, send_sem=loc.at[0], recv_sem=r_sem,
            device_id=sibling, device_id_type=MESH,
        ).wait_recv()

    def sent(ref, s_sem):
        pltpu.make_async_remote_copy(
            src_ref=ref, dst_ref=ref, send_sem=s_sem, recv_sem=loc.at[0],
            device_id=sibling, device_id_type=MESH,
        ).wait_send()

    def chosen(table, k):
        first, second = int(table[k][0][1]), int(table[k][1][1])
        return first if first == second else jnp.where(c == 0, first, second)

    def variants(table, k):
        first, second = table[k][0][0], table[k][1][0]
        return [(None, first)] if first == second else [(0, first), (1, second)]

    def on_core(core, action):
        return action if core is None else functools.partial(pl.when(c == core), action)

    gather_x = [chosen(GATHER, k) for k in range(3)]
    scatter_x = [chosen(SCATTER, k) for k in range(3)]
    inner = (z == 1) | (z == 2)
    z_offset = [0, 1, jnp.where(inner, 3, 2), jnp.where(inner, 2, 3)]

    def origin(x_early, rel):
        rz, ra, rb = rel
        ox = x ^ (x_early * ra + (1 - x_early) * rb)
        oy = y ^ (x_early * rb + (1 - x_early) * ra)
        return z ^ rz, ox, oy

    def wts_at(k, rel):
        oz, ox, oy = origin(gather_x[k], rel)
        start = (k * 4 + oy * 2 + c) * width + (oz * 2 + ox) * depth
        return wts.at[pl.ds(aligned(start, 32), depth), :]

    def psum_at(k, rel):
        oz, ox, oy = origin(scatter_x[k], rel)
        start = (k * 2 + oy) * width + (oz * 2 + ox) * depth
        return psum.at[pl.ds(aligned(start, 32), depth), :]

    def partner(x_early, dim, v):
        if dim == 0:
            return (w ^ (2 * v), n)
        x_hop = x_early if dim == 1 else 1 - x_early
        return (w ^ x_hop, n ^ (2 * (1 - x_hop)))

    def pass_on(k, rel, dim, v):
        there = list(rel)
        there[dim] = rel[dim] ^ v
        send(
            wts_at(k, rel), wts_at(k, rel), ag_s.at[k],
            ag_r.at[k, there[0] * 4 + there[1] * 2 + there[2]], partner(gather_x[k], dim, v),
        )

    def along_z(k, i, rel):
        if i == 0:
            pass_on(k, rel, 0, 1)
        pl.when(inner)(lambda: pass_on(k, rel, 0, 3 if i < 2 else 1))

    def hand_on(k, order, phase, i, rel):
        if phase >= 0 and order[phase] == 0:
            along_z(k, i, rel)
        for dim in order[phase + 1 :]:
            if dim == 0:
                along_z(k, i, rel)
            else:
                pass_on(k, rel, dim, 1)
        send(wts_at(k, rel), wts_at(k, rel), ag_s.at[k], sib_r.at[k], sibling)

    def own_along_z(k):
        along_z(k, 0, (0, 0, 0))

    def own_across(k):
        rel = (0, 0, 0)
        pass_on(k, rel, 1, 1)
        pass_on(k, rel, 2, 1)
        send(wts_at(k, rel), wts_at(k, rel), ag_s.at[k], sib_r.at[k], sibling)

    steps = {}

    def register(name, core, action):
        before, mine = steps.get(name), on_core(core, action)
        steps[name] = mine if before is None else lambda: (before(), mine())

    def gather_steps(k, core, z_first):
        order = (0, 1, 2) if z_first else (1, 0, 2)
        held = [(0, 0, 0)]

        def step(phase, named):
            rel = (z_offset[named[0]], named[1], named[2])
            got(wts_at(k, rel), ag_r.at[k, rel[0] * 4 + rel[1] * 2 + rel[2]])
            hand_on(k, order, phase, named[0], rel)

        for phase, dim in enumerate(order):
            fresh = []
            for i in range(1, z_count if dim == 0 else 2):
                for j, named in enumerate(held):
                    there = list(named)
                    there[dim] = i
                    fresh.append(tuple(there))
                    register((k, phase, i, j), core, functools.partial(step, phase, tuple(there)))
            held = held + fresh

    def add_up(k, rel, others):
        here_ref = psum_at(k, rel)
        total = here_ref[...].astype(F32)
        for other in others:
            total = total + other[...].astype(F32)
        return here_ref, total

    nearest_last = list(range(1, z_count)) + [0]

    def scatter_send(k, rz, ra):
        send(
            psum_at(k, (rz, ra, 1)), recv.at[k, rz * 2 + ra], rs_s.at[k],
            rs_r.at[k, rz * 2 + ra], partner(scatter_x[k], 2, 1),
        )

    def scatter_first(k):
        for rz in nearest_last:
            for ra in (1, 0):
                scatter_send(k, rz, ra)

    def scatter_first_part(k, part):
        if part == 0:
            for rz in nearest_last:
                scatter_send(k, rz, 1)

        @pl.when(scatter_x[k] == 1 - part)
        def _():
            for rz in nearest_last:
                scatter_send(k, rz, 0)

    def scatter_steps(k):
        for core, z_first in variants(SCATTER, k):
            scatter_steps_on(k, core, z_first)

    def scatter_steps_on(k, core, z_first):
        second = 2 * z_count
        third = second + (z_count if z_first else 2 * (z_count - 1))

        def fresh(start, i):
            got(recv.at[k, start + i], rs_r.at[k, start + i])
            return recv.at[k, start + i]

        fresh1 = functools.partial(fresh, 0)
        fresh2 = functools.partial(fresh, second)
        fresh3 = functools.partial(fresh, third)
        x_early = scatter_x[k]

        def sum_on(rel, others, slot, to):
            ref, total = add_up(k, rel, others)
            ref[...] = total.astype(BF16)
            send(ref, recv.at[k, slot], rs_s.at[k], rs_r.at[k, slot], to)

        def finish_sum(others):
            _, total = add_up(k, (0, 0, 0), others)
            out_g[k] = total

        if z_first:

            def early_hop(rz):
                sum_on((rz, 1, 0), [fresh1(rz * 2 + 1)], second + rz, partner(x_early, 1, 1))

            def z_hop(rz):
                others = [fresh1(rz * 2), fresh2(rz)]
                sum_on((rz, 0, 0), others, third + rz - 1, partner(x_early, 0, rz))

            for rz in range(z_count):
                register(("rs", k, "a", rz), core, functools.partial(early_hop, rz))
                if rz > 0:
                    register(("rs", k, "b", rz), core, functools.partial(z_hop, rz))

            def last():
                finish_sum([fresh1(0), fresh2(0)] + [fresh3(i) for i in range(z_count - 1)])

        else:

            def z_hop(rz, ra):
                i = (rz - 1) * 2 + ra
                sum_on((rz, ra, 0), [fresh1(rz * 2 + ra)], second + i, partner(x_early, 0, rz))

            def early_hop():
                others = [fresh1(1)] + [fresh2(i * 2 + 1) for i in range(z_count - 1)]
                sum_on((0, 1, 0), others, third, partner(x_early, 1, 1))

            for rz in range(1, z_count):
                for ra in range(2):
                    register(("rs", k, "a", rz, ra), core, functools.partial(z_hop, rz, ra))
            register(("rs", k, "b"), core, early_hop)

            def last():
                finish_sum([fresh1(0)] + [fresh2(i * 2) for i in range(z_count - 1)] + [fresh3(0)])

        register(("rs", k, "c"), core, last)

    point = [0]

    def service(before_last=None):
        point[0] += 1
        names = SCHEDULE.get(point[0], ())
        for i, name in enumerate(names):
            if before_last is not None and i == len(names) - 1:
                before_last()
            steps.pop(name)()

    def weights_here(k):
        service()
        got(wts.at[pl.ds(0, 2 * width), :], sib_r.at[k])

    def weight(k, j, columns=slice(None)):
        return wts[pl.ds(aligned((k * 4 + j) * width, 128), width), columns]

    def own_place(k):
        return pl.ds(aligned((k * 4 + n) * width + w * depth, 32), depth)

    barrier = pltpu.get_barrier_semaphore()
    for to in wide_partners + narrow_partners:
        pl.semaphore_signal(barrier, inc=1, device_id=to, device_id_type=MESH)
    wts[own_place(0), 0:192] = wqkv[0]
    wts[own_place(0), 192:384] = wqkv[2]
    wts[own_place(0), 384:576] = wqkv[1]
    wts[own_place(0), 576:768] = jnp.transpose(wout[...].astype(F32)).astype(BF16)
    wts[own_place(1), :] = wfc1[...]
    wts[own_place(2), :] = wfc2[...]
    smalls[w] = jnp.zeros(smalls.shape[1:], F32)
    smalls[w, 0:8, 0:depth] = norm_bias[...].astype(F32)
    hidden_bias = fc1_bias[...].astype(F32).reshape(1, 4 * depth)
    for r in range(4):
        smalls[w, 8 + r : 9 + r, 0:depth] = hidden_bias[:, r * depth : (r + 1) * depth]

    pl.semaphore_wait(barrier, len(wide_partners) + len(narrow_partners))

    rows_here = pl.ds(aligned(n * block, 128), block)

    def rows_of(to):
        return pl.ds(aligned(to[1] * block, 128), block)

    for i, to in enumerate(wide_partners):
        send(smalls.at[w], smalls.at[w], small_s.at[i], small_r.at[i], to)
    for i, to in enumerate(narrow_partners):
        send(tok.at[to[1]], xrow.at[rows_here, :], tok_s.at[i], tok_r.at[i], to)
    own_along_z(0)
    own_across(0)
    own_tok = pltpu.make_async_copy(tok.at[n], xrow.at[rows_here, :], loc.at[1])
    own_tok.start()
    own_gout = pltpu.make_async_copy(gout.at[n], urow.at[rows_here, :], loc.at[2])
    own_gout.start()

    def start_gout():
        for i, to in enumerate(narrow_partners):
            send(gout.at[to[1]], urow.at[rows_here, :], gout_s.at[i], gout_r.at[i], to)

    for k in range(3):
        for core, z_first in variants(GATHER, k):
            gather_steps(k, core, z_first)
    steps[("z1",)] = functools.partial(own_along_z, 1)
    steps[("xy1",)] = functools.partial(own_across, 1)
    steps[("z2",)] = functools.partial(own_along_z, 2)
    steps[("xy2",)] = functools.partial(own_across, 2)
    steps[("gout",)] = start_gout

    ids = clip[n]
    place = lax.broadcasted_iota(jnp.int32, (1, length), 1)
    ids = jnp.where(ids >= 0, ids, -1 - place).astype(F32)
    ids_down = jnp.transpose(jnp.broadcast_to(ids, (128, length)))[:, 0:1]
    mask[...] = jnp.where(ids_down == ids, 0.0, -1e30)

    for i, to in enumerate(wide_partners):
        got(smalls.at[to[0]], small_r.at[i])
    qbias[...] = jnp.zeros_like(qbias)
    vbias[...] = jnp.zeros_like(vbias)
    for i in range(wide):
        part = smalls[i]
        vecs[:, i * depth : (i + 1) * depth] = part[0:8, 0:depth]
        j, half_at = i // 2, (i % 2) * depth
        qbias[j, :, half_at : half_at + depth] = part[2:3, 0:depth]
        vbias[j, :, 64 + half_at : 64 + half_at + depth] = part[3:4, 0:depth]
        for r in range(4):
            at = (i % 2) * 4 * depth + r * depth
            hbias[j, :, at : at + depth] = part[8 + r : 9 + r, 0:depth]

    service()
    own_tok.wait()
    for i, to in enumerate(narrow_partners):
        got(xrow.at[rows_of(to), :], tok_r.at[i])

    def norm_forward(source, gain, shift, column, target):
        def body(i, _):
            rows = pl.ds(aligned(i * block, 128), block)
            v = source[rows, :].astype(F32)
            average = jnp.mean(v, axis=-1, keepdims=True)
            centred = v - average
            rr = lax.rsqrt(jnp.mean(centred * centred, axis=-1, keepdims=True) + 1e-6)
            stats[rows, column : column + 1] = average
            stats[rows, column + 1 : column + 2] = rr
            target[rows, :] = (centred * rr * vecs[gain : gain + 1] + vecs[shift : shift + 1]).astype(BF16)
            return 0

        lax.fori_loop(0, 4, body, 0)

    norm_forward(xrow, 0, 1, 0, normed1)
    service()

    weights_here(0)
    lane = lax.broadcasted_iota(jnp.int32, (1, 256), 1)
    low = lane[:, 0:128] < 64
    for j in range(4):
        projected = dot(normed1[...], weight(0, j, slice(0, 640)), NN)
        slot = slice(256 * j, 256 * j + 256)
        query = (projected[:, 0:256] + qbias[j]).astype(BF16).astype(F32) * 0.125
        qs[:, slot] = jnp.where(lane < 192, query, 0.0).astype(BF16)
        value = projected[:, 128:384] + vbias[j]
        vs[:, slot] = jnp.where(lane >= 64, value, 0.0).astype(BF16)
        ks[:, slot] = jnp.where(lane < 192, projected[:, 384:640], 0.0).astype(BF16)
        service()

    def lanes(j, second):
        return pl.ds(aligned(256 * j + 128 * second, 128), 128)

    def only(head, values):
        return jnp.where(low if head == 0 else ~low, values, jnp.zeros_like(values))

    def query_of(j, head):
        return only(head, qs[:, lanes(j, 0)]) if head < 2 else qs[:, lanes(j, 1)]

    def key_of(j, head):
        return ks[:, lanes(j, 0)] if head < 2 else ks[:, lanes(j, 1)]

    for j in range(4):
        mixed = []
        for head in range(3):
            scores = dot(query_of(j, head), key_of(j, head), NT) + mask[...]
            row_max = jnp.max(scores, axis=1, keepdims=True)
            weights = jnp.exp(scores - row_max)
            row_sum = jnp.sum(weights, axis=1, keepdims=True)
            probs = (weights * (1.0 / row_sum)).astype(BF16)
            lse[j, :, head : head + 1] = row_max + jnp.log(row_sum)
            service()
            value = vs[:, lanes(j, 0)] if head == 0 else vs[:, lanes(j, 1)]
            mixed.append(dot(probs, value, NN))
            service()
        heads[:, lanes(j, 0)] = mixed[0].astype(BF16)
        heads[:, lanes(j, 1)] = jnp.where(low, mixed[1], mixed[2]).astype(BF16)

    fb[...] = xrow[...].astype(F32) + vecs[4:5]
    for j in range(4):
        fb[...] += dot(heads[:, 256 * j : 256 * j + 256], weight(0, j, slice(512, 768)), NT)
        service()
    fa[...] = fb[...]
    norm_forward(fa, 5, 6, 2, normed2)

    weights_here(1)
    for j in range(4):
        pre = dot(normed2[...], weight(1, j), NN) + hbias[j]
        service()
        cumulative = 0.5 * (1.0 + lax.erf(pre * (0.5**0.5)))
        density = jnp.exp(pre * pre * -0.5) * (0.5 / jnp.pi) ** 0.5
        act[j] = (pre * cumulative).astype(BF16)
        dgelu[j] = (cumulative + pre * density).astype(BF16)
        service()

    def give(k, j, slot, product):
        if k < 2:
            sent(gsend.at[slot], gs_s.at[slot])
        gsend[slot] = product.astype(BF16)
        place = pl.ds(aligned((k * 2 + j) * width, 128), width)
        send(gsend.at[slot], psum.at[place, :], gs_s.at[slot], gs_r.at[k * 2 + j], sibling)

    def keep(k, j, product):
        place = pl.ds(aligned((k * 2 + j) * width, 128), width)
        service()
        got(psum.at[place, :], gs_r.at[k * 2 + j])
        psum[place, :] = (product + psum[place, :].astype(F32)).astype(BF16)

    service()
    own_gout.wait()
    for i, to in enumerate(narrow_partners):
        got(urow.at[rows_of(to), :], gout_r.at[i])
    for j in range(2):
        give(2, j, j, dot(urow[...], act[2 * j + 1 - c], TN))
        service()
    for j in range(2):
        keep(2, j, dot(urow[...], act[2 * j + c], TN))
        service()
    scatter_first(2)
    scatter_steps(2)
    weights_here(2)

    outacc = late if LATE_OUTPUT else fb

    def output():
        for j in range(4):
            outacc[...] = (fa if j == 0 else outacc)[...] + dot(act[j], weight(2, j), NT)
            service()
        outrow[...] = (outacc[...] + vecs[7:8]).astype(BF16)
        for i, to in enumerate(narrow_partners):
            send(outrow.at[rows_of(to), :], out_tok.at[n], ot_s.at[i], ot_r.at[i], to)
        copy = pltpu.make_async_copy(outrow.at[rows_here, :], out_tok.at[n], loc.at[3])
        copy.start()
        return copy

    if LATE_OUTPUT == 0:
        own_out = output()

    def put(row, i, values):
        vpart[i, row : row + 1, 0:depth] = values

    def put_row(row, values):
        for i in range(wide):
            put(row, i, values[:, i * depth : (i + 1) * depth])

    def column_sum(values):
        return jnp.sum(values.astype(F32), axis=0, keepdims=True)

    vpart[...] = jnp.zeros_like(vpart)
    put_row(7, column_sum(urow[...]))
    for j in range(4):
        grad = dot(urow[...], weight(2, j), NN) * dgelu[j].astype(F32)
        dgelu[j] = grad.astype(BF16)
        total = column_sum(dgelu[j])
        for i in range(2):
            for r in range(4):
                at = (i * 4 + r) * depth
                put(8 + r, 2 * j + i, total[:, at : at + depth])
        service()
    for j in range(2):
        give(1, j, j, dot(normed2[...], dgelu[2 * j + 1 - c], TN))
        service()
    for j in range(4):
        product = dot(dgelu[j], weight(1, j), NT)
        fb[...] = product if j == 0 else fb[...] + product
        service()
    for j in range(2):
        keep(1, j, dot(normed2[...], dgelu[2 * j + c], TN))
        service()
    scatter_first(1)
    scatter_steps(1)

    def norm_backward(source, grad, gain, column, extra, target, rounded):
        def body(i, sums):
            rows = pl.ds(aligned(i * block, 128), block)
            rr = stats[rows, column + 1 : column + 2]
            xhat = (source[rows, :].astype(F32) - stats[rows, column : column + 1]) * rr
            n_grad = grad[rows, :]
            u = n_grad * vecs[gain : gain + 1]
            inner = u - jnp.mean(u, axis=-1, keepdims=True) - xhat * jnp.mean(u * xhat, axis=-1, keepdims=True)
            result = rr * inner + extra[rows, :].astype(F32)
            if target is not None:
                target[rows, :] = result
            low_result = result.astype(BF16)
            rounded[rows, :] = low_result
            return (
                sums[0] + slab_sum(n_grad * xhat),
                sums[1] + slab_sum(n_grad),
                sums[2] + slab_sum(low_result.astype(F32)),
            )

        zero = jnp.zeros((8, width), F32)
        sums = lax.fori_loop(0, 4, body, (zero, zero, zero))
        return [jnp.sum(s, axis=0, keepdims=True) for s in sums]

    gain2, shift2, attn_total = norm_backward(fa, fb, 5, 2, urow, fb, attn_grad)
    if LATE_OUTPUT == 1:
        own_out = output()
    put_row(5, gain2)
    put_row(6, shift2)
    put_row(4, attn_total)

    for j in range(4):
        back = dot(attn_grad[...], weight(0, j, slice(512, 768)), NN)
        dheads[:, 256 * j : 256 * j + 256] = jnp.where(lane >= 64, back, 0.0).astype(BF16)
        service()

    def attention_backward(j):
        def value_of(head):
            return vs[:, lanes(j, 0)] if head == 0 else vs[:, lanes(j, 1)]

        def upstream_of(head):
            if head == 0:
                return dheads[:, lanes(j, 0)]
            return only(head - 1, dheads[:, lanes(j, 1)])

        dq, dk, dv = [], [], []
        for head in range(3):
            query, key, up = query_of(j, head), key_of(j, head), upstream_of(head)
            second = int(head > 0)
            delta = jnp.sum(
                up.astype(F32) * heads[:, lanes(j, second)].astype(F32), axis=1, keepdims=True
            )
            scores = dot(query, key, NT) + mask[...]
            soft = jnp.exp(scores - lse[j, :, head : head + 1])
            prob_grad = dot(up, value_of(head), NT)
            score_grad = (soft * (prob_grad - delta)).astype(BF16)
            service()
            dq.append(dot(score_grad, key, NN))
            dk.append(dot(score_grad, query, TN))
            dv.append(dot(soft.astype(BF16), up, TN))
            service()
        dqkv[j, :, 0:128] = (jnp.where(low, dq[0], dq[1]) * 0.125).astype(BF16)
        dqkv[j, :, 128:256] = (dq[2] * 0.125 + dv[0]).astype(BF16)
        dqkv[j, :, 256:384] = (dv[1] + dv[2]).astype(BF16)
        dqkv[j, :, 384:512] = (dk[0] + dk[1]).astype(BF16)
        dqkv[j, :, 512:640] = dk[2].astype(BF16)
        total = column_sum(dqkv[j, :, 0:384])
        for i in range(2):
            put(2, 2 * j + i, total[:, i * depth : (i + 1) * depth])
            put(3, 2 * j + i, total[:, (2 + i) * depth : (3 + i) * depth])

    def projection_grad(j):
        first = dot(normed1[...], dqkv[j], TN)
        second = dot(attn_grad[...], heads[:, pl.ds(aligned(256 * j, 128), 256)], TN)
        return jnp.concatenate(
            [first[:, 0:512], first[:, 512:640] + second[:, 0:128], second[:, 128:256]], axis=1
        )

    for i, half in enumerate((1 - y, y)):
        for own in (False, True):
            j = 2 * half + (c if own else 1 - c)
            attention_backward(j)
            if own:
                keep(0, half, projection_grad(j))
            else:
                give(0, half, i, projection_grad(j))
            service()
        scatter_first_part(0, i)
        if i == 0:
            scatter_steps(0)
            if LATE_OUTPUT == 2:
                own_out = output()
    for j in range(4):
        product = dot(dqkv[j], weight(0, j, slice(0, 640)), NT)
        fa[...] = product if j == 0 else fa[...] + product
        service()

    gain1, shift1, _ = norm_backward(xrow, fa, 0, 0, fb, None, gtrow)
    for i, to in enumerate(narrow_partners):
        rows = pl.ds(aligned(to[1] * block, 128), block)
        send(gtrow.at[rows, :], out_gtok.at[n], gt_s.at[i], gt_r.at[i], to)
    own_gtok = pltpu.make_async_copy(gtrow.at[rows_here, :], out_gtok.at[n], loc.at[4])
    own_gtok.start()
    service()
    put_row(0, gain1)
    put_row(1, shift1)
    for i, to in enumerate(wide_partners):
        send(vpart.at[to[0]], vrecv.at[i], vp_s.at[i], vp_r.at[i], to)

    def share_vectors():
        total = vpart[w]
        for i in range(len(wide_partners)):
            got(vrecv.at[i], vp_r.at[i])
            total = total + vrecv[i]
        vsum[...] = total
        for i, to in enumerate(narrow_partners):
            send(vsum, vnar.at[i], vn_s.at[i], vn_r.at[i], to)

    service(share_vectors)
    assert not steps
    total = vsum[...]
    for i in range(3):
        got(vnar.at[i], vn_r.at[i])
        total = total + vnar[i]
    out_vec[...] = total

    for i, to in enumerate(narrow_partners):
        got(out_tok.at[to[1]], ot_r.at[i])
        got(out_gtok.at[to[1]], gt_r.at[i])
        sent(tok.at[0], tok_s.at[i])
        sent(gout.at[0], gout_s.at[i])
        sent(outrow.at[pl.ds(0, block), :], ot_s.at[i])
        sent(gtrow.at[pl.ds(0, block), :], gt_s.at[i])
        sent(vsum, vn_s.at[i])
    for i in range(len(wide_partners)):
        sent(smalls.at[0], small_s.at[i])
        sent(vpart.at[0], vp_s.at[i])
    for k in range(3):
        for core, z_first in variants(GATHER, k):
            z_sends = (1, 2 + 3) if z_first else (2, 4 + 6)
            across = (1 + 3) + (1 + 3 + 4) if z_first else 1 + (1 + 1 + 6)
            for place, count in zip((~inner, inner), z_sends):
                rows = (count + across + 4 * z_count) * depth
                all_sent = functools.partial(sent, wts.at[pl.ds(0, rows), :], ag_s.at[k])
                pl.when(place if core is None else place & (c == core))(all_sent)
        sends = 4 * z_count - 1
        sent(psum.at[pl.ds(0, sends * depth), :], rs_s.at[k])
    for slot in range(2):
        sent(gsend.at[slot], gs_s.at[slot])
    own_out.wait()
    own_gtok.wait()


def settle_kernel(tok, gtok, g, vec, out_tok, out_gtok, out_qkv, out_proj, out_fc1, out_fc2, out_nb, out_fb):
    out_tok[...] = tok[...]
    out_gtok[...] = gtok[...].astype(F32)

    @pl.when(pl.program_id(0) == 0)
    def _():
        depth, part = out_qkv.shape[1:]
        out_qkv[0] = g[0, :, 0:part]
        out_qkv[1] = g[0, :, 2 * part : 3 * part]
        out_qkv[2] = g[0, :, part : 2 * part]
        out_proj[...] = jnp.transpose(g[0, :, 3 * part :])
        out_fc1[...] = g[1]
        out_fc2[...] = g[2]
        out_nb[...] = vec[0:8, 0:depth]
        pieces = [vec[8 + r : 9 + r, 0:depth] for r in range(4)]
        out_fb[...] = jnp.concatenate(pieces, axis=1).reshape(4 * depth)


def fused_local(tokens, clip_ids, w_qkv, w_out, w_fc1, w_fc2, norm_bias, fc1_bias, grad_out):
    micro, _, block, width = tokens.shape
    depth, hidden = w_fc1.shape
    wide = width // depth
    z_count = wide // 2
    length = micro * block

    def anywhere():
        return pl.BlockSpec(memory_space=pl.ANY)

    def vmem():
        return pl.BlockSpec(memory_space=pltpu.VMEM)

    def flat(*shape):
        return pltpu.VMEM(shape, BF16)

    def wide_type(*shape):
        return pltpu.VMEM(shape, F32)

    def sems(*shape):
        return pltpu.SemaphoreType.DMA(shape)

    out_tok, out_gtok, out_g, out_vec = pl.pallas_call(
        row_kernel,
        out_shape=(
            jax.ShapeDtypeStruct((micro, block, width), BF16),
            jax.ShapeDtypeStruct((micro, block, width), BF16),
            jax.ShapeDtypeStruct((3, depth, width), F32),
            jax.ShapeDtypeStruct((16, 128), F32),
        ),
        in_specs=[anywhere()] + [vmem()] * 7 + [anywhere()],
        out_specs=(anywhere(), anywhere(), vmem(), vmem()),
        scratch_shapes=[
            flat(12 * width, hidden),
            flat(6 * width, hidden),
            flat(2, width, hidden),
            flat(3, 4 * z_count - 1, depth, hidden),
            *[flat(length, width)] * 7,
            *[flat(length, 1024)] * 5,
            flat(4, length, hidden),
            flat(4, length, hidden),
            flat(4, length, 640),
            wide_type(length, width),
            wide_type(length, width),
            wide_type(length if LATE_OUTPUT else 8, width),
            wide_type(length, length),
            wide_type(length, 128),
            wide_type(4, length, 128),
            wide_type(wide, 16, 128),
            wide_type(8, width),
            wide_type(4, 1, 256),
            wide_type(4, 1, 256),
            wide_type(4, 1, hidden),
            wide_type(wide, 16, 128),
            wide_type(wide - 1, 16, 128),
            wide_type(16, 128),
            wide_type(3, 16, 128),
            sems(3), sems(3), sems(3), sems(3), sems(wide - 1), sems(wide - 1),
            sems(3), sems(3, 4 * z_count), sems(3), sems(2), sems(6),
            sems(3), sems(3, 4 * z_count - 1),
            sems(3), sems(3), sems(3), sems(3), sems(wide - 1), sems(wide - 1), sems(3), sems(3),
            sems(5),
        ],
        compiler_params=pltpu.CompilerParams(
            collective_id=0, has_side_effects=True, vmem_limit_bytes=63 * 2**20
        ),
    )(
        tokens.reshape(micro, block, width), clip_ids, w_qkv, w_out, w_fc1, w_fc2.T, norm_bias,
        fc1_bias, grad_out.reshape(micro, block, width),
    )
    part = width // 4
    shapes = [(3, depth, part), (part, depth), (depth, width), (depth, width), (8, depth), (4 * depth,)]
    rows_spec = pl.BlockSpec((micro // 2, block, width), lambda i: (i, 0, 0))

    def fixed(shape):
        return pl.BlockSpec(shape, lambda i: (0,) * len(shape))

    out, gtok, grad_qkv, grad_proj, grad_fc1, grad_fc2, grad_nb, grad_fb = pl.pallas_call(
        settle_kernel,
        grid=(2,),
        out_shape=[
            jax.ShapeDtypeStruct((micro, block, width), BF16),
            jax.ShapeDtypeStruct((micro, block, width), F32),
            *[jax.ShapeDtypeStruct(shape, F32) for shape in shapes],
        ],
        in_specs=[rows_spec, rows_spec, fixed((3, depth, width)), fixed((16, 128))],
        out_specs=[rows_spec, rows_spec, *[fixed(shape) for shape in shapes]],
    )(out_tok, out_gtok, out_g, out_vec)
    return (
        out[:, None],
        gtok[:, None],
        grad_qkv,
        grad_proj,
        grad_fc1,
        grad_fc2.T,
        grad_nb,
        grad_fb,
    )


def layer_norm(values, scaling, shifting):
    average = jnp.mean(values, axis=-1, keepdims=True)
    centred = values - average
    variance = jnp.mean(centred * centred, axis=-1, keepdims=True)
    return centred * lax.rsqrt(variance + 1e-06) * scaling + shifting


def exact_gelu(values):
    return jax.nn.gelu(values, approximate=False)


def block_scores(query_block, keys, clip_block, clip_row, block_start, score_scale):
    block_rows = query_block.shape[0]
    length = keys.shape[0]
    scores = (
        jnp.einsum("qhd,khd->hqk", query_block, keys, preferred_element_type=jnp.float32)
        * score_scale
    )
    key_place = lax.broadcasted_iota(jnp.int32, (block_rows, length), 1)
    query_place = block_start + lax.broadcasted_iota(jnp.int32, (block_rows, length), 0)
    allowed = (clip_block[:, None] == clip_row[None, :]) & (clip_row[None, :] >= 0) | (
        query_place == key_place
    )
    return jnp.where(allowed[None], scores, -1e30)


def row_forward(query, keys, values, clip_row, score_scale):
    length = query.shape[0]
    block_rows = min(512, length)

    def one_block(block_start):
        scores = block_scores(query, keys, clip_row, clip_row, block_start, score_scale)
        row_max = jnp.max(scores, axis=-1, keepdims=True)
        weights = jnp.exp(scores - row_max)
        row_sum = jnp.sum(weights, axis=-1, keepdims=True)
        probabilities = (weights / row_sum).astype(jnp.bfloat16)
        mixed = jnp.einsum(
            "hqk,khd->qhd", probabilities, values, preferred_element_type=jnp.float32
        )
        return (mixed, (row_max + jnp.log(row_sum))[..., 0])

    starts = lax.broadcasted_iota(jnp.int32, (length // block_rows,), 0) * block_rows
    mixed, log_totals = lax.map(one_block, starts)
    return (mixed.reshape(length, -1), log_totals)


def row_backward(query, keys, values, clip_row, log_totals, grad_heads, score_scale):
    length = query.shape[0]
    block_rows = min(512, length)

    def one_block(running, element):
        key_grad, value_grad = running
        block_start, block_totals = element
        scores = block_scores(query, keys, clip_row, clip_row, block_start, score_scale)
        probabilities = jnp.exp(scores - block_totals[..., None])
        prob_grad = jnp.einsum(
            "qhd,khd->hqk", grad_heads, values, preferred_element_type=jnp.float32
        )
        value_grad = value_grad + jnp.einsum(
            "hqk,qhd->khd",
            probabilities.astype(jnp.bfloat16),
            grad_heads,
            preferred_element_type=jnp.float32,
        )
        score_grad = probabilities * (
            prob_grad - jnp.sum(probabilities * prob_grad, axis=-1, keepdims=True)
        )
        score_grad = score_grad.astype(jnp.bfloat16)
        query_grad = (
            jnp.einsum("hqk,khd->qhd", score_grad, keys, preferred_element_type=jnp.float32)
            * score_scale
        )
        key_grad = (
            key_grad
            + jnp.einsum("hqk,qhd->khd", score_grad, query, preferred_element_type=jnp.float32)
            * score_scale
        )
        return ((key_grad, value_grad), query_grad)

    starts = lax.broadcasted_iota(jnp.int32, (length // block_rows,), 0) * block_rows
    zero_grads = jnp.zeros(keys.shape, jnp.float32)
    (key_grad, value_grad), query_grads = lax.scan(
        one_block, (zero_grads, zero_grads), (starts, log_totals)
    )
    return (query_grads.reshape(query.shape), key_grad, value_grad)


def local(tokens, clip_ids, w_qkv, w_out, w_fc1, w_fc2, norm_bias, fc1_bias, grad_out):
    micro_count = tokens.shape[0]
    row_count = tokens.shape[1]
    width = tokens.shape[3]
    local_width = w_qkv.shape[2]
    local_hidden = w_fc1.shape[1]
    heads_here = local_width // HEAD_DIM
    score_scale = HEAD_DIM ** (-0.5)
    narrow_index = lax.axis_index("narrow")

    def spread_rows(values):
        return lax.all_gather(values, "narrow", axis=1, tiled=True)

    def fold_rows(values):
        return lax.psum_scatter(values, "narrow", scatter_dimension=1, tiled=True)

    def spread_grads(values):
        return lax.all_gather(values, "narrow", axis=1, tiled=True)

    def fold_grads(values):
        return lax.psum_scatter(values, "narrow", scatter_dimension=1, tiled=True)

    def forward_rows(element):
        return row_forward(element[0], element[1], element[2], element[3], score_scale)

    def backward_rows(element):
        return row_backward(
            element[0], element[1], element[2], element[3], element[4], element[5], score_scale
        )

    results = []
    input_grads = []
    shards = None
    for number in range(micro_count):
        qkv_full = lax.all_gather(w_qkv, "wide", axis=1, tiled=True)
        out_full = lax.all_gather(w_out, "wide", axis=1, tiled=True)
        fc1_full = lax.all_gather(w_fc1, "wide", axis=0, tiled=True)
        fc2_full = lax.all_gather(w_fc2, "wide", axis=1, tiled=True)
        vector_full = lax.all_gather(norm_bias, "wide", axis=1, tiled=True)
        hidden_bias_full = lax.all_gather(fc1_bias, "wide", axis=0, tiled=True)
        vectors = vector_full.astype(jnp.float32)
        hidden_total = hidden_bias_full.shape[0]
        column_start = narrow_index * local_width
        hidden_start = narrow_index * local_hidden
        fc_bias = lax.dynamic_slice_in_dim(hidden_bias_full, hidden_start, local_hidden, 0).astype(
            jnp.float32
        )
        query_bias = lax.dynamic_slice_in_dim(vectors[2], column_start, local_width, 0)
        value_bias = lax.dynamic_slice_in_dim(vectors[3], column_start, local_width, 0)
        inputs = tokens[number].astype(jnp.float32)
        clip_rows = clip_ids[number]
        normed1 = layer_norm(inputs, vectors[0], vectors[1]).astype(jnp.bfloat16)
        rows_one = spread_rows(normed1)
        length = rows_one.shape[1]
        projected = jnp.einsum(
            "rld,jde->jrle", rows_one, qkv_full, preferred_element_type=jnp.float32
        )
        bias_three = jnp.stack([query_bias, jnp.zeros_like(query_bias), value_bias])
        qkv_low = (projected + bias_three[:, None, None, :]).astype(jnp.bfloat16)
        split_heads = qkv_low.reshape(3, row_count, length, heads_here, HEAD_DIM)
        attended, log_totals = lax.map(
            forward_rows, (split_heads[0], split_heads[1], split_heads[2], clip_rows)
        )
        attended = attended.astype(jnp.bfloat16)
        attention_part = jnp.einsum(
            "rle,ed->rld", attended, out_full, preferred_element_type=jnp.float32
        )
        hidden1 = inputs + fold_rows(attention_part) + vectors[4]
        normed2 = layer_norm(hidden1, vectors[5], vectors[6]).astype(jnp.bfloat16)
        rows_two = spread_rows(normed2)
        pre_act = (
            jnp.einsum("rld,df->rlf", rows_two, fc1_full, preferred_element_type=jnp.float32)
            + fc_bias
        )
        act_low = exact_gelu(pre_act).astype(jnp.bfloat16)
        mlp_part = jnp.einsum("rlf,fd->rld", act_low, fc2_full, preferred_element_type=jnp.float32)
        result = (hidden1 + fold_rows(mlp_part) + vectors[7]).astype(jnp.bfloat16)
        upstream = grad_out[number].astype(jnp.float32)
        up_low = grad_out[number]
        fc2_bias_grad = jnp.sum(upstream, axis=(0, 1))
        up_rows = spread_grads(up_low)
        fc2_grad = jnp.einsum("rlf,rld->fd", act_low, up_rows, preferred_element_type=jnp.float32)
        act_grad = jnp.einsum("rld,fd->rlf", up_rows, fc2_full, preferred_element_type=jnp.float32)
        _, gelu_pull = jax.vjp(exact_gelu, pre_act)
        pre_grad = gelu_pull(act_grad)[0].astype(jnp.bfloat16)
        fc1_bias_grad = jnp.sum(pre_grad.astype(jnp.float32), axis=(0, 1))
        fc1_grad = jnp.einsum("rld,rlf->df", rows_two, pre_grad, preferred_element_type=jnp.float32)
        normed2_grad = fold_grads(
            jnp.einsum("rlf,df->rld", pre_grad, fc1_full, preferred_element_type=jnp.float32)
        )
        _, norm2_pull = jax.vjp(layer_norm, hidden1, vectors[5], vectors[6])
        hidden1_grad, gain2_grad, shift2_grad = norm2_pull(normed2_grad)
        hidden1_grad = hidden1_grad + upstream
        attn_low = hidden1_grad.astype(jnp.bfloat16)
        out_bias_grad = jnp.sum(attn_low.astype(jnp.float32), axis=(0, 1))
        attn_rows = spread_grads(attn_low)
        out_grad = jnp.einsum(
            "rle,rld->ed", attended, attn_rows, preferred_element_type=jnp.float32
        )
        heads_grad = jnp.einsum(
            "rld,ed->rle", attn_rows, out_full, preferred_element_type=jnp.float32
        ).astype(jnp.bfloat16)
        heads_grad = heads_grad.reshape(row_count, length, heads_here, HEAD_DIM)
        query_grad, key_grad, value_grad = lax.map(
            backward_rows,
            (split_heads[0], split_heads[1], split_heads[2], clip_rows, log_totals, heads_grad),
        )
        qkv_grad = (
            jnp.stack([query_grad, key_grad, value_grad])
            .reshape(3, row_count, length, local_width)
            .astype(jnp.bfloat16)
        )
        qkv_grad_wide = qkv_grad.astype(jnp.float32)
        query_bias_grad = jnp.sum(qkv_grad_wide[0], axis=(0, 1))
        value_bias_grad = jnp.sum(qkv_grad_wide[2], axis=(0, 1))
        qkv_weight_grad = jnp.einsum(
            "rld,jrle->jde", rows_one, qkv_grad, preferred_element_type=jnp.float32
        )
        normed1_grad = fold_grads(
            jnp.einsum("jrle,jde->rld", qkv_grad, qkv_full, preferred_element_type=jnp.float32)
        )
        _, norm1_pull = jax.vjp(layer_norm, inputs, vectors[0], vectors[1])
        input_grad, gain1_grad, shift1_grad = norm1_pull(normed1_grad)
        input_grad = input_grad + hidden1_grad
        blank_width = jnp.zeros((width,), jnp.float32)
        query_placed = lax.dynamic_update_slice_in_dim(
            blank_width, query_bias_grad, column_start, 0
        )
        value_placed = lax.dynamic_update_slice_in_dim(
            blank_width, value_bias_grad, column_start, 0
        )
        vector_grad = jnp.stack(
            [
                gain1_grad,
                shift1_grad,
                query_placed,
                value_placed,
                out_bias_grad,
                gain2_grad,
                shift2_grad,
                fc2_bias_grad,
            ]
        )
        hidden_placed = lax.dynamic_update_slice_in_dim(
            jnp.zeros((hidden_total,), jnp.float32), fc1_bias_grad, hidden_start, 0
        )
        grads = (qkv_weight_grad, out_grad, fc1_grad, fc2_grad, vector_grad, hidden_placed)
        result, input_grad, grads = (result, input_grad, grads)
        results.append(result)
        input_grads.append(input_grad)
        vector_sums = lax.psum(
            (
                lax.psum_scatter(grads[4], "wide", scatter_dimension=1, tiled=True),
                lax.psum_scatter(grads[5], "wide", scatter_dimension=0, tiled=True),
            ),
            "narrow",
        )
        settled = (
            lax.psum_scatter(grads[0], "wide", scatter_dimension=1, tiled=True),
            lax.psum_scatter(grads[1], "wide", scatter_dimension=1, tiled=True),
            lax.psum_scatter(grads[2], "wide", scatter_dimension=0, tiled=True),
            lax.psum_scatter(grads[3], "wide", scatter_dimension=1, tiled=True),
            vector_sums[0],
            vector_sums[1],
        )
        shards = settled if shards is None else jax.tree.map(jnp.add, shards, settled)
    return (
        jnp.stack(results),
        jnp.stack(input_grads),
        shards[0],
        shards[1],
        shards[2],
        shards[3],
        shards[4],
        shards[5],
    )


def solution(mesh):
    in_specs = (
        P(None, "wide", "narrow", None),
        P(None, "wide", None),
        P(None, "wide", "narrow"),
        P("narrow", "wide"),
        P("wide", "narrow"),
        P("narrow", "wide"),
        P(None, "wide"),
        P("wide"),
        P(None, "wide", "narrow", None),
    )
    out_specs = (
        P(None, "wide", "narrow", None),
        P(None, "wide", "narrow", None),
        P(None, "wide", "narrow"),
        P("narrow", "wide"),
        P("wide", "narrow"),
        P("narrow", "wide"),
        P(None, "wide"),
        P("wide"),
    )

    def fits(tokens, w_qkv, w_fc1):
        wide, narrow = mesh.shape["wide"], mesh.shape["narrow"]
        width, hidden = w_fc1.shape
        return (
            wide == 8
            and narrow == 4
            and tokens.shape[:2] == (narrow, wide)
            and tokens.shape[2] % (128 * narrow) == 0
            and width == 12 * HEAD_DIM
            and hidden == narrow * width
        )

    def whole(tokens, clip_ids, w_qkv, w_out, w_fc1, w_fc2, norm_bias, fc1_bias, grad_out):
        chosen = fused_local if fits(tokens, w_qkv, w_fc1) else local
        placed = jax.shard_map(chosen, mesh=mesh, in_specs=in_specs, out_specs=out_specs, check_vma=False)
        return placed(tokens, clip_ids, w_qkv, w_out, w_fc1, w_fc2, norm_bias, fc1_bias, grad_out)

    return whole
```

```python
import functools

import jax
import jax.numpy as jnp
from jax import lax
from jax.experimental import pallas as pl
from jax.experimental.pallas import tpu as pltpu
from jax.sharding import PartitionSpec as P

HEAD_DIM = 64
LATE_OUTPUT = 0
MESH = pl.DeviceIdType.MESH
BF16 = jnp.bfloat16
F32 = jnp.float32
NN = (((1,), (0,)), ((), ()))
NT = (((1,), (1,)), ((), ()))
TN = (((0,), (0,)), ((), ()))
GATHER = (((False, False), (False, False)), ((False, True), (False, False)), ((True, True), (True, False)))
SCATTER = (((True, False), (True, False)), ((False, True), (True, False)), ((False, True), (False, False)))
SCHEDULE = {
    1: (("xy1",), ("z1",), ("gout",), (0, 1, 1, 0), (0, 1, 2, 0), (0, 0, 1, 0), (0, 1, 3, 0), (0, 1, 2, 1), (0, 1, 1, 1), (1, 2, 1, 0),),
    2: ((0, 1, 3, 1),),
    3: ((0, 2, 1, 4), (0, 2, 1, 0), (1, 0, 1, 0), (0, 2, 1, 1), (0, 2, 1, 5), (0, 2, 1, 3), ("z2",), (0, 2, 1, 6), ("xy2",), (1, 1, 2, 0), (0, 2, 1, 2), (0, 2, 1, 7), (1, 1, 1, 0),),
    4: ((1, 1, 1, 1), (1, 1, 2, 1),),
    8: ((1, 2, 1, 1),),
    10: ((1, 1, 3, 0),),
    19: ((1, 1, 3, 1), (2, 0, 1, 0),),
    21: ((2, 1, 1, 0),),
    27: ((1, 2, 1, 4),),
    28: ((2, 0, 2, 0), (1, 2, 1, 5),),
    29: ((1, 2, 1, 6), (1, 2, 1, 3),),
    31: ((1, 2, 1, 2), (1, 2, 1, 7),),
    32: ((2, 0, 3, 0),),
    36: ((2, 2, 1, 0),),
    37: ((2, 1, 1, 1),),
    43: ((2, 2, 1, 2),),
    44: ((2, 1, 1, 2),),
    47: ((2, 1, 1, 3),),
    48: ((2, 2, 1, 1), (2, 2, 1, 3), (2, 2, 1, 4),),
    49: ((2, 2, 1, 6),),
    52: ((2, 2, 1, 5), (2, 2, 1, 7),),
    55: (("rs", 2, "a", 1, 1),),
    56: (("rs", 2, "a", 2, 1),),
    58: (("rs", 2, "a", 3, 1),),
    67: (("rs", 2, "a", 3, 0),),
    72: (("rs", 2, "a", 2, 0),),
    73: (("rs", 2, "b"),),
    81: (("rs", 1, "a", 2),),
    83: (("rs", 1, "a", 2, 0), ("rs", 1, "a", 3, 1),),
    88: (("rs", 1, "a", 2, 1), ("rs", 1, "a", 3, 0),),
    94: (("rs", 1, "a", 3),),
    95: (("rs", 2, "a", 1, 0),),
    96: (("rs", 1, "a", 0),),
    98: (("rs", 1, "a", 1),),
    100: (("rs", 1, "a", 1, 1), ("rs", 1, "b", 2), ("rs", 0, "a", 1), ("rs", 1, "a", 1, 0), ("rs", 0, "a", 3),),
    103: (("rs", 0, "a", 2),),
    104: (("rs", 1, "b", 3),),
    106: (("rs", 1, "b"), ("rs", 0, "a", 0),),
    108: (("rs", 0, "b", 1),),
    110: (("rs", 0, "b", 2), ("rs", 2, "c"), ("rs", 0, "b", 3), ("rs", 1, "b", 1), ("rs", 1, "c"), ("rs", 0, "c"),),
}


def dot(a, b, dims):
    return lax.dot_general(a, b, dims, preferred_element_type=F32)


def aligned(value, step):
    return value if isinstance(value, int) else pl.multiple_of(value, step)


def slab_sum(values):
    rows, width = values.shape
    return jnp.sum(values.reshape(rows // 8, 8, width), axis=0)


def row_kernel(
    tok, clip, wqkv, wout, wfc1, wfc2, norm_bias, fc1_bias, gout,
    out_tok, out_gtok, out_g, out_vec,
    wts, psum, gsend, recv,
    xrow, urow, normed1, normed2, attn_grad, outrow, gtrow,
    qs, ks, vs, heads, dheads, act, dgelu, dqkv,
    fa, fb, late, mask, stats, lse,
    smalls, vecs, qbias, vbias, hbias, vpart, vrecv, vsum, vnar,
    tok_s, tok_r, gout_s, gout_r, small_s, small_r,
    ag_s, ag_r, sib_r, gs_s, gs_r, rs_s, rs_r,
    ot_s, ot_r, gt_s, gt_r, vp_s, vp_r, vn_s, vn_r, loc,
):
    depth, width = wfc1.shape[0], tok.shape[-1]
    wide = width // depth
    z_count = wide // 2
    w = lax.axis_index("wide")
    n = lax.axis_index("narrow")
    z, x, y, c = w // 2, w % 2, n // 2, n % 2
    length = xrow.shape[0]
    block = length // 4
    here = (w, n)
    sibling = (w, n ^ 1)
    wide_partners = [(w ^ v, n) for v in range(1, wide)]
    narrow_partners = [(w, n ^ v) for v in range(1, 4)]

    def send(src, dst, s_sem, r_sem, to):
        pltpu.make_async_remote_copy(
            src_ref=src, dst_ref=dst, send_sem=s_sem, recv_sem=r_sem,
            device_id=to, device_id_type=MESH,
        ).start()

    def got(ref, r_sem):
        pltpu.make_async_remote_copy(
            src_ref=ref, dst_ref=ref, send_sem=loc.at[0], recv_sem=r_sem,
            device_id=sibling, device_id_type=MESH,
        ).wait_recv()

    def sent(ref, s_sem):
        pltpu.make_async_remote_copy(
            src_ref=ref, dst_ref=ref, send_sem=s_sem, recv_sem=loc.at[0],
            device_id=sibling, device_id_type=MESH,
        ).wait_send()

    def chosen(table, k):
        first, second = int(table[k][0][1]), int(table[k][1][1])
        return first if first == second else jnp.where(c == 0, first, second)

    def variants(table, k):
        first, second = table[k][0][0], table[k][1][0]
        return [(None, first)] if first == second else [(0, first), (1, second)]

    def on_core(core, action):
        return action if core is None else functools.partial(pl.when(c == core), action)

    gather_x = [chosen(GATHER, k) for k in range(3)]
    scatter_x = [chosen(SCATTER, k) for k in range(3)]
    inner = (z == 1) | (z == 2)
    z_offset = [0, 1, jnp.where(inner, 3, 2), jnp.where(inner, 2, 3)]

    def origin(x_early, rel):
        rz, ra, rb = rel
        ox = x ^ (x_early * ra + (1 - x_early) * rb)
        oy = y ^ (x_early * rb + (1 - x_early) * ra)
        return z ^ rz, ox, oy

    def wts_at(k, rel):
        oz, ox, oy = origin(gather_x[k], rel)
        start = (k * 4 + oy * 2 + c) * width + (oz * 2 + ox) * depth
        return wts.at[pl.ds(aligned(start, 32), depth), :]

    def psum_at(k, rel):
        oz, ox, oy = origin(scatter_x[k], rel)
        start = (k * 2 + oy) * width + (oz * 2 + ox) * depth
        return psum.at[pl.ds(aligned(start, 32), depth), :]

    def partner(x_early, dim, v):
        if dim == 0:
            return (w ^ (2 * v), n)
        x_hop = x_early if dim == 1 else 1 - x_early
        return (w ^ x_hop, n ^ (2 * (1 - x_hop)))

    def pass_on(k, rel, dim, v):
        there = list(rel)
        there[dim] = rel[dim] ^ v
        send(
            wts_at(k, rel), wts_at(k, rel), ag_s.at[k],
            ag_r.at[k, there[0] * 4 + there[1] * 2 + there[2]], partner(gather_x[k], dim, v),
        )

    def along_z(k, i, rel):
        if i == 0:
            pass_on(k, rel, 0, 1)
        pl.when(inner)(lambda: pass_on(k, rel, 0, 3 if i < 2 else 1))

    def hand_on(k, order, phase, i, rel):
        if phase >= 0 and order[phase] == 0:
            along_z(k, i, rel)
        for dim in order[phase + 1 :]:
            if dim == 0:
                along_z(k, i, rel)
            else:
                pass_on(k, rel, dim, 1)
        send(wts_at(k, rel), wts_at(k, rel), ag_s.at[k], sib_r.at[k], sibling)

    def own_along_z(k):
        along_z(k, 0, (0, 0, 0))

    def own_across(k):
        rel = (0, 0, 0)
        pass_on(k, rel, 1, 1)
        pass_on(k, rel, 2, 1)
        send(wts_at(k, rel), wts_at(k, rel), ag_s.at[k], sib_r.at[k], sibling)

    steps = {}

    def register(name, core, action):
        before, mine = steps.get(name), on_core(core, action)
        steps[name] = mine if before is None else lambda: (before(), mine())

    def gather_steps(k, core, z_first):
        order = (0, 1, 2) if z_first else (1, 0, 2)
        held = [(0, 0, 0)]

        def step(phase, named):
            rel = (z_offset[named[0]], named[1], named[2])
            got(wts_at(k, rel), ag_r.at[k, rel[0] * 4 + rel[1] * 2 + rel[2]])
            hand_on(k, order, phase, named[0], rel)

        for phase, dim in enumerate(order):
            fresh = []
            for i in range(1, z_count if dim == 0 else 2):
                for j, named in enumerate(held):
                    there = list(named)
                    there[dim] = i
                    fresh.append(tuple(there))
                    register((k, phase, i, j), core, functools.partial(step, phase, tuple(there)))
            held = held + fresh

    def add_up(k, rel, others):
        here_ref = psum_at(k, rel)
        total = here_ref[...].astype(F32)
        for other in others:
            total = total + other[...].astype(F32)
        return here_ref, total

    nearest_last = list(range(1, z_count)) + [0]

    def scatter_send(k, rz, ra):
        send(
            psum_at(k, (rz, ra, 1)), recv.at[k, rz * 2 + ra], rs_s.at[k],
            rs_r.at[k, rz * 2 + ra], partner(scatter_x[k], 2, 1),
        )

    def scatter_first(k):
        for rz in nearest_last:
            for ra in (1, 0):
                scatter_send(k, rz, ra)

    def scatter_first_part(k, part):
        if part == 0:
            for rz in nearest_last:
                scatter_send(k, rz, 1)

        @pl.when(scatter_x[k] == 1 - part)
        def _():
            for rz in nearest_last:
                scatter_send(k, rz, 0)

    def scatter_steps(k):
        for core, z_first in variants(SCATTER, k):
            scatter_steps_on(k, core, z_first)

    def scatter_steps_on(k, core, z_first):
        second = 2 * z_count
        third = second + (z_count if z_first else 2 * (z_count - 1))

        def fresh(start, i):
            got(recv.at[k, start + i], rs_r.at[k, start + i])
            return recv.at[k, start + i]

        fresh1 = functools.partial(fresh, 0)
        fresh2 = functools.partial(fresh, second)
        fresh3 = functools.partial(fresh, third)
        x_early = scatter_x[k]

        def sum_on(rel, others, slot, to):
            ref, total = add_up(k, rel, others)
            ref[...] = total.astype(BF16)
            send(ref, recv.at[k, slot], rs_s.at[k], rs_r.at[k, slot], to)

        def finish_sum(others):
            _, total = add_up(k, (0, 0, 0), others)
            out_g[k] = total

        if z_first:

            def early_hop(rz):
                sum_on((rz, 1, 0), [fresh1(rz * 2 + 1)], second + rz, partner(x_early, 1, 1))

            def z_hop(rz):
                others = [fresh1(rz * 2), fresh2(rz)]
                sum_on((rz, 0, 0), others, third + rz - 1, partner(x_early, 0, rz))

            for rz in range(z_count):
                register(("rs", k, "a", rz), core, functools.partial(early_hop, rz))
                if rz > 0:
                    register(("rs", k, "b", rz), core, functools.partial(z_hop, rz))

            def last():
                finish_sum([fresh1(0), fresh2(0)] + [fresh3(i) for i in range(z_count - 1)])

        else:

            def z_hop(rz, ra):
                i = (rz - 1) * 2 + ra
                sum_on((rz, ra, 0), [fresh1(rz * 2 + ra)], second + i, partner(x_early, 0, rz))

            def early_hop():
                others = [fresh1(1)] + [fresh2(i * 2 + 1) for i in range(z_count - 1)]
                sum_on((0, 1, 0), others, third, partner(x_early, 1, 1))

            for rz in range(1, z_count):
                for ra in range(2):
                    register(("rs", k, "a", rz, ra), core, functools.partial(z_hop, rz, ra))
            register(("rs", k, "b"), core, early_hop)

            def last():
                finish_sum([fresh1(0)] + [fresh2(i * 2) for i in range(z_count - 1)] + [fresh3(0)])

        register(("rs", k, "c"), core, last)

    point = [0]

    def service(before_last=None):
        point[0] += 1
        names = SCHEDULE.get(point[0], ())
        for i, name in enumerate(names):
            if before_last is not None and i == len(names) - 1:
                before_last()
            steps.pop(name)()

    def weights_here(k):
        service()
        got(wts.at[pl.ds(0, 2 * width), :], sib_r.at[k])

    def weight(k, j, columns=slice(None)):
        return wts[pl.ds(aligned((k * 4 + j) * width, 128), width), columns]

    def own_place(k):
        return pl.ds(aligned((k * 4 + n) * width + w * depth, 32), depth)

    barrier = pltpu.get_barrier_semaphore()
    for to in wide_partners + narrow_partners:
        pl.semaphore_signal(barrier, inc=1, device_id=to, device_id_type=MESH)
    wts[own_place(0), 0:192] = wqkv[0]
    wts[own_place(0), 192:384] = wqkv[2]
    wts[own_place(0), 384:576] = wqkv[1]
    wts[own_place(0), 576:768] = jnp.transpose(wout[...].astype(F32)).astype(BF16)
    smalls[w] = jnp.zeros(smalls.shape[1:], F32)
    smalls[w, 0:8, 0:depth] = norm_bias[...].astype(F32)
    hidden_bias = fc1_bias[...].astype(F32).reshape(1, 4 * depth)
    for r in range(4):
        smalls[w, 8 + r : 9 + r, 0:depth] = hidden_bias[:, r * depth : (r + 1) * depth]

    pl.semaphore_wait(barrier, len(wide_partners) + len(narrow_partners))

    rows_here = pl.ds(aligned(n * block, 128), block)

    def rows_of(to):
        return pl.ds(aligned(to[1] * block, 128), block)

    for i, to in enumerate(narrow_partners):
        send(tok.at[to[1]], xrow.at[rows_here, :], tok_s.at[i], tok_r.at[i], to)
    own_along_z(0)
    own_across(0)
    for i, to in enumerate(wide_partners):
        send(smalls.at[w], smalls.at[w], small_s.at[i], small_r.at[i], to)
    own_tok = pltpu.make_async_copy(tok.at[n], xrow.at[rows_here, :], loc.at[1])
    own_tok.start()
    own_gout = pltpu.make_async_copy(gout.at[n], urow.at[rows_here, :], loc.at[2])
    own_gout.start()
    wts[own_place(1), :] = wfc1[...]
    wts[own_place(2), :] = wfc2[...]

    def start_gout():
        for i, to in enumerate(narrow_partners):
            send(gout.at[to[1]], urow.at[rows_here, :], gout_s.at[i], gout_r.at[i], to)

    for k in range(3):
        for core, z_first in variants(GATHER, k):
            gather_steps(k, core, z_first)
    steps[("z1",)] = functools.partial(own_along_z, 1)
    steps[("xy1",)] = functools.partial(own_across, 1)
    steps[("z2",)] = functools.partial(own_along_z, 2)
    steps[("xy2",)] = functools.partial(own_across, 2)
    steps[("gout",)] = start_gout

    ids = clip[n]
    place = lax.broadcasted_iota(jnp.int32, (1, length), 1)
    ids = jnp.where(ids >= 0, ids, -1 - place).astype(F32)
    ids_down = jnp.transpose(jnp.broadcast_to(ids, (128, length)))[:, 0:1]
    mask[...] = jnp.where(ids_down == ids, 0.0, -1e30)

    for i, to in enumerate(wide_partners):
        got(smalls.at[to[0]], small_r.at[i])
    qbias[...] = jnp.zeros_like(qbias)
    vbias[...] = jnp.zeros_like(vbias)
    for i in range(wide):
        part = smalls[i]
        vecs[:, i * depth : (i + 1) * depth] = part[0:8, 0:depth]
        j, half_at = i // 2, (i % 2) * depth
        qbias[j, :, half_at : half_at + depth] = part[2:3, 0:depth]
        vbias[j, :, 64 + half_at : 64 + half_at + depth] = part[3:4, 0:depth]
        for r in range(4):
            at = (i % 2) * 4 * depth + r * depth
            hbias[j, :, at : at + depth] = part[8 + r : 9 + r, 0:depth]

    service()
    own_tok.wait()
    for i, to in enumerate(narrow_partners):
        got(xrow.at[rows_of(to), :], tok_r.at[i])

    def norm_forward(source, gain, shift, column, target):
        def body(i, _):
            rows = pl.ds(aligned(i * block, 128), block)
            v = source[rows, :].astype(F32)
            average = jnp.mean(v, axis=-1, keepdims=True)
            centred = v - average
            rr = lax.rsqrt(jnp.mean(centred * centred, axis=-1, keepdims=True) + 1e-6)
            stats[rows, column : column + 1] = average
            stats[rows, column + 1 : column + 2] = rr
            target[rows, :] = (centred * rr * vecs[gain : gain + 1] + vecs[shift : shift + 1]).astype(BF16)
            return 0

        lax.fori_loop(0, 4, body, 0)

    norm_forward(xrow, 0, 1, 0, normed1)
    service()

    weights_here(0)
    lane = lax.broadcasted_iota(jnp.int32, (1, 256), 1)
    low = lane[:, 0:128] < 64
    for j in range(4):
        projected = dot(normed1[...], weight(0, j, slice(0, 640)), NN)
        slot = slice(256 * j, 256 * j + 256)
        query = (projected[:, 0:256] + qbias[j]).astype(BF16).astype(F32) * 0.125
        qs[:, slot] = jnp.where(lane < 192, query, 0.0).astype(BF16)
        value = projected[:, 128:384] + vbias[j]
        vs[:, slot] = jnp.where(lane >= 64, value, 0.0).astype(BF16)
        ks[:, slot] = jnp.where(lane < 192, projected[:, 384:640], 0.0).astype(BF16)
        service()

    def lanes(j, second):
        return pl.ds(aligned(256 * j + 128 * second, 128), 128)

    def only(head, values):
        return jnp.where(low if head == 0 else ~low, values, jnp.zeros_like(values))

    def query_of(j, head):
        return only(head, qs[:, lanes(j, 0)]) if head < 2 else qs[:, lanes(j, 1)]

    def key_of(j, head):
        return ks[:, lanes(j, 0)] if head < 2 else ks[:, lanes(j, 1)]

    for j in range(4):
        mixed = []
        for head in range(3):
            scores = dot(query_of(j, head), key_of(j, head), NT) + mask[...]
            row_max = jnp.max(scores, axis=1, keepdims=True)
            weights = jnp.exp(scores - row_max)
            row_sum = jnp.sum(weights, axis=1, keepdims=True)
            probs = (weights * (1.0 / row_sum)).astype(BF16)
            lse[j, :, head : head + 1] = row_max + jnp.log(row_sum)
            service()
            value = vs[:, lanes(j, 0)] if head == 0 else vs[:, lanes(j, 1)]
            mixed.append(dot(probs, value, NN))
            service()
        heads[:, lanes(j, 0)] = mixed[0].astype(BF16)
        heads[:, lanes(j, 1)] = jnp.where(low, mixed[1], mixed[2]).astype(BF16)

    fb[...] = xrow[...].astype(F32) + vecs[4:5]
    for j in range(4):
        fb[...] += dot(heads[:, 256 * j : 256 * j + 256], weight(0, j, slice(512, 768)), NT)
        service()
    fa[...] = fb[...]
    norm_forward(fa, 5, 6, 2, normed2)

    weights_here(1)
    for j in range(4):
        pre = dot(normed2[...], weight(1, j), NN) + hbias[j]
        service()
        cumulative = 0.5 * (1.0 + lax.erf(pre * (0.5**0.5)))
        density = jnp.exp(pre * pre * -0.5) * (0.5 / jnp.pi) ** 0.5
        act[j] = (pre * cumulative).astype(BF16)
        dgelu[j] = (cumulative + pre * density).astype(BF16)
        service()

    def give(k, j, slot, product):
        if k < 2:
            sent(gsend.at[slot], gs_s.at[slot])
        gsend[slot] = product.astype(BF16)
        place = pl.ds(aligned((k * 2 + j) * width, 128), width)
        send(gsend.at[slot], psum.at[place, :], gs_s.at[slot], gs_r.at[k * 2 + j], sibling)

    def keep(k, j, product):
        place = pl.ds(aligned((k * 2 + j) * width, 128), width)
        service()
        got(psum.at[place, :], gs_r.at[k * 2 + j])
        psum[place, :] = (product + psum[place, :].astype(F32)).astype(BF16)

    service()
    own_gout.wait()
    for i, to in enumerate(narrow_partners):
        got(urow.at[rows_of(to), :], gout_r.at[i])
    for j in range(2):
        give(2, j, j, dot(urow[...], act[2 * j + 1 - c], TN))
        service()
    for j in range(2):
        keep(2, j, dot(urow[...], act[2 * j + c], TN))
        service()
    scatter_first(2)
    scatter_steps(2)
    weights_here(2)

    outacc = late if LATE_OUTPUT else fb

    def output():
        for j in range(4):
            outacc[...] = (fa if j == 0 else outacc)[...] + dot(act[j], weight(2, j), NT)
            service()
        outrow[...] = (outacc[...] + vecs[7:8]).astype(BF16)
        for i, to in enumerate(narrow_partners):
            send(outrow.at[rows_of(to), :], out_tok.at[n], ot_s.at[i], ot_r.at[i], to)
        copy = pltpu.make_async_copy(outrow.at[rows_here, :], out_tok.at[n], loc.at[3])
        copy.start()
        return copy

    if LATE_OUTPUT == 0:
        own_out = output()

    def put(row, i, values):
        vpart[i, row : row + 1, 0:depth] = values

    def put_row(row, values):
        for i in range(wide):
            put(row, i, values[:, i * depth : (i + 1) * depth])

    def column_sum(values):
        return jnp.sum(values.astype(F32), axis=0, keepdims=True)

    vpart[...] = jnp.zeros_like(vpart)
    put_row(7, column_sum(urow[...]))
    for j in range(4):
        grad = dot(urow[...], weight(2, j), NN) * dgelu[j].astype(F32)
        dgelu[j] = grad.astype(BF16)
        total = column_sum(dgelu[j])
        for i in range(2):
            for r in range(4):
                at = (i * 4 + r) * depth
                put(8 + r, 2 * j + i, total[:, at : at + depth])
        service()
    for j in range(2):
        give(1, j, j, dot(normed2[...], dgelu[2 * j + 1 - c], TN))
        service()
    for j in range(4):
        product = dot(dgelu[j], weight(1, j), NT)
        fb[...] = product if j == 0 else fb[...] + product
        service()
    for j in range(2):
        keep(1, j, dot(normed2[...], dgelu[2 * j + c], TN))
        service()
    scatter_first(1)
    scatter_steps(1)

    def norm_backward(source, grad, gain, column, extra, target, rounded):
        def body(i, sums):
            rows = pl.ds(aligned(i * block, 128), block)
            rr = stats[rows, column + 1 : column + 2]
            xhat = (source[rows, :].astype(F32) - stats[rows, column : column + 1]) * rr
            n_grad = grad[rows, :]
            u = n_grad * vecs[gain : gain + 1]
            inner = u - jnp.mean(u, axis=-1, keepdims=True) - xhat * jnp.mean(u * xhat, axis=-1, keepdims=True)
            result = rr * inner + extra[rows, :].astype(F32)
            if target is not None:
                target[rows, :] = result
            low_result = result.astype(BF16)
            rounded[rows, :] = low_result
            return (
                sums[0] + slab_sum(n_grad * xhat),
                sums[1] + slab_sum(n_grad),
                sums[2] + slab_sum(low_result.astype(F32)),
            )

        zero = jnp.zeros((8, width), F32)
        sums = lax.fori_loop(0, 4, body, (zero, zero, zero))
        return [jnp.sum(s, axis=0, keepdims=True) for s in sums]

    gain2, shift2, attn_total = norm_backward(fa, fb, 5, 2, urow, fb, attn_grad)
    if LATE_OUTPUT == 1:
        own_out = output()
    put_row(5, gain2)
    put_row(6, shift2)
    put_row(4, attn_total)

    for j in range(4):
        back = dot(attn_grad[...], weight(0, j, slice(512, 768)), NN)
        dheads[:, 256 * j : 256 * j + 256] = jnp.where(lane >= 64, back, 0.0).astype(BF16)
        service()

    def attention_backward(j):
        def value_of(head):
            return vs[:, lanes(j, 0)] if head == 0 else vs[:, lanes(j, 1)]

        def upstream_of(head):
            if head == 0:
                return dheads[:, lanes(j, 0)]
            return only(head - 1, dheads[:, lanes(j, 1)])

        dq, dk, dv = [], [], []
        for head in range(3):
            query, key, up = query_of(j, head), key_of(j, head), upstream_of(head)
            second = int(head > 0)
            delta = jnp.sum(
                up.astype(F32) * heads[:, lanes(j, second)].astype(F32), axis=1, keepdims=True
            )
            scores = dot(query, key, NT) + mask[...]
            soft = jnp.exp(scores - lse[j, :, head : head + 1])
            prob_grad = dot(up, value_of(head), NT)
            score_grad = (soft * (prob_grad - delta)).astype(BF16)
            service()
            dq.append(dot(score_grad, key, NN))
            dk.append(dot(score_grad, query, TN))
            dv.append(dot(soft.astype(BF16), up, TN))
            service()
        dqkv[j, :, 0:128] = (jnp.where(low, dq[0], dq[1]) * 0.125).astype(BF16)
        dqkv[j, :, 128:256] = (dq[2] * 0.125 + dv[0]).astype(BF16)
        dqkv[j, :, 256:384] = (dv[1] + dv[2]).astype(BF16)
        dqkv[j, :, 384:512] = (dk[0] + dk[1]).astype(BF16)
        dqkv[j, :, 512:640] = dk[2].astype(BF16)
        total = column_sum(dqkv[j, :, 0:384])
        for i in range(2):
            put(2, 2 * j + i, total[:, i * depth : (i + 1) * depth])
            put(3, 2 * j + i, total[:, (2 + i) * depth : (3 + i) * depth])

    def projection_grad(j):
        first = dot(normed1[...], dqkv[j], TN)
        second = dot(attn_grad[...], heads[:, pl.ds(aligned(256 * j, 128), 256)], TN)
        return jnp.concatenate(
            [first[:, 0:512], first[:, 512:640] + second[:, 0:128], second[:, 128:256]], axis=1
        )

    for i, half in enumerate((1 - y, y)):
        for own in (False, True):
            j = 2 * half + (c if own else 1 - c)
            attention_backward(j)
            if own:
                keep(0, half, projection_grad(j))
            else:
                give(0, half, i, projection_grad(j))
            service()
        scatter_first_part(0, i)
        if i == 0:
            scatter_steps(0)
            if LATE_OUTPUT == 2:
                own_out = output()
    for j in range(4):
        product = dot(dqkv[j], weight(0, j, slice(0, 640)), NT)
        fa[...] = product if j == 0 else fa[...] + product
        service()

    gain1, shift1, _ = norm_backward(xrow, fa, 0, 0, fb, None, gtrow)
    for i, to in enumerate(narrow_partners):
        rows = pl.ds(aligned(to[1] * block, 128), block)
        send(gtrow.at[rows, :], out_gtok.at[n], gt_s.at[i], gt_r.at[i], to)
    own_gtok = pltpu.make_async_copy(gtrow.at[rows_here, :], out_gtok.at[n], loc.at[4])
    own_gtok.start()
    service()
    put_row(0, gain1)
    put_row(1, shift1)
    for i, to in enumerate(wide_partners):
        send(vpart.at[to[0]], vrecv.at[i], vp_s.at[i], vp_r.at[i], to)

    def share_vectors():
        total = vpart[w]
        for i in range(len(wide_partners)):
            got(vrecv.at[i], vp_r.at[i])
            total = total + vrecv[i]
        vsum[...] = total
        for i, to in enumerate(narrow_partners):
            send(vsum, vnar.at[i], vn_s.at[i], vn_r.at[i], to)

    service(share_vectors)
    assert not steps
    total = vsum[...]
    for i in range(3):
        got(vnar.at[i], vn_r.at[i])
        total = total + vnar[i]
    out_vec[...] = total

    for i, to in enumerate(narrow_partners):
        got(out_tok.at[to[1]], ot_r.at[i])
        got(out_gtok.at[to[1]], gt_r.at[i])
        sent(tok.at[0], tok_s.at[i])
        sent(gout.at[0], gout_s.at[i])
        sent(outrow.at[pl.ds(0, block), :], ot_s.at[i])
        sent(gtrow.at[pl.ds(0, block), :], gt_s.at[i])
        sent(vsum, vn_s.at[i])
    for i in range(len(wide_partners)):
        sent(smalls.at[0], small_s.at[i])
        sent(vpart.at[0], vp_s.at[i])
    for k in range(3):
        for core, z_first in variants(GATHER, k):
            z_sends = (1, 2 + 3) if z_first else (2, 4 + 6)
            across = (1 + 3) + (1 + 3 + 4) if z_first else 1 + (1 + 1 + 6)
            for place, count in zip((~inner, inner), z_sends):
                rows = (count + across + 4 * z_count) * depth
                all_sent = functools.partial(sent, wts.at[pl.ds(0, rows), :], ag_s.at[k])
                pl.when(place if core is None else place & (c == core))(all_sent)
        sends = 4 * z_count - 1
        sent(psum.at[pl.ds(0, sends * depth), :], rs_s.at[k])
    for slot in range(2):
        sent(gsend.at[slot], gs_s.at[slot])
    own_out.wait()
    own_gtok.wait()


def settle_kernel(tok, gtok, g, vec, out_tok, out_gtok, out_qkv, out_proj, out_fc1, out_fc2, out_nb, out_fb):
    out_tok[...] = tok[...]
    out_gtok[...] = gtok[...].astype(F32)

    @pl.when(pl.program_id(0) == 0)
    def _():
        depth, part = out_qkv.shape[1:]
        out_qkv[0] = g[0, :, 0:part]
        out_qkv[1] = g[0, :, 2 * part : 3 * part]
        out_qkv[2] = g[0, :, part : 2 * part]
        out_proj[...] = jnp.transpose(g[0, :, 3 * part :])
        out_fc1[...] = g[1]
        out_fc2[...] = g[2]
        out_nb[...] = vec[0:8, 0:depth]
        pieces = [vec[8 + r : 9 + r, 0:depth] for r in range(4)]
        out_fb[...] = jnp.concatenate(pieces, axis=1).reshape(4 * depth)


def fused_local(tokens, clip_ids, w_qkv, w_out, w_fc1, w_fc2, norm_bias, fc1_bias, grad_out):
    micro, _, block, width = tokens.shape
    depth, hidden = w_fc1.shape
    wide = width // depth
    z_count = wide // 2
    length = micro * block

    def anywhere():
        return pl.BlockSpec(memory_space=pl.ANY)

    def vmem():
        return pl.BlockSpec(memory_space=pltpu.VMEM)

    def flat(*shape):
        return pltpu.VMEM(shape, BF16)

    def wide_type(*shape):
        return pltpu.VMEM(shape, F32)

    def sems(*shape):
        return pltpu.SemaphoreType.DMA(shape)

    out_tok, out_gtok, out_g, out_vec = pl.pallas_call(
        row_kernel,
        out_shape=(
            jax.ShapeDtypeStruct((micro, block, width), BF16),
            jax.ShapeDtypeStruct((micro, block, width), BF16),
            jax.ShapeDtypeStruct((3, depth, width), F32),
            jax.ShapeDtypeStruct((16, 128), F32),
        ),
        in_specs=[anywhere()] + [vmem()] * 7 + [anywhere()],
        out_specs=(anywhere(), anywhere(), vmem(), vmem()),
        scratch_shapes=[
            flat(12 * width, hidden),
            flat(6 * width, hidden),
            flat(2, width, hidden),
            flat(3, 4 * z_count - 1, depth, hidden),
            *[flat(length, width)] * 7,
            *[flat(length, 1024)] * 5,
            flat(4, length, hidden),
            flat(4, length, hidden),
            flat(4, length, 640),
            wide_type(length, width),
            wide_type(length, width),
            wide_type(length if LATE_OUTPUT else 8, width),
            wide_type(length, length),
            wide_type(length, 128),
            wide_type(4, length, 128),
            wide_type(wide, 16, 128),
            wide_type(8, width),
            wide_type(4, 1, 256),
            wide_type(4, 1, 256),
            wide_type(4, 1, hidden),
            wide_type(wide, 16, 128),
            wide_type(wide - 1, 16, 128),
            wide_type(16, 128),
            wide_type(3, 16, 128),
            sems(3), sems(3), sems(3), sems(3), sems(wide - 1), sems(wide - 1),
            sems(3), sems(3, 4 * z_count), sems(3), sems(2), sems(6),
            sems(3), sems(3, 4 * z_count - 1),
            sems(3), sems(3), sems(3), sems(3), sems(wide - 1), sems(wide - 1), sems(3), sems(3),
            sems(5),
        ],
        compiler_params=pltpu.CompilerParams(
            collective_id=0, has_side_effects=True, vmem_limit_bytes=63 * 2**20
        ),
    )(
        tokens.reshape(micro, block, width), clip_ids, w_qkv, w_out, w_fc1, w_fc2.T, norm_bias,
        fc1_bias, grad_out.reshape(micro, block, width),
    )
    part = width // 4
    shapes = [(3, depth, part), (part, depth), (depth, width), (depth, width), (8, depth), (4 * depth,)]
    rows_spec = pl.BlockSpec((micro // 2, block, width), lambda i: (i, 0, 0))

    def fixed(shape):
        return pl.BlockSpec(shape, lambda i: (0,) * len(shape))

    out, gtok, grad_qkv, grad_proj, grad_fc1, grad_fc2, grad_nb, grad_fb = pl.pallas_call(
        settle_kernel,
        grid=(2,),
        out_shape=[
            jax.ShapeDtypeStruct((micro, block, width), BF16),
            jax.ShapeDtypeStruct((micro, block, width), F32),
            *[jax.ShapeDtypeStruct(shape, F32) for shape in shapes],
        ],
        in_specs=[rows_spec, rows_spec, fixed((3, depth, width)), fixed((16, 128))],
        out_specs=[rows_spec, rows_spec, *[fixed(shape) for shape in shapes]],
    )(out_tok, out_gtok, out_g, out_vec)
    return (
        out[:, None],
        gtok[:, None],
        grad_qkv,
        grad_proj,
        grad_fc1,
        grad_fc2.T,
        grad_nb,
        grad_fb,
    )


def layer_norm(values, scaling, shifting):
    average = jnp.mean(values, axis=-1, keepdims=True)
    centred = values - average
    variance = jnp.mean(centred * centred, axis=-1, keepdims=True)
    return centred * lax.rsqrt(variance + 1e-06) * scaling + shifting


def exact_gelu(values):
    return jax.nn.gelu(values, approximate=False)


def block_scores(query_block, keys, clip_block, clip_row, block_start, score_scale):
    block_rows = query_block.shape[0]
    length = keys.shape[0]
    scores = (
        jnp.einsum("qhd,khd->hqk", query_block, keys, preferred_element_type=jnp.float32)
        * score_scale
    )
    key_place = lax.broadcasted_iota(jnp.int32, (block_rows, length), 1)
    query_place = block_start + lax.broadcasted_iota(jnp.int32, (block_rows, length), 0)
    allowed = (clip_block[:, None] == clip_row[None, :]) & (clip_row[None, :] >= 0) | (
        query_place == key_place
    )
    return jnp.where(allowed[None], scores, -1e30)


def row_forward(query, keys, values, clip_row, score_scale):
    length = query.shape[0]
    block_rows = min(512, length)

    def one_block(block_start):
        scores = block_scores(query, keys, clip_row, clip_row, block_start, score_scale)
        row_max = jnp.max(scores, axis=-1, keepdims=True)
        weights = jnp.exp(scores - row_max)
        row_sum = jnp.sum(weights, axis=-1, keepdims=True)
        probabilities = (weights / row_sum).astype(jnp.bfloat16)
        mixed = jnp.einsum(
            "hqk,khd->qhd", probabilities, values, preferred_element_type=jnp.float32
        )
        return (mixed, (row_max + jnp.log(row_sum))[..., 0])

    starts = lax.broadcasted_iota(jnp.int32, (length // block_rows,), 0) * block_rows
    mixed, log_totals = lax.map(one_block, starts)
    return (mixed.reshape(length, -1), log_totals)


def row_backward(query, keys, values, clip_row, log_totals, grad_heads, score_scale):
    length = query.shape[0]
    block_rows = min(512, length)

    def one_block(running, element):
        key_grad, value_grad = running
        block_start, block_totals = element
        scores = block_scores(query, keys, clip_row, clip_row, block_start, score_scale)
        probabilities = jnp.exp(scores - block_totals[..., None])
        prob_grad = jnp.einsum(
            "qhd,khd->hqk", grad_heads, values, preferred_element_type=jnp.float32
        )
        value_grad = value_grad + jnp.einsum(
            "hqk,qhd->khd",
            probabilities.astype(jnp.bfloat16),
            grad_heads,
            preferred_element_type=jnp.float32,
        )
        score_grad = probabilities * (
            prob_grad - jnp.sum(probabilities * prob_grad, axis=-1, keepdims=True)
        )
        score_grad = score_grad.astype(jnp.bfloat16)
        query_grad = (
            jnp.einsum("hqk,khd->qhd", score_grad, keys, preferred_element_type=jnp.float32)
            * score_scale
        )
        key_grad = (
            key_grad
            + jnp.einsum("hqk,qhd->khd", score_grad, query, preferred_element_type=jnp.float32)
            * score_scale
        )
        return ((key_grad, value_grad), query_grad)

    starts = lax.broadcasted_iota(jnp.int32, (length // block_rows,), 0) * block_rows
    zero_grads = jnp.zeros(keys.shape, jnp.float32)
    (key_grad, value_grad), query_grads = lax.scan(
        one_block, (zero_grads, zero_grads), (starts, log_totals)
    )
    return (query_grads.reshape(query.shape), key_grad, value_grad)


def local(tokens, clip_ids, w_qkv, w_out, w_fc1, w_fc2, norm_bias, fc1_bias, grad_out):
    micro_count = tokens.shape[0]
    row_count = tokens.shape[1]
    width = tokens.shape[3]
    local_width = w_qkv.shape[2]
    local_hidden = w_fc1.shape[1]
    heads_here = local_width // HEAD_DIM
    score_scale = HEAD_DIM ** (-0.5)
    narrow_index = lax.axis_index("narrow")

    def spread_rows(values):
        return lax.all_gather(values, "narrow", axis=1, tiled=True)

    def fold_rows(values):
        return lax.psum_scatter(values, "narrow", scatter_dimension=1, tiled=True)

    def spread_grads(values):
        return lax.all_gather(values, "narrow", axis=1, tiled=True)

    def fold_grads(values):
        return lax.psum_scatter(values, "narrow", scatter_dimension=1, tiled=True)

    def forward_rows(element):
        return row_forward(element[0], element[1], element[2], element[3], score_scale)

    def backward_rows(element):
        return row_backward(
            element[0], element[1], element[2], element[3], element[4], element[5], score_scale
        )

    results = []
    input_grads = []
    shards = None
    for number in range(micro_count):
        qkv_full = lax.all_gather(w_qkv, "wide", axis=1, tiled=True)
        out_full = lax.all_gather(w_out, "wide", axis=1, tiled=True)
        fc1_full = lax.all_gather(w_fc1, "wide", axis=0, tiled=True)
        fc2_full = lax.all_gather(w_fc2, "wide", axis=1, tiled=True)
        vector_full = lax.all_gather(norm_bias, "wide", axis=1, tiled=True)
        hidden_bias_full = lax.all_gather(fc1_bias, "wide", axis=0, tiled=True)
        vectors = vector_full.astype(jnp.float32)
        hidden_total = hidden_bias_full.shape[0]
        column_start = narrow_index * local_width
        hidden_start = narrow_index * local_hidden
        fc_bias = lax.dynamic_slice_in_dim(hidden_bias_full, hidden_start, local_hidden, 0).astype(
            jnp.float32
        )
        query_bias = lax.dynamic_slice_in_dim(vectors[2], column_start, local_width, 0)
        value_bias = lax.dynamic_slice_in_dim(vectors[3], column_start, local_width, 0)
        inputs = tokens[number].astype(jnp.float32)
        clip_rows = clip_ids[number]
        normed1 = layer_norm(inputs, vectors[0], vectors[1]).astype(jnp.bfloat16)
        rows_one = spread_rows(normed1)
        length = rows_one.shape[1]
        projected = jnp.einsum(
            "rld,jde->jrle", rows_one, qkv_full, preferred_element_type=jnp.float32
        )
        bias_three = jnp.stack([query_bias, jnp.zeros_like(query_bias), value_bias])
        qkv_low = (projected + bias_three[:, None, None, :]).astype(jnp.bfloat16)
        split_heads = qkv_low.reshape(3, row_count, length, heads_here, HEAD_DIM)
        attended, log_totals = lax.map(
            forward_rows, (split_heads[0], split_heads[1], split_heads[2], clip_rows)
        )
        attended = attended.astype(jnp.bfloat16)
        attention_part = jnp.einsum(
            "rle,ed->rld", attended, out_full, preferred_element_type=jnp.float32
        )
        hidden1 = inputs + fold_rows(attention_part) + vectors[4]
        normed2 = layer_norm(hidden1, vectors[5], vectors[6]).astype(jnp.bfloat16)
        rows_two = spread_rows(normed2)
        pre_act = (
            jnp.einsum("rld,df->rlf", rows_two, fc1_full, preferred_element_type=jnp.float32)
            + fc_bias
        )
        act_low = exact_gelu(pre_act).astype(jnp.bfloat16)
        mlp_part = jnp.einsum("rlf,fd->rld", act_low, fc2_full, preferred_element_type=jnp.float32)
        result = (hidden1 + fold_rows(mlp_part) + vectors[7]).astype(jnp.bfloat16)
        upstream = grad_out[number].astype(jnp.float32)
        up_low = grad_out[number]
        fc2_bias_grad = jnp.sum(upstream, axis=(0, 1))
        up_rows = spread_grads(up_low)
        fc2_grad = jnp.einsum("rlf,rld->fd", act_low, up_rows, preferred_element_type=jnp.float32)
        act_grad = jnp.einsum("rld,fd->rlf", up_rows, fc2_full, preferred_element_type=jnp.float32)
        _, gelu_pull = jax.vjp(exact_gelu, pre_act)
        pre_grad = gelu_pull(act_grad)[0].astype(jnp.bfloat16)
        fc1_bias_grad = jnp.sum(pre_grad.astype(jnp.float32), axis=(0, 1))
        fc1_grad = jnp.einsum("rld,rlf->df", rows_two, pre_grad, preferred_element_type=jnp.float32)
        normed2_grad = fold_grads(
            jnp.einsum("rlf,df->rld", pre_grad, fc1_full, preferred_element_type=jnp.float32)
        )
        _, norm2_pull = jax.vjp(layer_norm, hidden1, vectors[5], vectors[6])
        hidden1_grad, gain2_grad, shift2_grad = norm2_pull(normed2_grad)
        hidden1_grad = hidden1_grad + upstream
        attn_low = hidden1_grad.astype(jnp.bfloat16)
        out_bias_grad = jnp.sum(attn_low.astype(jnp.float32), axis=(0, 1))
        attn_rows = spread_grads(attn_low)
        out_grad = jnp.einsum(
            "rle,rld->ed", attended, attn_rows, preferred_element_type=jnp.float32
        )
        heads_grad = jnp.einsum(
            "rld,ed->rle", attn_rows, out_full, preferred_element_type=jnp.float32
        ).astype(jnp.bfloat16)
        heads_grad = heads_grad.reshape(row_count, length, heads_here, HEAD_DIM)
        query_grad, key_grad, value_grad = lax.map(
            backward_rows,
            (split_heads[0], split_heads[1], split_heads[2], clip_rows, log_totals, heads_grad),
        )
        qkv_grad = (
            jnp.stack([query_grad, key_grad, value_grad])
            .reshape(3, row_count, length, local_width)
            .astype(jnp.bfloat16)
        )
        qkv_grad_wide = qkv_grad.astype(jnp.float32)
        query_bias_grad = jnp.sum(qkv_grad_wide[0], axis=(0, 1))
        value_bias_grad = jnp.sum(qkv_grad_wide[2], axis=(0, 1))
        qkv_weight_grad = jnp.einsum(
            "rld,jrle->jde", rows_one, qkv_grad, preferred_element_type=jnp.float32
        )
        normed1_grad = fold_grads(
            jnp.einsum("jrle,jde->rld", qkv_grad, qkv_full, preferred_element_type=jnp.float32)
        )
        _, norm1_pull = jax.vjp(layer_norm, inputs, vectors[0], vectors[1])
        input_grad, gain1_grad, shift1_grad = norm1_pull(normed1_grad)
        input_grad = input_grad + hidden1_grad
        blank_width = jnp.zeros((width,), jnp.float32)
        query_placed = lax.dynamic_update_slice_in_dim(
            blank_width, query_bias_grad, column_start, 0
        )
        value_placed = lax.dynamic_update_slice_in_dim(
            blank_width, value_bias_grad, column_start, 0
        )
        vector_grad = jnp.stack(
            [
                gain1_grad,
                shift1_grad,
                query_placed,
                value_placed,
                out_bias_grad,
                gain2_grad,
                shift2_grad,
                fc2_bias_grad,
            ]
        )
        hidden_placed = lax.dynamic_update_slice_in_dim(
            jnp.zeros((hidden_total,), jnp.float32), fc1_bias_grad, hidden_start, 0
        )
        grads = (qkv_weight_grad, out_grad, fc1_grad, fc2_grad, vector_grad, hidden_placed)
        result, input_grad, grads = (result, input_grad, grads)
        results.append(result)
        input_grads.append(input_grad)
        vector_sums = lax.psum(
            (
                lax.psum_scatter(grads[4], "wide", scatter_dimension=1, tiled=True),
                lax.psum_scatter(grads[5], "wide", scatter_dimension=0, tiled=True),
            ),
            "narrow",
        )
        settled = (
            lax.psum_scatter(grads[0], "wide", scatter_dimension=1, tiled=True),
            lax.psum_scatter(grads[1], "wide", scatter_dimension=1, tiled=True),
            lax.psum_scatter(grads[2], "wide", scatter_dimension=0, tiled=True),
            lax.psum_scatter(grads[3], "wide", scatter_dimension=1, tiled=True),
            vector_sums[0],
            vector_sums[1],
        )
        shards = settled if shards is None else jax.tree.map(jnp.add, shards, settled)
    return (
        jnp.stack(results),
        jnp.stack(input_grads),
        shards[0],
        shards[1],
        shards[2],
        shards[3],
        shards[4],
        shards[5],
    )


def solution(mesh):
    in_specs = (
        P(None, "wide", "narrow", None),
        P(None, "wide", None),
        P(None, "wide", "narrow"),
        P("narrow", "wide"),
        P("wide", "narrow"),
        P("narrow", "wide"),
        P(None, "wide"),
        P("wide"),
        P(None, "wide", "narrow", None),
    )
    out_specs = (
        P(None, "wide", "narrow", None),
        P(None, "wide", "narrow", None),
        P(None, "wide", "narrow"),
        P("narrow", "wide"),
        P("wide", "narrow"),
        P("narrow", "wide"),
        P(None, "wide"),
        P("wide"),
    )

    def fits(tokens, w_qkv, w_fc1):
        wide, narrow = mesh.shape["wide"], mesh.shape["narrow"]
        width, hidden = w_fc1.shape
        return (
            wide == 8
            and narrow == 4
            and tokens.shape[:2] == (narrow, wide)
            and tokens.shape[2] % (128 * narrow) == 0
            and width == 12 * HEAD_DIM
            and hidden == narrow * width
        )

    def whole(tokens, clip_ids, w_qkv, w_out, w_fc1, w_fc2, norm_bias, fc1_bias, grad_out):
        chosen = fused_local if fits(tokens, w_qkv, w_fc1) else local
        placed = jax.shard_map(chosen, mesh=mesh, in_specs=in_specs, out_specs=out_specs, check_vma=False)
        return placed(tokens, clip_ids, w_qkv, w_out, w_fc1, w_fc2, norm_bias, fc1_bias, grad_out)

    return whole
```
